32 devices in a mesh: row: 8 (over y, x, core), col: 4 (over z).
Axes of the slice: x: 2, y: 2, z: 4, core: 2. Of those that a mesh axis runs over, the one named last changes fastest.
Arguments:
- vectors: float32 [16, 4096], P(None, ('row', 'col')), may hold values from -6 to 6
- diagonal_energy: float32 [4096], P(('row', 'col')), may hold values from 0.45 to 61
- tiles: float32 [8, 4, 16, 128, 128], P('row', 'col'), may hold values from -0.25 to 0.25
- tile_rows: int32 [8, 4, 16], P('row', 'col'), may hold values from 0 to 3, as said below
- tile_cols: int32 [8, 4, 16], P('row', 'col'), may hold values from 0 to 7
- tile_count: int32 [8, 4], P('row', 'col'), may hold values from 1 to 16
Outputs:
- residual: float32 [16, 4096], P(None, ('row', 'col'))
- rayleigh: float32 [16, 16], replicated
- gram: float32 [16, 16], replicated
The draws below stay inside these ranges and needn't reach their ends.
Inputs may be any that keep to these rules, and one draw needn't show every extreme that they name: `tile_rows`: slots of one device name distinct pairs on or below the block diagonal as in the reference program; slots from tile_count[r, c] on are unused and hold arbitrary in-range values.
All inputs are finite; a program needn't handle non-finite values.
Results may differ from the reference program's by a relative error of at most 0.0003.
Values sent between devices are 32-bit elements; how exact they have to be, the bound alone decides.
No kernel may reach another device: no remote copies, remote signals or barrier semaphores. Data moves between devices by JAX's collectives and lax.ppermute only.
A program may use at most 64 MiB of HBM per device.

```python
import jax
import jax.numpy as jnp
from jax import lax

NV = 16
TILE = 128
SLOTS = 16
GRID_ROWS = 8
GRID_COLS = 4
DIM = 4096


def grid_pairs(key):
    candidates = GRID_ROWS * GRID_COLS
    keys = jax.random.split(key, candidates)

    def one_device(device_key, device):
        pair_key, count_key = jax.random.split(device_key)
        rpos = device // GRID_COLS
        cpos = device % GRID_COLS
        index = jnp.arange(candidates, dtype=jnp.int32)
        local_a = index % GRID_COLS
        local_b = index // GRID_COLS
        usable = (local_b < rpos) | (local_b == rpos) & (local_a >= cpos)
        noise = jax.random.randint(pair_key, (candidates,), 0, 65536, dtype=jnp.int32)
        score = jnp.where(usable, noise * candidates + index, -1 - index)
        _, picked = lax.top_k(score, SLOTS)
        wanted = jax.random.randint(count_key, (), SLOTS // 2, SLOTS + 1, dtype=jnp.int32)
        wanted = jnp.where(device == (GRID_ROWS - 1) * GRID_COLS, SLOTS, wanted)
        wanted = jnp.maximum(wanted, 1)
        count = jnp.minimum(jnp.sum(usable.astype(jnp.int32)), wanted)
        return (local_a[picked], local_b[picked], count)
    devices = jnp.arange(candidates, dtype=jnp.int32)
    arow, bcol, count = jax.vmap(one_device)(keys, devices)
    return (arow.reshape(GRID_ROWS, GRID_COLS, SLOTS), bcol.reshape(GRID_ROWS, GRID_COLS, SLOTS), count.reshape(GRID_ROWS, GRID_COLS))


def draw_tile_rows(key, part):
    return grid_pairs(key)[0]


def draw_tile_cols(key, part):
    return grid_pairs(key)[1]


def draw_tile_count(key, part):
    return grid_pairs(key)[2]


def draw_diagonal_energy(key, part):
    key = jax.random.fold_in(key, 7)
    position = jnp.arange(DIM, dtype=jnp.float32) / DIM
    base = jnp.exp(jnp.log(30.0) * position)
    factor = jnp.exp(jax.random.uniform(key, (DIM,), jnp.float32, -0.7, 0.7))
    return base * factor


def block_scale(key, extent, cuts, smallest, top_value):
    loudness, own = 1.0, jax.random.fold_in(key, 6)
    for dim, shards_of in cuts:
        heights = jnp.exp(jax.random.uniform(jax.random.fold_in(own, dim), (shards_of,), jnp.float32, smallest / len(cuts), top_value / len(cuts)))
        loudness = loudness * jnp.repeat(heights, extent[dim] // shards_of).reshape([-1 if axis == dim else 1 for axis in range(len(extent))])
    return loudness


def bell_draw(rng, shape, deviation, most, shards=(), kind=jnp.bfloat16):
    values = deviation * jax.random.normal(rng, shape, jnp.float32)
    if shards:
        values = values * block_scale(rng, shape, shards, -0.22, 0.18)
    return jnp.clip(values, -most, most).astype(kind)


def setup_inputs(seed: int = 0) -> dict:
    streams_of = jax.random.split(jax.random.key(seed), 7)
    return {
        "vectors": bell_draw(streams_of[0], (NV, DIM), 1.0, 6.0, ((1, 32),), jnp.float32),
        "diagonal_energy": draw_diagonal_energy(jax.random.fold_in(streams_of[6], 71), 0),
        "tiles": bell_draw(streams_of[2], (GRID_ROWS, GRID_COLS, SLOTS, TILE, TILE), ((256 * SLOTS) ** -0.5), 0.25, ((0, 8), (1, 4)), jnp.float32),
        "tile_rows": draw_tile_rows(jax.random.fold_in(streams_of[6], 71), 0),
        "tile_cols": draw_tile_cols(jax.random.fold_in(streams_of[6], 71), 0),
        "tile_count": draw_tile_count(jax.random.fold_in(streams_of[6], 71), 0),
    }


def reference(vectors, diagonal_energy, tiles, tile_rows, tile_cols, tile_count):
    hp = lax.Precision.HIGHEST
    blocks = GRID_ROWS * GRID_COLS
    blocked = vectors.reshape(NV, blocks, TILE)
    tile_flat = tiles.reshape(blocks, SLOTS, TILE, TILE)
    rows_flat = tile_rows.reshape(blocks, SLOTS).astype(jnp.int32)
    cols_flat = tile_cols.reshape(blocks, SLOTS).astype(jnp.int32)
    count_flat = tile_count.reshape(blocks).astype(jnp.int32)
    device_ids = jnp.arange(blocks, dtype=jnp.int32)

    def step(total, item):
        tile_set, arow, bcol, count, device = item
        rpos = device // GRID_COLS
        cpos = device % GRID_COLS
        block_i = rpos * GRID_COLS + arow
        block_j = bcol * GRID_COLS + cpos
        live = (jnp.arange(SLOTS, dtype=jnp.int32) < count).astype(jnp.float32)
        left = blocked[:, block_j, :]
        right = blocked[:, block_i, :]
        forward = jnp.einsum("vsk,snk->vsn", left, tile_set, precision=hp) * live[None, :, None]
        backward = jnp.einsum("vsn,snk->vsk", right, tile_set, precision=hp) * live[None, :, None]
        total = total.at[:, block_i, :].add(forward)
        total = total.at[:, block_j, :].add(backward)
        return total, None

    start = jnp.zeros((NV, blocks, TILE), jnp.float32)
    total, _ = lax.scan(step, start, (tile_flat, rows_flat, cols_flat, count_flat, device_ids))
    product = total.reshape(NV, DIM) + diagonal_energy[None, :] * vectors
    rayleigh = jnp.dot(vectors, product.T, precision=hp) / DIM
    residual = product - jnp.dot(rayleigh, vectors, precision=hp)
    gram = jnp.dot(residual, residual.T, precision=hp) / DIM
    return residual, rayleigh, gram
```

```python
import functools

import jax
import jax.numpy as jnp
from jax import lax
from jax.experimental import pallas as pl
from jax.experimental.pallas import tpu as pltpu
from jax.sharding import PartitionSpec as P

HP = lax.Precision.HIGHEST
LAST = (((1,), (1,)), ((), ()))
VMEM = pl.BlockSpec(memory_space=pltpu.VMEM)
SMEM = pl.BlockSpec(memory_space=pltpu.SMEM)


def mult(left, right):
    return lax.dot_general(left, right, (((1,), (0,)), ((), ())), precision=HP, preferred_element_type=jnp.float32)


def mult_last(left, right):
    return lax.dot_general(left, right, LAST, precision=HP, preferred_element_type=jnp.float32)


def shift(value, axis, step):
    size = lax.axis_size(axis)
    return lax.ppermute(value, axis, [(p, (p + step) % size) for p in range(size)])


def around(value, axis):
    return [shift(value, axis, step) for step in range(1, lax.axis_size(axis))]


def products_kernel(n_row, n_col, slots, *refs):
    place, arow, bcol, count, x_ref, d_ref = refs[:6]
    rest = refs[6:]
    from_col, rest = rest[: n_col - 1], rest[n_col - 1 :]
    from_row, rest = rest[: n_row - 1], rest[n_row - 1 :]
    tiles, rest = rest[0], rest[1:]
    to_col, rest = rest[:n_col], rest[n_col:]
    to_row, rest = rest[:n_row], rest[n_row:]
    x_rows, x_cols, row_terms, col_terms = rest
    me_row, me_col = place[0], place[1]
    own = x_ref[...]
    for step in range(n_col):
        x_rows[step] = own if step == 0 else from_col[step - 1][...]
        row_terms[step] = jnp.zeros_like(own)
    for step in range(n_row):
        x_cols[step] = own if step == 0 else from_row[step - 1][...]
        col_terms[step] = jnp.zeros_like(own)
    half = 0.5 * d_ref[...] * own
    row_terms[0] = half
    col_terms[0] = half
    live_total = count[0, 0]
    for slot in range(slots):
        a = arow[0, 0, slot]
        b = bcol[0, 0, slot]
        live = jnp.where(slot < live_total, 1.0, 0.0).astype(jnp.float32)
        tile = tiles[0, 0, slot]
        x_i = x_rows[lax.rem(me_col - a + n_col, n_col)] * live
        x_j = x_cols[lax.rem(me_row - b + n_row, n_row)] * live
        row_terms[lax.rem(a - me_col + n_col, n_col)] += mult_last(x_j, tile)
        col_terms[lax.rem(b - me_row + n_row, n_row)] += mult(x_i, tile)
    total = jnp.zeros((own.shape[0], own.shape[0]), jnp.float32)
    for step in range(n_col):
        total += mult_last(x_rows[(n_col - step) % n_col], row_terms[step])
        to_col[step][...] = row_terms[step]
    for step in range(n_row):
        to_row[step][0] = col_terms[step]
        to_row[step][1, :, : own.shape[0]] = total


def row_sum_kernel(count, *refs):
    out = refs[count]
    nvec = out.shape[0]
    total = refs[0][1, :, :nvec]
    for ref in refs[1:count]:
        total = total + ref[1, :, :nvec]
    out[...] = total


def residual_kernel(n_row, n_col, scale, *refs):
    x_ref, rest = refs[0], refs[1:]
    by_col, rest = rest[:n_col], rest[n_col:]
    by_row, rest = rest[:n_row], rest[n_row:]
    cross, rest = rest[:n_col], rest[n_col:]
    residual, rayleigh, gram = rest
    product = by_col[0][...] + by_row[0][0]
    for ref in by_col[1:]:
        product += ref[...]
    for ref in by_row[1:]:
        product += ref[0]
    half = cross[0][...]
    for ref in cross[1:]:
        half += ref[...]
    ray = (half + half.T) * scale
    rayleigh[...] = ray
    res = product - mult(ray, x_ref[...])
    residual[...] = res
    gram[...] = mult_last(res, res)


def sum_kernel(count, scale, *refs):
    out = refs[count]
    total = refs[0][...]
    for ref in refs[1:count]:
        total = total + ref[...]
    out[...] = total * scale


def per_device(vectors, diagonal_energy, tiles, tile_rows, tile_cols, tile_count):
    n_row = lax.axis_size("row")
    n_col = lax.axis_size("col")
    nvec, width = vectors.shape
    slots = tiles.shape[2]
    scale = 1.0 / float(n_row * n_col * width)
    block = jax.ShapeDtypeStruct((nvec, width), jnp.float32)
    pair = jax.ShapeDtypeStruct((2, nvec, width), jnp.float32)
    square = jax.ShapeDtypeStruct((nvec, nvec), jnp.float32)
    place = jnp.stack([lax.axis_index("row"), lax.axis_index("col")]).astype(jnp.int32)
    with jax.named_scope("share_vectors"):
        from_row = around(vectors, "row")
        from_col = around(vectors, "col")
    with jax.named_scope("tile_products"):
        terms = pl.pallas_call(
            functools.partial(products_kernel, n_row, n_col, slots),
            out_shape=[block] * n_col + [pair] * n_row,
            in_specs=[SMEM] * 4 + [VMEM] * (n_row + n_col + 1),
            out_specs=[VMEM] * (n_row + n_col),
            scratch_shapes=[
                pltpu.VMEM((n_col, nvec, width), jnp.float32),
                pltpu.VMEM((n_row, nvec, width), jnp.float32),
                pltpu.VMEM((n_col, nvec, width), jnp.float32),
                pltpu.VMEM((n_row, nvec, width), jnp.float32),
            ],
            compiler_params=pltpu.CompilerParams(vmem_limit_bytes=16 * 2**20),
            name="tile_products",
        )(place, tile_rows, tile_cols, tile_count, vectors, diagonal_energy.reshape(1, width), *from_col, *from_row, tiles)
    to_col, to_row = terms[:n_col], terms[n_col:]
    with jax.named_scope("return_products"):
        by_row = [to_row[0]] + [shift(to_row[step], "row", step) for step in range(1, n_row)]
        by_col = [to_col[0]] + [shift(to_col[step], "col", step) for step in range(1, n_col)]
    with jax.named_scope("rayleigh_sum"):
        cross = pl.pallas_call(
            functools.partial(row_sum_kernel, n_row),
            out_shape=square,
            in_specs=[VMEM] * n_row,
            out_specs=VMEM,
            name="rayleigh_over_row",
        )(*by_row)
        crosses = [cross] + around(cross, "col")
    with jax.named_scope("residual"):
        residual, rayleigh, part = pl.pallas_call(
            functools.partial(residual_kernel, n_row, n_col, scale),
            out_shape=[block, square, square],
            in_specs=[VMEM] * (1 + n_row + 2 * n_col),
            out_specs=[VMEM] * 3,
            name="residual",
        )(vectors, *by_col, *by_row, *crosses)
    with jax.named_scope("gram_sum"):
        for axis, factor in (("row", 1.0), ("col", scale)):
            size = lax.axis_size(axis)
            part = pl.pallas_call(
                functools.partial(sum_kernel, size, factor),
                out_shape=square,
                in_specs=[VMEM] * size,
                out_specs=VMEM,
                name="gram_over_" + axis,
            )(part, *around(part, axis))
    return (residual, rayleigh, part)


def solution(mesh):
    return jax.shard_map(
        per_device,
        mesh=mesh,
        in_specs=(
            P(None, ("row", "col")),
            P(("row", "col")),
            P("row", "col", None, None, None),
            P("row", "col", None),
            P("row", "col", None),
            P("row", "col"),
        ),
        out_specs=(P(None, ("row", "col")), P(), P()),
        check_vma=False,
    )
```

```python
import functools

import jax
import jax.numpy as jnp
from jax import lax
from jax.experimental import pallas as pl
from jax.experimental.pallas import tpu as pltpu
from jax.sharding import PartitionSpec as P

HP = lax.Precision.HIGHEST
LAST = (((1,), (1,)), ((), ()))
VMEM = pl.BlockSpec(memory_space=pltpu.VMEM)
SMEM = pl.BlockSpec(memory_space=pltpu.SMEM)


def mult(left, right):
    return lax.dot_general(left, right, (((1,), (0,)), ((), ())), precision=HP, preferred_element_type=jnp.float32)


def mult_last(left, right):
    return lax.dot_general(left, right, LAST, precision=HP, preferred_element_type=jnp.float32)


def swap(blocks, axis):
    return lax.all_to_all(blocks, axis, 0, 0, tiled=True)


def gather(value, axis):
    return swap(jnp.broadcast_to(value[None], (lax.axis_size(axis),) + value.shape), axis)


def products_kernel(n_row, n_col, slots, arow, bcol, count, x_ref, d_ref, x_rows, x_cols, tiles, row_terms, col_terms):
    own = x_ref[...]
    row_terms[...] = jnp.zeros_like(row_terms)
    col_terms[...] = jnp.zeros_like(col_terms)
    live_total = count[0, 0]
    for slot in range(slots):
        a = arow[0, 0, slot]
        b = bcol[0, 0, slot]
        live = jnp.where(slot < live_total, 1.0, 0.0).astype(jnp.float32)
        tile = tiles[0, 0, slot]
        row_terms[a] += mult_last(x_cols[b] * live, tile)
        col_terms[b, 0] += mult(x_rows[a] * live, tile)
    total = mult_last(own, 0.5 * d_ref[...] * own)
    for block in range(n_col):
        total += mult_last(x_rows[block], row_terms[block])
    wide = jnp.concatenate([total, jnp.zeros((own.shape[0], own.shape[1] - own.shape[0]), jnp.float32)], axis=1)
    for block in range(n_row):
        col_terms[block, 1] = wide


def spread(out, square):
    nvec = square.shape[0]
    wide = jnp.concatenate([square, jnp.zeros((nvec, out.shape[2] - nvec), jnp.float32)], axis=1)
    for block in range(out.shape[0]):
        out[block] = wide


def row_sum_kernel(by_row, out):
    out_block = jnp.sum(by_row[:, 1], axis=0)
    for block in range(out.shape[0]):
        out[block] = out_block


def residual_kernel(scale, x_ref, d_ref, by_col, by_row, cross, residual, rayleigh, gram):
    own = x_ref[...]
    nvec = own.shape[0]
    product = jnp.sum(by_col[...], axis=0) + jnp.sum(by_row[:, 0], axis=0) + d_ref[...] * own
    half = jnp.sum(cross[...], axis=0)[:, :nvec]
    ray = (half + half.T) * scale
    rayleigh[...] = ray
    res = product - mult(ray, own)
    residual[...] = res
    spread(gram, mult_last(res, res))


def again_kernel(parts, out):
    total = jnp.sum(parts[...], axis=0)
    for block in range(out.shape[0]):
        out[block] = total


def sum_kernel(scale, parts, out):
    out[...] = jnp.sum(parts[...], axis=0)[:, : out.shape[0]] * scale


def per_device(vectors, diagonal_energy, tiles, tile_rows, tile_cols, tile_count):
    n_row = lax.axis_size("row")
    n_col = lax.axis_size("col")
    nvec, width = vectors.shape
    slots = tiles.shape[2]
    scale = 1.0 / float(n_row * n_col * width)
    block = jax.ShapeDtypeStruct((nvec, width), jnp.float32)
    square = jax.ShapeDtypeStruct((nvec, nvec), jnp.float32)
    per_col = jax.ShapeDtypeStruct((n_col, nvec, width), jnp.float32)
    per_row = jax.ShapeDtypeStruct((n_row, nvec, width), jnp.float32)
    energy = diagonal_energy.reshape(1, width)
    with jax.named_scope("share_vectors"):
        x_cols = gather(vectors, "row")
        x_rows = gather(vectors, "col")
    with jax.named_scope("tile_products"):
        row_terms, col_terms = pl.pallas_call(
            functools.partial(products_kernel, n_row, n_col, slots),
            out_shape=[
                per_col,
                jax.ShapeDtypeStruct((n_row, 2, nvec, width), jnp.float32),
            ],
            in_specs=[SMEM] * 3 + [VMEM] * 5,
            out_specs=[VMEM] * 2,
            compiler_params=pltpu.CompilerParams(vmem_limit_bytes=16 * 2**20),
            name="tile_products",
        )(tile_rows, tile_cols, tile_count, vectors, energy, x_rows, x_cols, tiles)
    with jax.named_scope("return_products"):
        by_row = swap(col_terms, "row")
        by_col = swap(row_terms, "col")
    with jax.named_scope("rayleigh_sum"):
        cross = pl.pallas_call(
            row_sum_kernel, out_shape=per_col, in_specs=[VMEM], out_specs=VMEM, name="rayleigh_over_row"
        )(by_row)
        crosses = swap(cross, "col")
    with jax.named_scope("residual"):
        residual, rayleigh, part = pl.pallas_call(
            functools.partial(residual_kernel, scale),
            out_shape=[block, square, per_row],
            in_specs=[VMEM] * 5,
            out_specs=[VMEM] * 3,
            name="residual",
        )(vectors, energy, by_col, by_row, crosses)
    with jax.named_scope("gram_sum"):
        part = pl.pallas_call(
            again_kernel, out_shape=per_col, in_specs=[VMEM], out_specs=VMEM, name="gram_over_row"
        )(swap(part, "row"))
        gram = pl.pallas_call(
            functools.partial(sum_kernel, scale), out_shape=square, in_specs=[VMEM], out_specs=VMEM, name="gram_over_col"
        )(swap(part, "col"))
    return (residual, rayleigh, gram)


def solution(mesh):
    return jax.shard_map(
        per_device,
        mesh=mesh,
        in_specs=(
            P(None, ("row", "col")),
            P(("row", "col")),
            P("row", "col", None, None, None),
            P("row", "col", None),
            P("row", "col", None),
            P("row", "col"),
        ),
        out_specs=(P(None, ("row", "col")), P(), P()),
        check_vma=False,
    )
```

```python
import functools

import jax
import jax.numpy as jnp
from jax import lax
from jax.experimental import pallas as pl
from jax.experimental.pallas import tpu as pltpu
from jax.sharding import PartitionSpec as P

HP = lax.Precision.HIGHEST
VMEM = pl.BlockSpec(memory_space=pltpu.VMEM)
SMEM = pl.BlockSpec(memory_space=pltpu.SMEM)
BOTH = ("row", "col")


def mult(left, right):
    return lax.dot_general(left, right, (((1,), (0,)), ((), ())), precision=HP, preferred_element_type=jnp.float32)


def mult_last(left, right):
    return lax.dot_general(left, right, (((1,), (1,)), ((), ())), precision=HP, preferred_element_type=jnp.float32)


def swap(blocks):
    return lax.all_to_all(blocks, BOTH, 0, 0, tiled=True)


def own_lanes(nvec, width):
    row = lax.broadcasted_iota(jnp.int32, (nvec, width), 0)
    lane = lax.broadcasted_iota(jnp.int32, (nvec, width), 1)
    return lane // nvec == row % (width // nvec)


def packed_gram(left, right):
    nvec, width = left.shape
    per = width // nvec
    wide = mult_last(left, jnp.concatenate([right] * per, axis=0))
    wide = jnp.where(own_lanes(nvec, width), wide, 0.0)
    return jnp.sum(wide.reshape(nvec // per, per, width), axis=1)


def unpack(packed, nvec):
    rows, width = packed.shape
    per = width // nvec
    wide = jnp.concatenate([jnp.broadcast_to(packed[g : g + 1], (per, width)) for g in range(rows)], axis=0)
    wide = jnp.where(own_lanes(nvec, width), wide, 0.0)
    lane = lax.broadcasted_iota(jnp.int32, (width, nvec), 0)
    column = lax.broadcasted_iota(jnp.int32, (width, nvec), 1)
    return mult(wide, (lane % nvec == column).astype(jnp.float32))


def products_kernel(n_row, n_col, slots, place, arow, bcol, count, x_ref, d_ref, x_all, tiles, out, row_terms):
    own = x_ref[...]
    nvec = own.shape[0]
    me_row, me_col = place[0], place[1]
    out[...] = jnp.zeros_like(out)
    half = 0.5 * d_ref[...] * own
    row_terms[...] = jnp.zeros_like(row_terms)
    row_terms[me_col] = half
    out[me_row * n_col + me_col, :nvec] = half
    live_total = count[0, 0]
    for slot in range(slots):
        a = arow[0, 0, slot]
        i = me_row * n_col + a
        j = bcol[0, 0, slot] * n_col + me_col
        live = jnp.where(slot < live_total, 1.0, 0.0).astype(jnp.float32)
        tile = tiles[0, 0, slot]
        row_terms[a] += mult_last(x_all[j] * live, tile)
        out[j, :nvec] += mult(x_all[i] * live, tile)
    left, right = [], []
    for a in range(n_col):
        i = me_row * n_col + a
        terms = row_terms[a]
        out[i, :nvec] += terms
        part = packed_gram(x_all[i], terms)
        total = part if a == 0 else total + part
    for block in range(n_row * n_col):
        out[block, nvec : nvec + total.shape[0]] = total


def residual_kernel(scale, x_ref, parts, residual, rayleigh, out):
    own = x_ref[...]
    nvec = own.shape[0]
    both = jnp.sum(parts[...], axis=0)
    half = unpack(both[nvec : nvec + out.shape[1]], nvec)
    ray = (half + half.T) * scale
    rayleigh[...] = ray
    res = both[:nvec] - mult(ray, own)
    residual[...] = res
    part = packed_gram(res, res)
    for block in range(out.shape[0]):
        out[block] = part


def gram_kernel(scale, parts, out):
    out[...] = unpack(jnp.sum(parts[...], axis=0), out.shape[0]) * scale


def per_device(vectors, diagonal_energy, tiles, tile_rows, tile_cols, tile_count):
    n_row = lax.axis_size("row")
    n_col = lax.axis_size("col")
    devices = n_row * n_col
    nvec, width = vectors.shape
    slots = tiles.shape[2]
    scale = 1.0 / float(devices * width)
    packed_rows = nvec * nvec // width
    padded = nvec + 8 * (-(-packed_rows // 8))
    square = jax.ShapeDtypeStruct((nvec, nvec), jnp.float32)
    place = jnp.stack([lax.axis_index("row"), lax.axis_index("col")]).astype(jnp.int32)
    with jax.named_scope("share_vectors"):
        x_all = swap(jnp.broadcast_to(vectors[None], (devices, nvec, width)))
    with jax.named_scope("tile_products"):
        terms = pl.pallas_call(
            functools.partial(products_kernel, n_row, n_col, slots),
            out_shape=jax.ShapeDtypeStruct((devices, padded, width), jnp.float32),
            in_specs=[SMEM] * 4 + [VMEM] * 4,
            out_specs=VMEM,
            scratch_shapes=[pltpu.VMEM((n_col, nvec, width), jnp.float32)],
            compiler_params=pltpu.CompilerParams(vmem_limit_bytes=40 * 2**20),
            name="tile_products",
        )(place, tile_rows, tile_cols, tile_count, vectors, diagonal_energy.reshape(1, width), x_all, tiles)
    with jax.named_scope("return_products"):
        parts = swap(terms)
    with jax.named_scope("residual"):
        residual, rayleigh, grams = pl.pallas_call(
            functools.partial(residual_kernel, scale),
            out_shape=[
                jax.ShapeDtypeStruct((nvec, width), jnp.float32),
                square,
                jax.ShapeDtypeStruct((devices, packed_rows, width), jnp.float32),
            ],
            in_specs=[VMEM] * 2,
            out_specs=[VMEM] * 3,
            compiler_params=pltpu.CompilerParams(vmem_limit_bytes=40 * 2**20),
            name="residual",
        )(vectors, parts)
    with jax.named_scope("gram_sum"):
        gram = pl.pallas_call(
            functools.partial(gram_kernel, scale), out_shape=square, in_specs=[VMEM], out_specs=VMEM, name="gram_sum"
        )(swap(grams))
    return (residual, rayleigh, gram)


def solution(mesh):
    return jax.shard_map(
        per_device,
        mesh=mesh,
        in_specs=(
            P(None, ("row", "col")),
            P(("row", "col")),
            P("row", "col", None, None, None),
            P("row", "col", None),
            P("row", "col", None),
            P("row", "col"),
        ),
        out_specs=(P(None, ("row", "col")), P(), P()),
        check_vma=False,
    )
```

```python
import functools

import jax
import jax.numpy as jnp
from jax import lax
from jax.experimental import pallas as pl
from jax.experimental.pallas import tpu as pltpu
from jax.sharding import PartitionSpec as P

HP = lax.Precision.HIGHEST
VMEM = pl.BlockSpec(memory_space=pltpu.VMEM)
SMEM = pl.BlockSpec(memory_space=pltpu.SMEM)
BOTH = ("row", "col")


def mult(left, right):
    return lax.dot_general(left, right, (((1,), (0,)), ((), ())), precision=HP, preferred_element_type=jnp.float32)


def mult_last(left, right):
    return lax.dot_general(left, right, (((1,), (1,)), ((), ())), precision=HP, preferred_element_type=jnp.float32)


def swap(blocks):
    return lax.all_to_all(blocks, BOTH, 0, 0, tiled=True)


def own_lanes(nvec, width):
    row = lax.broadcasted_iota(jnp.int32, (nvec, width), 0)
    lane = lax.broadcasted_iota(jnp.int32, (nvec, width), 1)
    return lane // nvec == row % (width // nvec)


def packed_gram(left, right):
    nvec, width = left.shape
    per = width // nvec
    wide = mult_last(left, jnp.concatenate([right] * per, axis=0))
    wide = jnp.where(own_lanes(nvec, width), wide, 0.0)
    return jnp.sum(wide.reshape(nvec // per, per, width), axis=1)


def unpack(packed, nvec):
    rows, width = packed.shape
    per = width // nvec
    wide = jnp.concatenate([jnp.broadcast_to(packed[g : g + 1], (per, width)) for g in range(rows)], axis=0)
    wide = jnp.where(own_lanes(nvec, width), wide, 0.0)
    lane = lax.broadcasted_iota(jnp.int32, (width, nvec), 0)
    column = lax.broadcasted_iota(jnp.int32, (width, nvec), 1)
    return mult(wide, (lane % nvec == column).astype(jnp.float32))


def products_kernel(n_row, n_col, slots, place, arow, bcol, count, x_ref, d_ref, x_all, tiles, out, row_terms):
    own = x_ref[...]
    nvec = own.shape[0]
    me_row, me_col = place[0], place[1]
    out[...] = jnp.zeros_like(out)
    half = 0.5 * d_ref[...] * own
    row_terms[...] = jnp.zeros_like(row_terms)
    row_terms[me_col] = half
    out[me_row * n_col + me_col, :nvec] = half
    live_total = count[0, 0]
    for slot in range(slots):
        a = arow[0, 0, slot]
        i = me_row * n_col + a
        j = bcol[0, 0, slot] * n_col + me_col
        live = jnp.where(slot < live_total, 1.0, 0.0).astype(jnp.float32)
        tile = tiles[0, 0, slot]
        row_terms[a] += mult_last(x_all[j] * live, tile)
        out[j, :nvec] += mult(x_all[i] * live, tile)
    left, right = [], []
    for a in range(n_col):
        i = me_row * n_col + a
        terms = row_terms[a]
        out[i, :nvec] += terms
        part = packed_gram(x_all[i], terms)
        total = part if a == 0 else total + part
    for block in range(n_row * n_col):
        out[block, nvec : nvec + total.shape[0]] = total


def residual_kernel(scale, x_ref, parts, residual, rayleigh, out):
    own = x_ref[...]
    nvec = own.shape[0]
    both = jnp.sum(parts[...], axis=0)
    half = unpack(both[nvec : nvec + out.shape[0]], nvec)
    ray = (half + half.T) * scale
    rayleigh[...] = ray
    res = both[:nvec] - mult(ray, own)
    residual[...] = res
    out[...] = packed_gram(res, res)


def gram_kernel(scale, parts, out):
    out[...] = unpack(jnp.sum(parts[...], axis=0), out.shape[0]) * scale


def per_device(vectors, diagonal_energy, tiles, tile_rows, tile_cols, tile_count):
    n_row = lax.axis_size("row")
    n_col = lax.axis_size("col")
    devices = n_row * n_col
    nvec, width = vectors.shape
    slots = tiles.shape[2]
    scale = 1.0 / float(devices * width)
    packed_rows = nvec * nvec // width
    padded = nvec + 8 * (-(-packed_rows // 8))
    square = jax.ShapeDtypeStruct((nvec, nvec), jnp.float32)
    place = jnp.stack([lax.axis_index("row"), lax.axis_index("col")]).astype(jnp.int32)
    with jax.named_scope("share_vectors"):
        x_all = lax.all_gather(vectors, BOTH)
    with jax.named_scope("tile_products"):
        terms = pl.pallas_call(
            functools.partial(products_kernel, n_row, n_col, slots),
            out_shape=jax.ShapeDtypeStruct((devices, padded, width), jnp.float32),
            in_specs=[SMEM] * 4 + [VMEM] * 4,
            out_specs=VMEM,
            scratch_shapes=[pltpu.VMEM((n_col, nvec, width), jnp.float32)],
            compiler_params=pltpu.CompilerParams(vmem_limit_bytes=40 * 2**20),
            name="tile_products",
        )(place, tile_rows, tile_cols, tile_count, vectors, diagonal_energy.reshape(1, width), x_all, tiles)
    with jax.named_scope("return_products"):
        parts = swap(terms)
    with jax.named_scope("residual"):
        residual, rayleigh, part = pl.pallas_call(
            functools.partial(residual_kernel, scale),
            out_shape=[
                jax.ShapeDtypeStruct((nvec, width), jnp.float32),
                square,
                jax.ShapeDtypeStruct((packed_rows, width), jnp.float32),
            ],
            in_specs=[VMEM] * 2,
            out_specs=[VMEM] * 3,
            compiler_params=pltpu.CompilerParams(vmem_limit_bytes=40 * 2**20),
            name="residual",
        )(vectors, parts)
    with jax.named_scope("gram_sum"):
        gram = pl.pallas_call(
            functools.partial(gram_kernel, scale), out_shape=square, in_specs=[VMEM], out_specs=VMEM, name="gram_sum"
        )(lax.all_gather(part, BOTH))
    return (residual, rayleigh, gram)


def solution(mesh):
    return jax.shard_map(
        per_device,
        mesh=mesh,
        in_specs=(
            P(None, ("row", "col")),
            P(("row", "col")),
            P("row", "col", None, None, None),
            P("row", "col", None),
            P("row", "col", None),
            P("row", "col"),
        ),
        out_specs=(P(None, ("row", "col")), P(), P()),
        check_vma=False,
    )
```

```python
import functools

import jax
import jax.numpy as jnp
from jax import lax
from jax.experimental import pallas as pl
from jax.experimental.pallas import tpu as pltpu
from jax.sharding import PartitionSpec as P

HP = lax.Precision.HIGHEST
VMEM = pl.BlockSpec(memory_space=pltpu.VMEM)
SMEM = pl.BlockSpec(memory_space=pltpu.SMEM)


def mult(left, right):
    return lax.dot_general(left, right, (((1,), (0,)), ((), ())), precision=HP, preferred_element_type=jnp.float32)


def mult_last(left, right):
    return lax.dot_general(left, right, (((1,), (1,)), ((), ())), precision=HP, preferred_element_type=jnp.float32)


def swap(blocks, axis):
    return lax.all_to_all(blocks, axis, 0, 0, tiled=True)


def shift(value, axis, step):
    size = lax.axis_size(axis)
    return lax.ppermute(value, axis, [(p, (p + step) % size) for p in range(size)])


def own_lanes(nvec, width):
    row = lax.broadcasted_iota(jnp.int32, (nvec, width), 0)
    lane = lax.broadcasted_iota(jnp.int32, (nvec, width), 1)
    return lane // nvec == row % (width // nvec)


def packed_gram(left, right):
    nvec, width = left.shape
    per = width // nvec
    wide = mult_last(left, jnp.concatenate([right] * per, axis=0))
    wide = jnp.where(own_lanes(nvec, width), wide, 0.0)
    return jnp.sum(wide.reshape(nvec // per, per, width), axis=1)


def unpack(packed, nvec):
    rows, width = packed.shape
    per = width // nvec
    wide = jnp.concatenate([jnp.broadcast_to(packed[g : g + 1], (per, width)) for g in range(rows)], axis=0)
    wide = jnp.where(own_lanes(nvec, width), wide, 0.0)
    lane = lax.broadcasted_iota(jnp.int32, (width, nvec), 0)
    column = lax.broadcasted_iota(jnp.int32, (width, nvec), 1)
    return mult(wide, (lane % nvec == column).astype(jnp.float32))


def column_kernel(n_row, n_col, slots, place, arow, bcol, count, d_ref, *refs):
    x_rows, (x_cols, tiles, out, rows) = refs[:n_col], refs[n_col:]
    nvec, width = x_rows[0].shape
    me_row, me_col = place[0], place[1]
    for step in range(n_col):
        rows[step] = x_rows[step][...]
    out[...] = jnp.zeros_like(out)
    out[me_row, :nvec] = 0.5 * d_ref[...] * x_rows[0][...]
    for slot in range(slots):
        live = jnp.where(slot < count[0, 0], 1.0, 0.0).astype(jnp.float32)
        behind = lax.rem(me_col - arow[0, 0, slot] + n_col, n_col)
        out[bcol[0, 0, slot], :nvec] += mult(rows[behind] * live, tiles[0, 0, slot])
    total = jnp.zeros((nvec * nvec // width, width), jnp.float32)
    for block in range(n_row):
        total += packed_gram(x_cols[block], out[block, :nvec])
    for block in range(n_row):
        out[block, nvec : nvec + total.shape[0]] = total


def row_kernel(n_col, slots, place, arow, bcol, count, d_ref, x_ref, x_cols, tiles, after, out):
    del after
    out[...] = jnp.zeros_like(out)
    out[0] = 0.5 * d_ref[...] * x_ref[...]
    for slot in range(slots):
        live = jnp.where(slot < count[0, 0], 1.0, 0.0).astype(jnp.float32)
        ahead = lax.rem(arow[0, 0, slot] - place[1] + n_col, n_col)
        out[ahead] += mult_last(x_cols[bcol[0, 0, slot]] * live, tiles[0, 0, slot])


def join_kernel(by_row, terms, *outs):
    nvec = terms.shape[1]
    both = jnp.sum(by_row[...], axis=0)
    outs[0][:nvec] = both[:nvec] + terms[0]
    for step in range(1, len(outs)):
        outs[step][:nvec] = terms[step]
    for out in outs:
        out[nvec:] = both[nvec:]


def residual_kernel(scale, x_ref, *refs):
    parts, (residual, rayleigh, out) = refs[:-3], refs[-3:]
    own = x_ref[...]
    nvec = own.shape[0]
    both = parts[0][...]
    for part in parts[1:]:
        both += part[...]
    half = unpack(both[nvec : nvec + out.shape[1]], nvec)
    ray = (half + half.T) * scale
    rayleigh[...] = ray
    res = both[:nvec] - mult(ray, own)
    residual[...] = res
    part = packed_gram(res, res)
    for block in range(out.shape[0]):
        out[block] = part


def gram_kernel(scale, parts, out):
    out[...] = unpack(jnp.sum(parts[...], axis=0), out.shape[0]) * scale


def per_device(vectors, diagonal_energy, tiles, tile_rows, tile_cols, tile_count):
    n_row = lax.axis_size("row")
    n_col = lax.axis_size("col")
    devices = n_row * n_col
    nvec, width = vectors.shape
    slots = tiles.shape[2]
    scale = 1.0 / float(devices * width)
    packed_rows = nvec * nvec // width
    padded = nvec + 8 * (-(-packed_rows // 8))
    block = jax.ShapeDtypeStruct((nvec, width), jnp.float32)
    joined = jax.ShapeDtypeStruct((padded, width), jnp.float32)
    square = jax.ShapeDtypeStruct((nvec, nvec), jnp.float32)
    place = jnp.stack([lax.axis_index("row"), lax.axis_index("col")]).astype(jnp.int32)
    energy = diagonal_energy.reshape(1, width)
    params = pltpu.CompilerParams(vmem_limit_bytes=24 * 2**20)
    with jax.named_scope("share_vectors"):
        x_cols = swap(jnp.broadcast_to(vectors[None], (n_row, nvec, width)), "row")
        x_rows = [vectors] + [shift(vectors, "col", step) for step in range(1, n_col)]
    with jax.named_scope("column_terms"):
        col_terms = pl.pallas_call(
            functools.partial(column_kernel, n_row, n_col, slots),
            out_shape=jax.ShapeDtypeStruct((n_row, padded, width), jnp.float32),
            in_specs=[SMEM] * 4 + [VMEM] * (n_col + 3),
            out_specs=VMEM,
            scratch_shapes=[pltpu.VMEM((n_col, nvec, width), jnp.float32)],
            compiler_params=params,
            cost_estimate=pl.CostEstimate(flops=12 * slots * nvec * width * width, bytes_accessed=2**20, transcendentals=0),
            name="column_terms",
        )(place, tile_rows, tile_cols, tile_count, energy, *x_rows, x_cols, tiles)
    with jax.named_scope("return_column_terms"):
        by_row = swap(col_terms, "row")
    with jax.named_scope("row_terms"):
        row_terms = pl.pallas_call(
            functools.partial(row_kernel, n_col, slots),
            out_shape=jax.ShapeDtypeStruct((n_col, nvec, width), jnp.float32),
            in_specs=[SMEM] * 4 + [VMEM] * 4 + [pl.BlockSpec(memory_space=pl.ANY)],
            out_specs=VMEM,
            compiler_params=params,
            cost_estimate=pl.CostEstimate(flops=12 * slots * nvec * width * width, bytes_accessed=2**20, transcendentals=0),
            name="row_terms",
        )(place, tile_rows, tile_cols, tile_count, energy, vectors, x_cols, tiles, col_terms)
    with jax.named_scope("return_row_terms"):
        sends = pl.pallas_call(
            join_kernel, out_shape=[joined] * n_col, in_specs=[VMEM] * 2, out_specs=[VMEM] * n_col, name="join"
        )(by_row, row_terms)
        parts = [sends[0]] + [shift(sends[step], "col", step) for step in range(1, n_col)]
    with jax.named_scope("residual"):
        residual, rayleigh, grams = pl.pallas_call(
            functools.partial(residual_kernel, scale),
            out_shape=[block, square, jax.ShapeDtypeStruct((devices, packed_rows, width), jnp.float32)],
            in_specs=[VMEM] * (1 + n_col),
            out_specs=[VMEM] * 3,
            compiler_params=params,
            name="residual",
        )(vectors, *parts)
    with jax.named_scope("gram_sum"):
        gram = pl.pallas_call(
            functools.partial(gram_kernel, scale), out_shape=square, in_specs=[VMEM], out_specs=VMEM, name="gram_sum"
        )(swap(grams, ("row", "col")))
    return (residual, rayleigh, gram)


def solution(mesh):
    return jax.shard_map(
        per_device,
        mesh=mesh,
        in_specs=(
            P(None, ("row", "col")),
            P(("row", "col")),
            P("row", "col", None, None, None),
            P("row", "col", None),
            P("row", "col", None),
            P("row", "col"),
        ),
        out_specs=(P(None, ("row", "col")), P(), P()),
        check_vma=False,
    )
```

```python
import functools

import jax
import jax.numpy as jnp
from jax import lax
from jax.experimental import pallas as pl
from jax.experimental.pallas import tpu as pltpu
from jax.sharding import PartitionSpec as P

HP = lax.Precision.HIGHEST
VMEM = pl.BlockSpec(memory_space=pltpu.VMEM)
SMEM = pl.BlockSpec(memory_space=pltpu.SMEM)


def mult(left, right):
    return lax.dot_general(left, right, (((1,), (0,)), ((), ())), precision=HP, preferred_element_type=jnp.float32)


def mult_last(left, right):
    return lax.dot_general(left, right, (((1,), (1,)), ((), ())), precision=HP, preferred_element_type=jnp.float32)


def swap(blocks, axis):
    return lax.all_to_all(blocks, axis, 0, 0, tiled=True)


def shift(value, axis, step):
    size = lax.axis_size(axis)
    return lax.ppermute(value, axis, [(p, (p + step) % size) for p in range(size)])


def own_lanes(nvec, width):
    row = lax.broadcasted_iota(jnp.int32, (nvec, width), 0)
    lane = lax.broadcasted_iota(jnp.int32, (nvec, width), 1)
    return lane // nvec == row % (width // nvec)


def packed_gram(left, right):
    nvec, width = left.shape
    per = width // nvec
    wide = mult_last(left, jnp.concatenate([right] * per, axis=0))
    wide = jnp.where(own_lanes(nvec, width), wide, 0.0)
    return jnp.sum(wide.reshape(nvec // per, per, width), axis=1)


def unpack(packed, nvec):
    rows, width = packed.shape
    per = width // nvec
    wide = jnp.concatenate([jnp.broadcast_to(packed[g : g + 1], (per, width)) for g in range(rows)], axis=0)
    wide = jnp.where(own_lanes(nvec, width), wide, 0.0)
    lane = lax.broadcasted_iota(jnp.int32, (width, nvec), 0)
    column = lax.broadcasted_iota(jnp.int32, (width, nvec), 1)
    return mult(wide, (lane % nvec == column).astype(jnp.float32))


def split(value):
    first = value.astype(jnp.bfloat16)
    rest = value - first.astype(jnp.float32)
    second = rest.astype(jnp.bfloat16)
    return first, second, (rest - second.astype(jnp.float32)).astype(jnp.bfloat16)


def stack_split(value):
    return jnp.concatenate(split(value), axis=0)


def parts_product(stacked, parts, dims):
    nvec = stacked.shape[0] // 3
    total = None
    for used, part in zip((1, 2, 3), parts[::-1]):
        wide = lax.dot_general(stacked[: used * nvec], part, dims, preferred_element_type=jnp.float32)
        for row in reversed(range(used)):
            piece = wide[row * nvec : (row + 1) * nvec]
            total = piece if total is None else total + piece
    return total


def column_kernel(n_row, n_col, slots, place, arow, bcol, count, d_ref, *refs):
    x_rows, (tiles, out, *parts, rows, sums) = refs[:n_col], refs[n_col:]
    me_row, me_col = place[0], place[1]
    for step in range(n_col):
        rows[step] = stack_split(x_rows[step][...])
    sums[...] = jnp.zeros_like(sums)
    sums[me_row] = 0.5 * d_ref[...] * x_rows[0][...]
    for slot in range(slots):
        pieces = split(tiles[0, 0, slot])
        for part, piece in zip(parts, pieces):
            part[slot] = piece
        behind = lax.rem(me_col - arow[0, 0, slot] + n_col, n_col)
        block = jnp.where(slot < count[0, 0], bcol[0, 0, slot], n_row)
        sums[block] += parts_product(rows[behind], pieces, (((1,), (0,)), ((), ())))
    out[...] = sums[:n_row]


def row_kernel(n_row, n_col, slots, place, arow, bcol, count, d_ref, *refs):
    x_rows, (x_cols, col_terms, *parts, out, cols, sums) = refs[:n_col], refs[n_col:]
    nvec, width = x_rows[0].shape
    me_row, me_col = place[0], place[1]
    for block in range(n_row):
        cols[block] = stack_split(x_cols[block])
    sums[...] = jnp.zeros_like(sums)
    sums[0] = 0.5 * d_ref[...] * x_rows[0][...]
    for slot in range(slots):
        behind = lax.rem(me_col - arow[0, 0, slot] + n_col, n_col)
        behind = jnp.where(slot < count[0, 0], behind, n_col)
        pieces = [part[slot] for part in parts]
        sums[behind] += parts_product(cols[bcol[0, 0, slot]], pieces, (((1,), (1,)), ((), ())))
    total = jnp.zeros((nvec * nvec // width, width), jnp.float32)
    for step in range(n_col):
        total += packed_gram(x_rows[step][...], sums[step])
    out[...] = jnp.zeros_like(out)
    for block in range(n_row):
        out[block * n_col + me_col, :nvec] = col_terms[block]
    for step in range(n_col):
        out[me_row * n_col + lax.rem(me_col - step + n_col, n_col), :nvec] += sums[step]
    for block in range(n_row * n_col):
        out[block, nvec : nvec + total.shape[0]] = total


def residual_kernel(scale, x_ref, parts, residual, rayleigh, out):
    own = x_ref[...]
    nvec = own.shape[0]
    both = jnp.sum(parts[...], axis=0)
    half = unpack(both[nvec : nvec + out.shape[1]], nvec)
    ray = (half + half.T) * scale
    rayleigh[...] = ray
    res = both[:nvec] - mult(ray, own)
    residual[...] = res
    part = packed_gram(res, res)
    for block in range(out.shape[0]):
        out[block] = part


def gram_kernel(scale, parts, out):
    out[...] = unpack(jnp.sum(parts[...], axis=0), out.shape[0]) * scale


def per_device(vectors, diagonal_energy, tiles, tile_rows, tile_cols, tile_count):
    n_row = lax.axis_size("row")
    n_col = lax.axis_size("col")
    devices = n_row * n_col
    nvec, width = vectors.shape
    slots = tiles.shape[2]
    scale = 1.0 / float(devices * width)
    packed_rows = nvec * nvec // width
    padded = nvec + 8 * (-(-packed_rows // 8))
    block = jax.ShapeDtypeStruct((nvec, width), jnp.float32)
    square = jax.ShapeDtypeStruct((nvec, nvec), jnp.float32)
    part = jax.ShapeDtypeStruct((slots, width, width), jnp.bfloat16)
    place = jnp.stack([lax.axis_index("row"), lax.axis_index("col")]).astype(jnp.int32)
    energy = diagonal_energy.reshape(1, width)
    params = pltpu.CompilerParams(vmem_limit_bytes=40 * 2**20)
    cost = pl.CostEstimate(flops=12 * slots * nvec * width * width, bytes_accessed=2**20, transcendentals=0)
    with jax.named_scope("share_vectors"):
        x_rows = [vectors] + [shift(vectors, "col", step) for step in range(1, n_col)]
        x_cols = swap(jnp.broadcast_to(vectors[None], (n_row, nvec, width)), "row")
    with jax.named_scope("column_terms"):
        col_terms, *parts = pl.pallas_call(
            functools.partial(column_kernel, n_row, n_col, slots),
            out_shape=[jax.ShapeDtypeStruct((n_row, nvec, width), jnp.float32), part, part, part],
            in_specs=[SMEM] * 4 + [VMEM] * (n_col + 2),
            out_specs=[VMEM] * 4,
            scratch_shapes=[
                pltpu.VMEM((n_col, 3 * nvec, width), jnp.bfloat16),
                pltpu.VMEM((n_row + 1, nvec, width), jnp.float32),
            ],
            compiler_params=params,
            cost_estimate=cost,
            name="column_terms",
        )(place, tile_rows, tile_cols, tile_count, energy, *x_rows, tiles)
    with jax.named_scope("row_terms"):
        terms = pl.pallas_call(
            functools.partial(row_kernel, n_row, n_col, slots),
            out_shape=jax.ShapeDtypeStruct((devices, padded, width), jnp.float32),
            in_specs=[SMEM] * 4 + [VMEM] * (n_col + 6),
            out_specs=VMEM,
            scratch_shapes=[
                pltpu.VMEM((n_row, 3 * nvec, width), jnp.bfloat16),
                pltpu.VMEM((n_col + 1, nvec, width), jnp.float32),
            ],
            compiler_params=params,
            cost_estimate=cost,
            name="row_terms",
        )(place, tile_rows, tile_cols, tile_count, energy, *x_rows, x_cols, col_terms, *parts)
    with jax.named_scope("return_products"):
        sums = swap(terms, ("row", "col"))
    with jax.named_scope("residual"):
        residual, rayleigh, grams = pl.pallas_call(
            functools.partial(residual_kernel, scale),
            out_shape=[block, square, jax.ShapeDtypeStruct((devices, packed_rows, width), jnp.float32)],
            in_specs=[VMEM] * 2,
            out_specs=[VMEM] * 3,
            compiler_params=params,
            name="residual",
        )(vectors, sums)
    with jax.named_scope("gram_sum"):
        gram = pl.pallas_call(
            functools.partial(gram_kernel, scale), out_shape=square, in_specs=[VMEM], out_specs=VMEM, name="gram_sum"
        )(swap(grams, ("row", "col")))
    return (residual, rayleigh, gram)


def solution(mesh):
    return jax.shard_map(
        per_device,
        mesh=mesh,
        in_specs=(
            P(None, ("row", "col")),
            P(("row", "col")),
            P("row", "col", None, None, None),
            P("row", "col", None),
            P("row", "col", None),
            P("row", "col"),
        ),
        out_specs=(P(None, ("row", "col")), P(), P()),
        check_vma=False,
    )
```

```python
import functools

import jax
import jax.numpy as jnp
from jax import lax
from jax.experimental import pallas as pl
from jax.experimental.pallas import tpu as pltpu
from jax.sharding import PartitionSpec as P

HP = lax.Precision.HIGHEST
VMEM = pl.BlockSpec(memory_space=pltpu.VMEM)
SMEM = pl.BlockSpec(memory_space=pltpu.SMEM)


def mult(left, right):
    return lax.dot_general(left, right, (((1,), (0,)), ((), ())), precision=HP, preferred_element_type=jnp.float32)


def mult_last(left, right):
    return lax.dot_general(left, right, (((1,), (1,)), ((), ())), precision=HP, preferred_element_type=jnp.float32)


def swap(blocks, axis):
    return lax.all_to_all(blocks, axis, 0, 0, tiled=True)


def trade(value, axis, flip):
    size = lax.axis_size(axis)
    return lax.ppermute(value, axis, [(p, p ^ flip) for p in range(size)])


def own_lanes(nvec, width):
    row = lax.broadcasted_iota(jnp.int32, (nvec, width), 0)
    lane = lax.broadcasted_iota(jnp.int32, (nvec, width), 1)
    return lane // nvec == row % (width // nvec)


def packed_gram(left, right):
    nvec, width = left.shape
    per = width // nvec
    wide = mult_last(left, jnp.concatenate([right] * per, axis=0))
    wide = jnp.where(own_lanes(nvec, width), wide, 0.0)
    return jnp.sum(wide.reshape(nvec // per, per, width), axis=1)


def unpack(packed, nvec):
    rows, width = packed.shape
    per = width // nvec
    wide = jnp.concatenate([jnp.broadcast_to(packed[g : g + 1], (per, width)) for g in range(rows)], axis=0)
    wide = jnp.where(own_lanes(nvec, width), wide, 0.0)
    lane = lax.broadcasted_iota(jnp.int32, (width, nvec), 0)
    column = lax.broadcasted_iota(jnp.int32, (width, nvec), 1)
    return mult(wide, (lane % nvec == column).astype(jnp.float32))


def split(value):
    first = value.astype(jnp.bfloat16)
    rest = value - first.astype(jnp.float32)
    second = rest.astype(jnp.bfloat16)
    return first, second, (rest - second.astype(jnp.float32)).astype(jnp.bfloat16)


def stack_split(value):
    return jnp.concatenate(split(value), axis=0)


def parts_product(stacked, parts, dims):
    nvec = stacked.shape[0] // 3
    total = None
    for used, part in zip((1, 2, 3), parts[::-1]):
        wide = lax.dot_general(stacked[: used * nvec], part, dims, preferred_element_type=jnp.float32)
        for row in reversed(range(used)):
            piece = wide[row * nvec : (row + 1) * nvec]
            total = piece if total is None else total + piece
    return total


def pair_kernel(x_ref, other, out):
    out[0] = x_ref[...]
    out[1] = other[...]


def column_kernel(n_row, n_col, slots, place, arow, bcol, count, d_ref, *refs):
    x_rows, (tiles, out, *parts, rows, sums) = refs[:n_col], refs[n_col:]
    me_row, me_col = place[0], place[1]
    for flip in range(n_col):
        rows[flip] = stack_split(x_rows[flip][...])
    sums[...] = jnp.zeros_like(sums)
    sums[0] = 0.5 * d_ref[...] * x_rows[0][...]
    for slot in range(slots):
        pieces = split(tiles[0, 0, slot])
        for part, piece in zip(parts, pieces):
            part[slot] = piece
        block = jnp.where(slot < count[0, 0], bcol[0, 0, slot] ^ me_row, n_row)
        sums[block] += parts_product(rows[arow[0, 0, slot] ^ me_col], pieces, (((1,), (0,)), ((), ())))
    out[...] = sums[:n_row]


def row_kernel(n_row, n_col, slots, place, arow, bcol, count, d_ref, *refs):
    x_rows, refs = refs[:n_col], refs[n_col:]
    x_pairs, (col_terms, *parts, out, to_core, cols, sums) = refs[: n_row // 2], refs[n_row // 2 :]
    nvec, width = x_rows[0].shape
    me_row, me_col = place[0], place[1]
    for flip in range(n_row):
        cols[flip] = stack_split(x_pairs[flip // 2][flip % 2])
    sums[...] = jnp.zeros_like(sums)
    sums[0] = 0.5 * d_ref[...] * x_rows[0][...]
    for slot in range(slots):
        block = jnp.where(slot < count[0, 0], arow[0, 0, slot] ^ me_col, n_col)
        pieces = [part[slot] for part in parts]
        sums[block] += parts_product(cols[bcol[0, 0, slot] ^ me_row], pieces, (((1,), (1,)), ((), ())))
    out[...] = sums[:n_col]
    for chip in range(n_row // 2):
        to_core[chip * nvec : (chip + 1) * nvec] = col_terms[2 * chip + 1]
    total = packed_gram(x_rows[0][...], sums[0])
    for flip in range(1, n_col):
        total += packed_gram(x_rows[flip][...], sums[flip])
    to_core[n_row // 2 * nvec :] = jnp.concatenate([total, jnp.zeros((to_core.shape[0] - n_row // 2 * nvec - total.shape[0], width), jnp.float32)], axis=0)


def chip_kernel(col_terms, mine, other, *outs):
    nvec = col_terms.shape[1]
    tail = len(outs) * nvec
    for chip, out in enumerate(outs):
        out[:nvec] = col_terms[2 * chip] + other[chip * nvec : (chip + 1) * nvec]
        out[nvec:] = mine[tail:] + other[tail:]


def join_kernel(n_chip, *refs):
    by_row, (terms, *outs) = refs[:n_chip], refs[n_chip:]
    nvec = terms.shape[1]
    both = by_row[0][...]
    for part in by_row[1:]:
        both += part[...]
    outs[0][:nvec] = both[:nvec] + terms[0]
    for flip in range(1, len(outs)):
        outs[flip][:nvec] = terms[flip]
    for out in outs:
        out[nvec:] = both[nvec:]


def residual_kernel(scale, x_ref, *refs):
    parts, (residual, rayleigh, out) = refs[:-3], refs[-3:]
    own = x_ref[...]
    nvec = own.shape[0]
    both = parts[0][...]
    for part in parts[1:]:
        both += part[...]
    half = unpack(both[nvec : nvec + out.shape[1]], nvec)
    ray = (half + half.T) * scale
    rayleigh[...] = ray
    res = both[:nvec] - mult(ray, own)
    residual[...] = res
    part = packed_gram(res, res)
    for block in range(out.shape[0]):
        out[block] = part


def gram_kernel(scale, parts, out):
    out[...] = unpack(jnp.sum(parts[...], axis=0), out.shape[0]) * scale


def per_device(vectors, diagonal_energy, tiles, tile_rows, tile_cols, tile_count):
    n_row = lax.axis_size("row")
    n_col = lax.axis_size("col")
    devices = n_row * n_col
    nvec, width = vectors.shape
    slots = tiles.shape[2]
    scale = 1.0 / float(devices * width)
    packed_rows = nvec * nvec // width
    padded = nvec + 8 * (-(-packed_rows // 8))
    n_chip = n_row // 2
    block = jax.ShapeDtypeStruct((nvec, width), jnp.float32)
    joined = jax.ShapeDtypeStruct((padded, width), jnp.float32)
    square = jax.ShapeDtypeStruct((nvec, nvec), jnp.float32)
    part = jax.ShapeDtypeStruct((slots, width, width), jnp.bfloat16)
    place = jnp.stack([lax.axis_index("row"), lax.axis_index("col")]).astype(jnp.int32)
    energy = diagonal_energy.reshape(1, width)
    params = pltpu.CompilerParams(vmem_limit_bytes=24 * 2**20)
    cost = pl.CostEstimate(flops=12 * slots * nvec * width * width, bytes_accessed=2**20, transcendentals=0)
    with jax.named_scope("share_vectors"):
        other = trade(vectors, "row", 1)
        x_rows = [vectors] + [trade(vectors, "col", flip) for flip in range(1, n_col)]
        pair = pl.pallas_call(
            pair_kernel,
            out_shape=jax.ShapeDtypeStruct((2, nvec, width), jnp.float32),
            in_specs=[VMEM] * 2,
            out_specs=VMEM,
            name="pair",
        )(vectors, other)
        x_pairs = [pair] + [trade(pair, "row", 2 * chip) for chip in range(1, n_chip)]
    with jax.named_scope("column_terms"):
        col_terms, *parts = pl.pallas_call(
            functools.partial(column_kernel, n_row, n_col, slots),
            out_shape=[jax.ShapeDtypeStruct((n_row, nvec, width), jnp.float32), part, part, part],
            in_specs=[SMEM] * 4 + [VMEM] * (n_col + 2),
            out_specs=[VMEM] * 4,
            scratch_shapes=[
                pltpu.VMEM((n_col, 3 * nvec, width), jnp.bfloat16),
                pltpu.VMEM((n_row + 1, nvec, width), jnp.float32),
            ],
            compiler_params=params,
            cost_estimate=cost,
            name="column_terms",
        )(place, tile_rows, tile_cols, tile_count, energy, *x_rows, tiles)
    with jax.named_scope("row_terms"):
        row_terms, to_core = pl.pallas_call(
            functools.partial(row_kernel, n_row, n_col, slots),
            out_shape=[
                jax.ShapeDtypeStruct((n_col, nvec, width), jnp.float32),
                jax.ShapeDtypeStruct((n_chip * nvec + padded - nvec, width), jnp.float32),
            ],
            in_specs=[SMEM] * 4 + [VMEM] * (1 + n_col + n_chip + 4),
            out_specs=[VMEM] * 2,
            scratch_shapes=[
                pltpu.VMEM((n_row, 3 * nvec, width), jnp.bfloat16),
                pltpu.VMEM((n_col + 1, nvec, width), jnp.float32),
            ],
            compiler_params=params,
            cost_estimate=cost,
            name="row_terms",
        )(place, tile_rows, tile_cols, tile_count, energy, *x_rows, *x_pairs, col_terms, *parts)
    with jax.named_scope("return_products"):
        chips = pl.pallas_call(
            chip_kernel, out_shape=[joined] * n_chip, in_specs=[VMEM] * 3, out_specs=[VMEM] * n_chip, name="chip_sum"
        )(col_terms, to_core, trade(to_core, "row", 1))
        by_row = [chips[0]] + [trade(chips[chip], "row", 2 * chip) for chip in range(1, n_chip)]
        sends = pl.pallas_call(
            functools.partial(join_kernel, n_chip),
            out_shape=[joined] * n_col,
            in_specs=[VMEM] * (n_chip + 1),
            out_specs=[VMEM] * n_col,
            name="row_sum",
        )(*by_row, row_terms)
        sums = [sends[0]] + [trade(sends[flip], "col", flip) for flip in range(1, n_col)]
    with jax.named_scope("residual"):
        residual, rayleigh, grams = pl.pallas_call(
            functools.partial(residual_kernel, scale),
            out_shape=[block, square, jax.ShapeDtypeStruct((devices, packed_rows, width), jnp.float32)],
            in_specs=[VMEM] * (1 + n_col),
            out_specs=[VMEM] * 3,
            compiler_params=params,
            name="residual",
        )(vectors, *sums)
    with jax.named_scope("gram_sum"):
        gram = pl.pallas_call(
            functools.partial(gram_kernel, scale), out_shape=square, in_specs=[VMEM], out_specs=VMEM, name="gram_sum"
        )(swap(grams, ("row", "col")))
    return (residual, rayleigh, gram)


def solution(mesh):
    return jax.shard_map(
        per_device,
        mesh=mesh,
        in_specs=(
            P(None, ("row", "col")),
            P(("row", "col")),
            P("row", "col", None, None, None),
            P("row", "col", None),
            P("row", "col", None),
            P("row", "col"),
        ),
        out_specs=(P(None, ("row", "col")), P(), P()),
        check_vma=False,
    )
```

```python
import functools

import jax
import jax.numpy as jnp
from jax import lax
from jax.experimental import pallas as pl
from jax.experimental.pallas import tpu as pltpu
from jax.sharding import PartitionSpec as P

HP = lax.Precision.HIGHEST
VMEM = pl.BlockSpec(memory_space=pltpu.VMEM)
SMEM = pl.BlockSpec(memory_space=pltpu.SMEM)


def mult(left, right):
    return lax.dot_general(left, right, (((1,), (0,)), ((), ())), precision=HP, preferred_element_type=jnp.float32)


def mult_last(left, right):
    return lax.dot_general(left, right, (((1,), (1,)), ((), ())), precision=HP, preferred_element_type=jnp.float32)


def swap(blocks, axis):
    return lax.all_to_all(blocks, axis, 0, 0, tiled=True)


def trade(value, axis, flip):
    size = lax.axis_size(axis)
    return lax.ppermute(value, axis, [(p, p ^ flip) for p in range(size)])


def own_lanes(nvec, width):
    row = lax.broadcasted_iota(jnp.int32, (nvec, width), 0)
    lane = lax.broadcasted_iota(jnp.int32, (nvec, width), 1)
    return lane // nvec == row % (width // nvec)


def packed_gram(left, right):
    nvec, width = left.shape
    per = width // nvec
    wide = mult_last(left, jnp.concatenate([right] * per, axis=0))
    wide = jnp.where(own_lanes(nvec, width), wide, 0.0)
    return jnp.sum(wide.reshape(nvec // per, per, width), axis=1)


def unpack(packed, nvec):
    rows, width = packed.shape
    per = width // nvec
    wide = jnp.concatenate([jnp.broadcast_to(packed[g : g + 1], (per, width)) for g in range(rows)], axis=0)
    wide = jnp.where(own_lanes(nvec, width), wide, 0.0)
    lane = lax.broadcasted_iota(jnp.int32, (width, nvec), 0)
    column = lax.broadcasted_iota(jnp.int32, (width, nvec), 1)
    return mult(wide, (lane % nvec == column).astype(jnp.float32))


def split(value):
    first = value.astype(jnp.bfloat16)
    rest = value - first.astype(jnp.float32)
    second = rest.astype(jnp.bfloat16)
    return first, second, (rest - second.astype(jnp.float32)).astype(jnp.bfloat16)


def stack_split(value):
    return jnp.concatenate(split(value), axis=0)


def parts_product(stacked, parts, dims):
    nvec = stacked.shape[0] // 3
    total = None
    for used, part in zip((1, 2, 3), parts[::-1]):
        wide = lax.dot_general(stacked[: used * nvec], part, dims, preferred_element_type=jnp.float32)
        for row in reversed(range(used)):
            piece = wide[row * nvec : (row + 1) * nvec]
            total = piece if total is None else total + piece
    return total


def pair_kernel(x_ref, other, out):
    out[0] = x_ref[...]
    out[1] = other[...]


def products_kernel(n_row, n_col, slots, place, arow, bcol, count, d_ref, *refs):
    x_rows, refs = refs[:n_col], refs[n_col:]
    x_pairs, refs = refs[: n_row // 2], refs[n_row // 2 :]
    tiles, row_out, col_out, to_core, rows, cols, row_sums, col_sums, held, sems = refs
    nvec, width = x_rows[0].shape
    me_row, me_col = place[0], place[1]
    copies = [pltpu.make_async_copy(tiles.at[0, 0, slot], held.at[slot], sems.at[slot]) for slot in range(slots)]
    for copy in copies:
        copy.start()
    for flip in range(n_col):
        rows[flip] = stack_split(x_rows[flip][...])
    for flip in range(n_row):
        cols[flip] = stack_split(x_pairs[flip // 2][flip % 2])
    half = 0.5 * d_ref[...] * x_rows[0][...]
    row_sums[...] = jnp.zeros_like(row_sums)
    col_sums[...] = jnp.zeros_like(col_sums)
    row_sums[0] = half
    col_sums[0] = half
    for slot in range(slots):
        live = slot < count[0, 0]
        i = arow[0, 0, slot] ^ me_col
        j = bcol[0, 0, slot] ^ me_row
        copies[slot].wait()
        pieces = split(held[slot])
        row_sums[jnp.where(live, i, n_col)] += parts_product(cols[j], pieces, (((1,), (1,)), ((), ())))
        col_sums[jnp.where(live, j, n_row)] += parts_product(rows[i], pieces, (((1,), (0,)), ((), ())))
    total = packed_gram(x_rows[0][...], row_sums[0])
    for flip in range(1, n_col):
        total += packed_gram(x_rows[flip][...], row_sums[flip])
    row_out[...] = row_sums[:n_col]
    for chip in range(n_row // 2):
        col_out[chip] = col_sums[2 * chip]
        to_core[chip * nvec : (chip + 1) * nvec] = col_sums[2 * chip + 1]
    rest = jnp.zeros((to_core.shape[0] - n_row // 2 * nvec - total.shape[0], width), jnp.float32)
    to_core[n_row // 2 * nvec :] = jnp.concatenate([total, rest], axis=0)


def chip_kernel(col_terms, mine, other, *outs):
    nvec = col_terms.shape[1]
    tail = len(outs) * nvec
    for chip, out in enumerate(outs):
        out[:nvec] = col_terms[chip] + other[chip * nvec : (chip + 1) * nvec]
        out[nvec:] = mine[tail:] + other[tail:]


def join_kernel(n_chip, *refs):
    by_row, (terms, *outs) = refs[:n_chip], refs[n_chip:]
    nvec = terms.shape[1]
    both = by_row[0][...]
    for part in by_row[1:]:
        both += part[...]
    outs[0][:nvec] = both[:nvec] + terms[0]
    for flip in range(1, len(outs)):
        outs[flip][:nvec] = terms[flip]
    for out in outs:
        out[nvec:] = both[nvec:]


def residual_kernel(scale, x_ref, *refs):
    parts, (residual, rayleigh, out) = refs[:-3], refs[-3:]
    own = x_ref[...]
    nvec = own.shape[0]
    both = parts[0][...]
    for part in parts[1:]:
        both += part[...]
    half = unpack(both[nvec : nvec + out.shape[1]], nvec)
    ray = (half + half.T) * scale
    rayleigh[...] = ray
    res = both[:nvec] - mult(ray, own)
    residual[...] = res
    part = packed_gram(res, res)
    for block in range(out.shape[0]):
        out[block] = part


def gram_kernel(scale, parts, out):
    out[...] = unpack(jnp.sum(parts[...], axis=0), out.shape[0]) * scale


def per_device(vectors, diagonal_energy, tiles, tile_rows, tile_cols, tile_count):
    n_row = lax.axis_size("row")
    n_col = lax.axis_size("col")
    devices = n_row * n_col
    nvec, width = vectors.shape
    slots = tiles.shape[2]
    scale = 1.0 / float(devices * width)
    packed_rows = nvec * nvec // width
    padded = nvec + 8 * (-(-packed_rows // 8))
    n_chip = n_row // 2
    block = jax.ShapeDtypeStruct((nvec, width), jnp.float32)
    joined = jax.ShapeDtypeStruct((padded, width), jnp.float32)
    square = jax.ShapeDtypeStruct((nvec, nvec), jnp.float32)
    place = jnp.stack([lax.axis_index("row"), lax.axis_index("col")]).astype(jnp.int32)
    energy = diagonal_energy.reshape(1, width)
    params = pltpu.CompilerParams(vmem_limit_bytes=16 * 2**20)
    with jax.named_scope("share_vectors"):
        other = trade(vectors, "row", 1)
        x_rows = [vectors] + [trade(vectors, "col", flip) for flip in range(1, n_col)]
        pair = pl.pallas_call(
            pair_kernel,
            out_shape=jax.ShapeDtypeStruct((2, nvec, width), jnp.float32),
            in_specs=[VMEM] * 2,
            out_specs=VMEM,
            compiler_params=params,
            name="pair",
        )(vectors, other)
        x_pairs = [pair] + [trade(pair, "row", 2 * chip) for chip in range(1, n_chip)]
    with jax.named_scope("tile_products"):
        row_terms, col_terms, to_core = pl.pallas_call(
            functools.partial(products_kernel, n_row, n_col, slots),
            out_shape=[
                jax.ShapeDtypeStruct((n_col, nvec, width), jnp.float32),
                jax.ShapeDtypeStruct((n_chip, nvec, width), jnp.float32),
                jax.ShapeDtypeStruct((n_chip * nvec + padded - nvec, width), jnp.float32),
            ],
            in_specs=[SMEM] * 4 + [VMEM] * (1 + n_col + n_chip) + [pl.BlockSpec(memory_space=pl.ANY)],
            out_specs=[VMEM] * 3,
            scratch_shapes=[
                pltpu.VMEM((n_col, 3 * nvec, width), jnp.bfloat16),
                pltpu.VMEM((n_row, 3 * nvec, width), jnp.bfloat16),
                pltpu.VMEM((n_col + 1, nvec, width), jnp.float32),
                pltpu.VMEM((n_row + 1, nvec, width), jnp.float32),
                pltpu.VMEM((slots, width, width), jnp.float32),
                pltpu.SemaphoreType.DMA((slots,)),
            ],
            compiler_params=pltpu.CompilerParams(vmem_limit_bytes=53 * 2**20),
            cost_estimate=pl.CostEstimate(flops=24 * slots * nvec * width * width, bytes_accessed=2**20, transcendentals=0),
            name="tile_products",
        )(place, tile_rows, tile_cols, tile_count, energy, *x_rows, *x_pairs, tiles)
    with jax.named_scope("return_products"):
        chips = pl.pallas_call(
            chip_kernel,
            out_shape=[joined] * n_chip,
            in_specs=[VMEM] * 3,
            out_specs=[VMEM] * n_chip,
            compiler_params=params,
            name="chip_sum",
        )(col_terms, to_core, trade(to_core, "row", 1))
        by_row = [chips[0]] + [trade(chips[chip], "row", 2 * chip) for chip in range(1, n_chip)]
        sends = pl.pallas_call(
            functools.partial(join_kernel, n_chip),
            out_shape=[joined] * n_col,
            in_specs=[VMEM] * (n_chip + 1),
            out_specs=[VMEM] * n_col,
            compiler_params=params,
            name="row_sum",
        )(*by_row, row_terms)
        sums = [sends[0]] + [trade(sends[flip], "col", flip) for flip in range(1, n_col)]
    with jax.named_scope("residual"):
        residual, rayleigh, grams = pl.pallas_call(
            functools.partial(residual_kernel, scale),
            out_shape=[block, square, jax.ShapeDtypeStruct((devices, packed_rows, width), jnp.float32)],
            in_specs=[VMEM] * (1 + n_col),
            out_specs=[VMEM] * 3,
            compiler_params=params,
            name="residual",
        )(vectors, *sums)
    with jax.named_scope("gram_sum"):
        gram = pl.pallas_call(
            functools.partial(gram_kernel, scale),
            out_shape=square,
            in_specs=[VMEM],
            out_specs=VMEM,
            compiler_params=params,
            name="gram_sum",
        )(swap(grams, ("row", "col")))
    return (residual, rayleigh, gram)


def solution(mesh):
    return jax.shard_map(
        per_device,
        mesh=mesh,
        in_specs=(
            P(None, ("row", "col")),
            P(("row", "col")),
            P("row", "col", None, None, None),
            P("row", "col", None),
            P("row", "col", None),
            P("row", "col"),
        ),
        out_specs=(P(None, ("row", "col")), P(), P()),
        check_vma=False,
    )
```

```python
import functools

import jax
import jax.numpy as jnp
from jax import lax
from jax.experimental import pallas as pl
from jax.experimental.pallas import tpu as pltpu
from jax.sharding import PartitionSpec as P

HP = lax.Precision.HIGHEST
VMEM = pl.BlockSpec(memory_space=pltpu.VMEM)
SMEM = pl.BlockSpec(memory_space=pltpu.SMEM)
CHUNKS = 4


def mult(left, right):
    return lax.dot_general(left, right, (((1,), (0,)), ((), ())), precision=HP, preferred_element_type=jnp.float32)


def mult_last(left, right):
    return lax.dot_general(left, right, (((1,), (1,)), ((), ())), precision=HP, preferred_element_type=jnp.float32)


def swap(blocks, axis):
    return lax.all_to_all(blocks, axis, 0, 0, tiled=True)


def trade(value, axis, flip):
    size = lax.axis_size(axis)
    return lax.ppermute(value, axis, [(p, p ^ flip) for p in range(size)])


def own_lanes(nvec, width):
    row = lax.broadcasted_iota(jnp.int32, (nvec, width), 0)
    lane = lax.broadcasted_iota(jnp.int32, (nvec, width), 1)
    return lane // nvec == row % (width // nvec)


def packed_gram(left, right):
    nvec, width = left[0].shape
    per = width // nvec
    right = jnp.concatenate(right, axis=1)
    wide = mult_last(jnp.concatenate(left, axis=1), jnp.concatenate([right] * per, axis=0))
    wide = jnp.where(own_lanes(nvec, width), wide, 0.0)
    return jnp.sum(wide.reshape(nvec // per, per, width), axis=1)


def unpack(packed, nvec):
    rows, width = packed.shape
    per = width // nvec
    wide = jnp.concatenate([jnp.broadcast_to(packed[g : g + 1], (per, width)) for g in range(rows)], axis=0)
    wide = jnp.where(own_lanes(nvec, width), wide, 0.0)
    lane = lax.broadcasted_iota(jnp.int32, (width, nvec), 0)
    column = lax.broadcasted_iota(jnp.int32, (width, nvec), 1)
    return mult(wide, (lane % nvec == column).astype(jnp.float32))


def split(value):
    first = value.astype(jnp.bfloat16)
    rest = value - first.astype(jnp.float32)
    second = rest.astype(jnp.bfloat16)
    return first, second, (rest - second.astype(jnp.float32)).astype(jnp.bfloat16)


def stack_split(value):
    return jnp.concatenate(split(value), axis=0)


def parts_product(stacked, parts, dims):
    nvec = stacked.shape[0] // 3
    total = None
    for used, part in zip((1, 2, 3), parts[::-1]):
        wide = lax.dot_general(stacked[: used * nvec], part, dims, preferred_element_type=jnp.float32)
        for row in reversed(range(used)):
            piece = wide[row * nvec : (row + 1) * nvec]
            total = piece if total is None else total + piece
    return total


def pair_kernel(x_ref, other, out):
    out[0] = x_ref[...]
    out[1] = other[...]


def products_kernel(n_row, n_col, slots, place, arow, bcol, count, d_ref, *refs):
    x_rows, refs = refs[:n_col], refs[n_col:]
    x_pairs, refs = refs[: n_row // 2], refs[n_row // 2 :]
    tiles, row_out, col_out, to_core, rows, cols, row_sums, col_sums, held, sems = refs
    nvec, width = x_rows[0].shape
    me_row, me_col = place[0], place[1]
    group = slots // CHUNKS
    copies = [
        pltpu.make_async_copy(tiles.at[0, 0, pl.ds(k * group, group)], held.at[pl.ds(k * group, group)], sems.at[k])
        for k in range(CHUNKS)
    ]
    for copy in copies:
        copy.start()
    for flip in range(n_col):
        rows[flip] = stack_split(x_rows[flip][...])
    for flip in range(n_row):
        cols[flip] = stack_split(x_pairs[flip // 2][flip % 2])
    half = 0.5 * d_ref[...] * x_rows[0][...]
    row_sums[...] = jnp.zeros_like(row_sums)
    col_sums[...] = jnp.zeros_like(col_sums)
    row_sums[0] = half
    col_sums[0] = half
    for slot in range(slots):
        live = slot < count[0, 0]
        i = arow[0, 0, slot] ^ me_col
        j = bcol[0, 0, slot] ^ me_row
        if slot % group == 0:
            copies[slot // group].wait()
        pieces = split(held[slot])
        row_sums[jnp.where(live, i, n_col)] += parts_product(cols[j], pieces, (((1,), (1,)), ((), ())))
        col_sums[jnp.where(live, j, n_row)] += parts_product(rows[i], pieces, (((1,), (0,)), ((), ())))
    total = packed_gram([x[...] for x in x_rows], [row_sums[flip] for flip in range(n_col)])
    row_out[...] = row_sums[:n_col]
    for chip in range(n_row // 2):
        col_out[chip] = col_sums[2 * chip]
        to_core[chip * nvec : (chip + 1) * nvec] = col_sums[2 * chip + 1]
    rest = jnp.zeros((to_core.shape[0] - n_row // 2 * nvec - total.shape[0], width), jnp.float32)
    to_core[n_row // 2 * nvec :] = jnp.concatenate([total, rest], axis=0)


def chip_kernel(col_terms, mine, other, *outs):
    nvec = col_terms.shape[1]
    tail = len(outs) * nvec
    for chip, out in enumerate(outs):
        out[:nvec] = col_terms[chip] + other[chip * nvec : (chip + 1) * nvec]
        out[nvec:] = mine[tail:] + other[tail:]


def join_kernel(n_chip, *refs):
    by_row, (terms, *outs) = refs[:n_chip], refs[n_chip:]
    nvec = terms.shape[1]
    both = by_row[0][...]
    for part in by_row[1:]:
        both += part[...]
    outs[0][:nvec] = both[:nvec] + terms[0]
    for flip in range(1, len(outs)):
        outs[flip][:nvec] = terms[flip]
    for out in outs:
        out[nvec:] = both[nvec:]


def residual_kernel(scale, x_ref, *refs):
    parts, (residual, rayleigh, out) = refs[:-3], refs[-3:]
    own = x_ref[...]
    nvec = own.shape[0]
    both = parts[0][...]
    for part in parts[1:]:
        both += part[...]
    half = unpack(both[nvec : nvec + out.shape[1]], nvec)
    ray = (half + half.T) * scale
    rayleigh[...] = ray
    res = both[:nvec] - mult(ray, own)
    residual[...] = res
    part = packed_gram([res], [res])
    for block in range(out.shape[0]):
        out[block] = part


def gram_kernel(scale, parts, out):
    out[...] = unpack(jnp.sum(parts[...], axis=0), out.shape[0]) * scale


def per_device(vectors, diagonal_energy, tiles, tile_rows, tile_cols, tile_count):
    n_row = lax.axis_size("row")
    n_col = lax.axis_size("col")
    devices = n_row * n_col
    nvec, width = vectors.shape
    slots = tiles.shape[2]
    scale = 1.0 / float(devices * width)
    packed_rows = nvec * nvec // width
    padded = nvec + 8 * (-(-packed_rows // 8))
    n_chip = n_row // 2
    block = jax.ShapeDtypeStruct((nvec, width), jnp.float32)
    joined = jax.ShapeDtypeStruct((padded, width), jnp.float32)
    square = jax.ShapeDtypeStruct((nvec, nvec), jnp.float32)
    place = jnp.stack([lax.axis_index("row"), lax.axis_index("col")]).astype(jnp.int32)
    energy = diagonal_energy.reshape(1, width)
    params = pltpu.CompilerParams(vmem_limit_bytes=16 * 2**20)
    with jax.named_scope("share_vectors"):
        other = trade(vectors, "row", 1)
        x_rows = [vectors] + [trade(vectors, "col", flip) for flip in range(1, n_col)]
        pair = pl.pallas_call(
            pair_kernel,
            out_shape=jax.ShapeDtypeStruct((2, nvec, width), jnp.float32),
            in_specs=[VMEM] * 2,
            out_specs=VMEM,
            compiler_params=params,
            name="pair",
        )(vectors, other)
        x_pairs = [pair] + [trade(pair, "row", 2 * chip) for chip in range(1, n_chip)]
    with jax.named_scope("tile_products"):
        row_terms, col_terms, to_core = pl.pallas_call(
            functools.partial(products_kernel, n_row, n_col, slots),
            out_shape=[
                jax.ShapeDtypeStruct((n_col, nvec, width), jnp.float32),
                jax.ShapeDtypeStruct((n_chip, nvec, width), jnp.float32),
                jax.ShapeDtypeStruct((n_chip * nvec + padded - nvec, width), jnp.float32),
            ],
            in_specs=[SMEM] * 4 + [VMEM] * (1 + n_col + n_chip) + [pl.BlockSpec(memory_space=pl.ANY)],
            out_specs=[VMEM] * 3,
            scratch_shapes=[
                pltpu.VMEM((n_col, 3 * nvec, width), jnp.bfloat16),
                pltpu.VMEM((n_row, 3 * nvec, width), jnp.bfloat16),
                pltpu.VMEM((n_col + 1, nvec, width), jnp.float32),
                pltpu.VMEM((n_row + 1, nvec, width), jnp.float32),
                pltpu.VMEM((slots, width, width), jnp.float32),
                pltpu.SemaphoreType.DMA((CHUNKS,)),
            ],
            compiler_params=pltpu.CompilerParams(vmem_limit_bytes=53 * 2**20),
            cost_estimate=pl.CostEstimate(flops=24 * slots * nvec * width * width, bytes_accessed=2**20, transcendentals=0),
            name="tile_products",
        )(place, tile_rows, tile_cols, tile_count, energy, *x_rows, *x_pairs, tiles)
    with jax.named_scope("return_products"):
        chips = pl.pallas_call(
            chip_kernel,
            out_shape=[joined] * n_chip,
            in_specs=[VMEM] * 3,
            out_specs=[VMEM] * n_chip,
            compiler_params=params,
            name="chip_sum",
        )(col_terms, to_core, trade(to_core, "row", 1))
        by_row = [chips[0]] + [trade(chips[chip], "row", 2 * chip) for chip in range(1, n_chip)]
        sends = pl.pallas_call(
            functools.partial(join_kernel, n_chip),
            out_shape=[joined] * n_col,
            in_specs=[VMEM] * (n_chip + 1),
            out_specs=[VMEM] * n_col,
            compiler_params=params,
            name="row_sum",
        )(*by_row, row_terms)
        sums = [sends[0]] + [trade(sends[flip], "col", flip) for flip in range(1, n_col)]
    with jax.named_scope("residual"):
        residual, rayleigh, grams = pl.pallas_call(
            functools.partial(residual_kernel, scale),
            out_shape=[block, square, jax.ShapeDtypeStruct((devices, packed_rows, width), jnp.float32)],
            in_specs=[VMEM] * (1 + n_col),
            out_specs=[VMEM] * 3,
            compiler_params=params,
            name="residual",
        )(vectors, *sums)
    with jax.named_scope("gram_sum"):
        gram = pl.pallas_call(
            functools.partial(gram_kernel, scale),
            out_shape=square,
            in_specs=[VMEM],
            out_specs=VMEM,
            compiler_params=params,
            name="gram_sum",
        )(swap(grams, ("row", "col")))
    return (residual, rayleigh, gram)


def solution(mesh):
    return jax.shard_map(
        per_device,
        mesh=mesh,
        in_specs=(
            P(None, ("row", "col")),
            P(("row", "col")),
            P("row", "col", None, None, None),
            P("row", "col", None),
            P("row", "col", None),
            P("row", "col"),
        ),
        out_specs=(P(None, ("row", "col")), P(), P()),
        check_vma=False,
    )
```

```python
import functools

import jax
import jax.numpy as jnp
from jax import lax
from jax.experimental import pallas as pl
from jax.experimental.pallas import tpu as pltpu
from jax.sharding import PartitionSpec as P

HP = lax.Precision.HIGHEST
VMEM = pl.BlockSpec(memory_space=pltpu.VMEM)
SMEM = pl.BlockSpec(memory_space=pltpu.SMEM)


def mult(left, right):
    return lax.dot_general(left, right, (((1,), (0,)), ((), ())), precision=HP, preferred_element_type=jnp.float32)


def mult_last(left, right):
    return lax.dot_general(left, right, (((1,), (1,)), ((), ())), precision=HP, preferred_element_type=jnp.float32)


def swap(blocks, axis):
    return lax.all_to_all(blocks, axis, 0, 0, tiled=True)


def trade(value, axis, flip):
    size = lax.axis_size(axis)
    return lax.ppermute(value, axis, [(p, p ^ flip) for p in range(size)])


def own_lanes(nvec, width):
    row = lax.broadcasted_iota(jnp.int32, (nvec, width), 0)
    lane = lax.broadcasted_iota(jnp.int32, (nvec, width), 1)
    return lane // nvec == row % (width // nvec)


def packed_gram(left, right):
    nvec, width = left[0].shape
    per = width // nvec
    right = jnp.concatenate(right, axis=1)
    wide = mult_last(jnp.concatenate(left, axis=1), jnp.concatenate([right] * per, axis=0))
    wide = jnp.where(own_lanes(nvec, width), wide, 0.0)
    return jnp.sum(wide.reshape(nvec // per, per, width), axis=1)


def unpack(packed, nvec):
    rows, width = packed.shape
    per = width // nvec
    wide = jnp.concatenate([jnp.broadcast_to(packed[g : g + 1], (per, width)) for g in range(rows)], axis=0)
    wide = jnp.where(own_lanes(nvec, width), wide, 0.0)
    lane = lax.broadcasted_iota(jnp.int32, (width, nvec), 0)
    column = lax.broadcasted_iota(jnp.int32, (width, nvec), 1)
    return mult(wide, (lane % nvec == column).astype(jnp.float32))


def split(value):
    first = value.astype(jnp.bfloat16)
    rest = value - first.astype(jnp.float32)
    second = rest.astype(jnp.bfloat16)
    return first, second, (rest - second.astype(jnp.float32)).astype(jnp.bfloat16)


def stack_split(value):
    return jnp.concatenate(split(value), axis=0)


def parts_product(stacked, parts, dims):
    nvec = stacked.shape[0] // 3
    total = None
    for used, part in zip((1, 2, 3), parts[::-1]):
        wide = lax.dot_general(stacked[: used * nvec], part, dims, preferred_element_type=jnp.float32)
        for row in reversed(range(used)):
            piece = wide[row * nvec : (row + 1) * nvec]
            total = piece if total is None else total + piece
    return total


def pair_kernel(x_ref, other, out):
    out[0] = x_ref[...]
    out[1] = other[...]


def column_kernel(n_row, n_col, slots, place, arow, bcol, count, d_ref, *refs):
    x_rows, (tiles, out, *parts, rows, sums) = refs[:n_col], refs[n_col:]
    me_row, me_col = place[0], place[1]
    for flip in range(n_col):
        rows[flip] = stack_split(x_rows[flip][...])
    sums[...] = jnp.zeros_like(sums)
    sums[0] = 0.5 * d_ref[...] * x_rows[0][...]
    for slot in range(slots):
        pieces = split(tiles[0, 0, slot])
        for part, piece in zip(parts, pieces):
            part[slot] = piece
        block = jnp.where(slot < count[0, 0], bcol[0, 0, slot] ^ me_row, n_row)
        sums[block] += parts_product(rows[arow[0, 0, slot] ^ me_col], pieces, (((1,), (0,)), ((), ())))
    out[...] = sums[:n_row]


def row_kernel(n_row, n_col, slots, place, arow, bcol, count, d_ref, *refs):
    x_rows, refs = refs[:n_col], refs[n_col:]
    x_pairs, (col_terms, *parts, out, to_core, cols, sums) = refs[: n_row // 2], refs[n_row // 2 :]
    nvec, width = x_rows[0].shape
    me_row, me_col = place[0], place[1]
    for flip in range(n_row):
        cols[flip] = stack_split(x_pairs[flip // 2][flip % 2])
    sums[...] = jnp.zeros_like(sums)
    sums[0] = 0.5 * d_ref[...] * x_rows[0][...]
    for slot in range(slots):
        block = jnp.where(slot < count[0, 0], arow[0, 0, slot] ^ me_col, n_col)
        pieces = [part[slot] for part in parts]
        sums[block] += parts_product(cols[bcol[0, 0, slot] ^ me_row], pieces, (((1,), (1,)), ((), ())))
    out[...] = sums[:n_col]
    for chip in range(n_row // 2):
        to_core[chip * nvec : (chip + 1) * nvec] = col_terms[2 * chip + 1]
    total = packed_gram([x[...] for x in x_rows], [sums[flip] for flip in range(n_col)])
    rest = jnp.zeros((to_core.shape[0] - n_row // 2 * nvec - total.shape[0], width), jnp.float32)
    to_core[n_row // 2 * nvec :] = jnp.concatenate([total, rest], axis=0)


def chip_kernel(col_terms, mine, other, *outs):
    nvec = col_terms.shape[1]
    tail = len(outs) * nvec
    for chip, out in enumerate(outs):
        out[:nvec] = col_terms[2 * chip] + other[chip * nvec : (chip + 1) * nvec]
        out[nvec:] = mine[tail:] + other[tail:]


def join_kernel(n_chip, *refs):
    by_row, (terms, *outs) = refs[:n_chip], refs[n_chip:]
    nvec = terms.shape[1]
    both = by_row[0][...]
    for part in by_row[1:]:
        both += part[...]
    outs[0][:nvec] = both[:nvec] + terms[0]
    for flip in range(1, len(outs)):
        outs[flip][:nvec] = terms[flip]
    for out in outs:
        out[nvec:] = both[nvec:]


def residual_kernel(scale, x_ref, *refs):
    parts, (residual, rayleigh, out) = refs[:-3], refs[-3:]
    own = x_ref[...]
    nvec = own.shape[0]
    both = parts[0][...]
    for part in parts[1:]:
        both += part[...]
    half = unpack(both[nvec : nvec + out.shape[1]], nvec)
    ray = (half + half.T) * scale
    rayleigh[...] = ray
    res = both[:nvec] - mult(ray, own)
    residual[...] = res
    part = packed_gram([res], [res])
    for block in range(out.shape[0]):
        out[block] = part


def gram_kernel(scale, parts, out):
    out[...] = unpack(jnp.sum(parts[...], axis=0), out.shape[0]) * scale


def per_device(vectors, diagonal_energy, tiles, tile_rows, tile_cols, tile_count):
    n_row = lax.axis_size("row")
    n_col = lax.axis_size("col")
    devices = n_row * n_col
    nvec, width = vectors.shape
    slots = tiles.shape[2]
    scale = 1.0 / float(devices * width)
    packed_rows = nvec * nvec // width
    padded = nvec + 8 * (-(-packed_rows // 8))
    n_chip = n_row // 2
    block = jax.ShapeDtypeStruct((nvec, width), jnp.float32)
    joined = jax.ShapeDtypeStruct((padded, width), jnp.float32)
    square = jax.ShapeDtypeStruct((nvec, nvec), jnp.float32)
    place = jnp.stack([lax.axis_index("row"), lax.axis_index("col")]).astype(jnp.int32)
    energy = diagonal_energy.reshape(1, width)
    part = jax.ShapeDtypeStruct((slots, width, width), jnp.bfloat16)
    params = pltpu.CompilerParams(vmem_limit_bytes=16 * 2**20)
    cost = pl.CostEstimate(flops=12 * slots * nvec * width * width, bytes_accessed=2**20, transcendentals=0)
    with jax.named_scope("share_vectors"):
        other = trade(vectors, "row", 1)
        x_rows = [vectors] + [trade(vectors, "col", flip) for flip in range(1, n_col)]
        pair = pl.pallas_call(
            pair_kernel,
            out_shape=jax.ShapeDtypeStruct((2, nvec, width), jnp.float32),
            in_specs=[VMEM] * 2,
            out_specs=VMEM,
            compiler_params=params,
            name="pair",
        )(vectors, other)
        x_pairs = [pair] + [trade(pair, "row", 2 * chip) for chip in range(1, n_chip)]
    with jax.named_scope("column_terms"):
        col_terms, *parts = pl.pallas_call(
            functools.partial(column_kernel, n_row, n_col, slots),
            out_shape=[jax.ShapeDtypeStruct((n_row, nvec, width), jnp.float32), part, part, part],
            in_specs=[SMEM] * 4 + [VMEM] * (n_col + 2),
            out_specs=[VMEM] * 4,
            scratch_shapes=[
                pltpu.VMEM((n_col, 3 * nvec, width), jnp.bfloat16),
                pltpu.VMEM((n_row + 1, nvec, width), jnp.float32),
            ],
            compiler_params=params,
            cost_estimate=cost,
            name="column_terms",
        )(place, tile_rows, tile_cols, tile_count, energy, *x_rows, tiles)
    with jax.named_scope("row_terms"):
        row_terms, to_core = pl.pallas_call(
            functools.partial(row_kernel, n_row, n_col, slots),
            out_shape=[
                jax.ShapeDtypeStruct((n_col, nvec, width), jnp.float32),
                jax.ShapeDtypeStruct((n_chip * nvec + padded - nvec, width), jnp.float32),
            ],
            in_specs=[SMEM] * 4 + [VMEM] * (1 + n_col + n_chip + 4),
            out_specs=[VMEM] * 2,
            scratch_shapes=[
                pltpu.VMEM((n_row, 3 * nvec, width), jnp.bfloat16),
                pltpu.VMEM((n_col + 1, nvec, width), jnp.float32),
            ],
            compiler_params=params,
            cost_estimate=cost,
            name="row_terms",
        )(place, tile_rows, tile_cols, tile_count, energy, *x_rows, *x_pairs, col_terms, *parts)
    with jax.named_scope("return_products"):
        chips = pl.pallas_call(
            chip_kernel,
            out_shape=[joined] * n_chip,
            in_specs=[VMEM] * 3,
            out_specs=[VMEM] * n_chip,
            compiler_params=params,
            name="chip_sum",
        )(col_terms, to_core, trade(to_core, "row", 1))
        by_row = [chips[0]] + [trade(chips[chip], "row", 2 * chip) for chip in range(1, n_chip)]
        sends = pl.pallas_call(
            functools.partial(join_kernel, n_chip),
            out_shape=[joined] * n_col,
            in_specs=[VMEM] * (n_chip + 1),
            out_specs=[VMEM] * n_col,
            compiler_params=params,
            name="row_sum",
        )(*by_row, row_terms)
        sums = [sends[0]] + [trade(sends[flip], "col", flip) for flip in range(1, n_col)]
    with jax.named_scope("residual"):
        residual, rayleigh, grams = pl.pallas_call(
            functools.partial(residual_kernel, scale),
            out_shape=[block, square, jax.ShapeDtypeStruct((devices, packed_rows, width), jnp.float32)],
            in_specs=[VMEM] * (1 + n_col),
            out_specs=[VMEM] * 3,
            compiler_params=params,
            name="residual",
        )(vectors, *sums)
    with jax.named_scope("gram_sum"):
        gram = pl.pallas_call(
            functools.partial(gram_kernel, scale),
            out_shape=square,
            in_specs=[VMEM],
            out_specs=VMEM,
            compiler_params=params,
            name="gram_sum",
        )(swap(grams, ("row", "col")))
    return (residual, rayleigh, gram)


def solution(mesh):
    return jax.shard_map(
        per_device,
        mesh=mesh,
        in_specs=(
            P(None, ("row", "col")),
            P(("row", "col")),
            P("row", "col", None, None, None),
            P("row", "col", None),
            P("row", "col", None),
            P("row", "col"),
        ),
        out_specs=(P(None, ("row", "col")), P(), P()),
        check_vma=False,
    )
```

```python
import functools

import jax
import jax.numpy as jnp
from jax import lax
from jax.experimental import pallas as pl
from jax.experimental.pallas import tpu as pltpu
from jax.sharding import PartitionSpec as P

HP = lax.Precision.HIGHEST
VMEM = pl.BlockSpec(memory_space=pltpu.VMEM)
SMEM = pl.BlockSpec(memory_space=pltpu.SMEM)


def mult(left, right):
    return lax.dot_general(left, right, (((1,), (0,)), ((), ())), precision=HP, preferred_element_type=jnp.float32)


def mult_last(left, right):
    return lax.dot_general(left, right, (((1,), (1,)), ((), ())), precision=HP, preferred_element_type=jnp.float32)


def swap(blocks, axis):
    return lax.all_to_all(blocks, axis, 0, 0, tiled=True)


def trade(value, axis, flip):
    size = lax.axis_size(axis)
    return lax.ppermute(value, axis, [(p, p ^ flip) for p in range(size)])


def own_lanes(nvec, width):
    row = lax.broadcasted_iota(jnp.int32, (nvec, width), 0)
    lane = lax.broadcasted_iota(jnp.int32, (nvec, width), 1)
    return lane // nvec == row % (width // nvec)


def packed_gram(left, right):
    nvec, width = right.shape
    per = width // nvec
    wide = mult_last(left, jnp.concatenate([right] * per, axis=0))
    mask = own_lanes(nvec, width)
    squares = []
    for first in range(0, left.shape[0], nvec):
        own = jnp.where(mask, wide[first : first + nvec], 0.0)
        squares.append(jnp.sum(own.reshape(nvec // per, per, width), axis=1))
    return squares


def unpack(packed, nvec):
    rows, width = packed[0].shape
    per = width // nvec
    lane = lax.broadcasted_iota(jnp.int32, (width, nvec), 0)
    column = lax.broadcasted_iota(jnp.int32, (width, nvec), 1)
    mask = own_lanes(nvec, width)
    wide = []
    for square in packed:
        spread = jnp.concatenate([jnp.broadcast_to(square[g : g + 1], (per, width)) for g in range(rows)], axis=0)
        wide.append(jnp.where(mask, spread, 0.0))
    return mult(jnp.concatenate(wide, axis=0), (lane % nvec == column).astype(jnp.float32))


def split(value):
    first = value.astype(jnp.bfloat16)
    rest = value - first.astype(jnp.float32)
    second = rest.astype(jnp.bfloat16)
    return first, second, (rest - second.astype(jnp.float32)).astype(jnp.bfloat16)


def stack_split(value):
    return jnp.concatenate(split(value), axis=0)


def parts_product(stacked, parts, dims):
    nvec = stacked.shape[0] // 3
    total = None
    for used, part in zip((1, 2, 3), parts[::-1]):
        wide = lax.dot_general(stacked[: used * nvec], part, dims, preferred_element_type=jnp.float32)
        for row in reversed(range(used)):
            piece = wide[row * nvec : (row + 1) * nvec]
            total = piece if total is None else total + piece
    return total


def pair_kernel(x_ref, other, out):
    out[0] = x_ref[...]
    out[1] = other[...]


def column_kernel(n_row, n_col, slots, place, arow, bcol, count, d_ref, *refs):
    x_rows, (tiles, keep, to_core, *parts, rows, sums) = refs[:n_col], refs[n_col:]
    me_row, me_col = place[0], place[1]
    for flip in range(n_col):
        rows[flip] = stack_split(x_rows[flip][...])
    sums[...] = jnp.zeros_like(sums)
    sums[0] = d_ref[...] * x_rows[0][...]
    for slot in range(slots):
        pieces = split(tiles[0, 0, slot])
        for part, piece in zip(parts, pieces):
            part[slot] = piece
        block = jnp.where(slot < count[0, 0], bcol[0, 0, slot] ^ me_row, n_row)
        sums[block] += parts_product(rows[arow[0, 0, slot] ^ me_col], pieces, (((1,), (0,)), ((), ())))
    for chip in range(n_row // 2):
        keep[chip] = sums[2 * chip]
        to_core[chip] = sums[2 * chip + 1]


def row_kernel(n_row, n_col, slots, place, arow, bcol, count, *refs):
    x_pairs, refs = refs[: n_row // 2], refs[n_row // 2 :]
    parts, outs, (cols, sums) = refs[:3], refs[3:-2], refs[-2:]
    me_row, me_col = place[0], place[1]
    for flip in range(n_row):
        cols[flip] = stack_split(x_pairs[flip // 2][flip % 2])
    sums[...] = jnp.zeros_like(sums)
    for slot in range(slots):
        block = jnp.where(slot < count[0, 0], arow[0, 0, slot] ^ me_col, n_col)
        pieces = [part[slot] for part in parts]
        sums[block] += parts_product(cols[bcol[0, 0, slot] ^ me_row], pieces, (((1,), (1,)), ((), ())))
    for flip, out in enumerate(outs):
        out[...] = sums[flip]


def chip_kernel(mine, other, *outs):
    for chip, out in enumerate(outs):
        out[...] = mine[chip] + other[chip]


def product_kernel(x_ref, *refs):
    parts, (product, out) = refs[:-2], refs[-2:]
    own = x_ref[...]
    total = parts[0][...]
    for part in parts[1:]:
        total += part[...]
    product[...] = total
    squares = packed_gram(jnp.concatenate([own, total], axis=0), total) + packed_gram(own, own)
    for block in range(out.shape[0]):
        for which, square in enumerate(squares):
            out[block, which] = square


def result_kernel(scale, x_ref, product, parts, residual, rayleigh, gram, sound):
    own = x_ref[...]
    nvec = own.shape[0]
    sums = jnp.sum(parts[...], axis=0)
    squares = unpack([sums[which] for which in range(3)], nvec) * scale
    ray, outer, inner = squares[:nvec], squares[nvec : 2 * nvec], squares[2 * nvec :]
    rayleigh[...] = ray
    residual[...] = product[...] - mult(ray, own)
    twice = mult(ray, ray)
    lifted = mult_last(mult(ray, inner), ray)
    result = outer - (twice + twice.T) + lifted
    gram[...] = result
    diagonal = lax.broadcasted_iota(jnp.int32, (nvec, nvec), 0) == lax.broadcasted_iota(jnp.int32, (nvec, nvec), 1)
    margin = jnp.sum(jnp.where(diagonal, 64.0 * result - (outer + lifted), 0.0))
    sound[0, 0] = (margin >= 0.0).astype(jnp.int32)


def gram_parts_kernel(residual, out):
    square = packed_gram(residual[...], residual[...])[0]
    for block in range(out.shape[0]):
        out[block] = square


def gram_kernel(scale, parts, out):
    out[...] = unpack([jnp.sum(parts[...], axis=0)], out.shape[0]) * scale


def per_device(vectors, diagonal_energy, tiles, tile_rows, tile_cols, tile_count):
    n_row = lax.axis_size("row")
    n_col = lax.axis_size("col")
    devices = n_row * n_col
    nvec, width = vectors.shape
    slots = tiles.shape[2]
    scale = 1.0 / float(devices * width)
    n_chip = n_row // 2
    packed_rows = nvec * nvec // width
    block = jax.ShapeDtypeStruct((nvec, width), jnp.float32)
    blocks = jax.ShapeDtypeStruct((n_chip, nvec, width), jnp.float32)
    square = jax.ShapeDtypeStruct((nvec, nvec), jnp.float32)
    part = jax.ShapeDtypeStruct((slots, width, width), jnp.bfloat16)
    place = jnp.stack([lax.axis_index("row"), lax.axis_index("col")]).astype(jnp.int32)
    energy = diagonal_energy.reshape(1, width)
    params = pltpu.CompilerParams(vmem_limit_bytes=16 * 2**20)
    cost = pl.CostEstimate(flops=12 * slots * nvec * width * width, bytes_accessed=2**20, transcendentals=0)
    with jax.named_scope("share_vectors"):
        other = trade(vectors, "row", 1)
        x_rows = [vectors] + [trade(vectors, "col", flip) for flip in range(1, n_col)]
        pair = pl.pallas_call(
            pair_kernel,
            out_shape=jax.ShapeDtypeStruct((2, nvec, width), jnp.float32),
            in_specs=[VMEM] * 2,
            out_specs=VMEM,
            compiler_params=params,
            name="pair",
        )(vectors, other)
        x_pairs = [pair] + [trade(pair, "row", 2 * chip) for chip in range(1, n_chip)]
    with jax.named_scope("column_terms"):
        keep, to_core, *parts = pl.pallas_call(
            functools.partial(column_kernel, n_row, n_col, slots),
            out_shape=[blocks, blocks, part, part, part],
            in_specs=[SMEM] * 4 + [VMEM] * (n_col + 2),
            out_specs=[VMEM] * 5,
            scratch_shapes=[
                pltpu.VMEM((n_col, 3 * nvec, width), jnp.bfloat16),
                pltpu.VMEM((n_row + 1, nvec, width), jnp.float32),
            ],
            compiler_params=params,
            cost_estimate=cost,
            name="column_terms",
        )(place, tile_rows, tile_cols, tile_count, energy, *x_rows, tiles)
        from_core = trade(to_core, "row", 1)
    with jax.named_scope("row_terms"):
        row_terms = pl.pallas_call(
            functools.partial(row_kernel, n_row, n_col, slots),
            out_shape=[block] * n_col,
            in_specs=[SMEM] * 4 + [VMEM] * (n_chip + 3),
            out_specs=[VMEM] * n_col,
            scratch_shapes=[
                pltpu.VMEM((n_row, 3 * nvec, width), jnp.bfloat16),
                pltpu.VMEM((n_col + 1, nvec, width), jnp.float32),
            ],
            compiler_params=params,
            cost_estimate=cost,
            name="row_terms",
        )(place, tile_rows, tile_cols, tile_count, *x_pairs, *parts)
    with jax.named_scope("return_products"):
        sums = [row_terms[0]] + [trade(row_terms[flip], "col", flip) for flip in range(1, n_col)]
        chips = pl.pallas_call(
            chip_kernel,
            out_shape=[block] * n_chip,
            in_specs=[VMEM] * 2,
            out_specs=[VMEM] * n_chip,
            compiler_params=params,
            name="chip_sum",
        )(keep, from_core)
        sums += [chips[0]] + [trade(chips[chip], "row", 2 * chip) for chip in range(1, n_chip)]
    with jax.named_scope("product"):
        product, squares = pl.pallas_call(
            product_kernel,
            out_shape=[block, jax.ShapeDtypeStruct((devices, 3, packed_rows, width), jnp.float32)],
            in_specs=[VMEM] * (1 + n_col + n_chip),
            out_specs=[VMEM] * 2,
            compiler_params=params,
            name="product",
        )(vectors, *sums)
    with jax.named_scope("results"):
        residual, rayleigh, gram, sound = pl.pallas_call(
            functools.partial(result_kernel, scale),
            out_shape=[block, square, square, jax.ShapeDtypeStruct((1, 1), jnp.int32)],
            in_specs=[VMEM] * 3,
            out_specs=[VMEM] * 3 + [SMEM],
            compiler_params=params,
            name="results",
        )(vectors, product, swap(squares, ("row", "col")))

    def from_residual(residual, gram):
        parts = pl.pallas_call(
            gram_parts_kernel,
            out_shape=jax.ShapeDtypeStruct((devices, packed_rows, width), jnp.float32),
            in_specs=[VMEM],
            out_specs=VMEM,
            compiler_params=params,
            name="gram_parts",
        )(residual)
        return pl.pallas_call(
            functools.partial(gram_kernel, scale),
            out_shape=square,
            in_specs=[VMEM],
            out_specs=VMEM,
            compiler_params=params,
            name="gram_sum",
        )(swap(parts, ("row", "col")))

    with jax.named_scope("gram"):
        gram = lax.cond(sound[0, 0] > 0, lambda residual, gram: gram, from_residual, residual, gram)
    return (residual, rayleigh, gram)


def solution(mesh):
    return jax.shard_map(
        per_device,
        mesh=mesh,
        in_specs=(
            P(None, ("row", "col")),
            P(("row", "col")),
            P("row", "col", None, None, None),
            P("row", "col", None),
            P("row", "col", None),
            P("row", "col"),
        ),
        out_specs=(P(None, ("row", "col")), P(), P()),
        check_vma=False,
    )
```

```python
import functools

import jax
import jax.numpy as jnp
from jax import lax
from jax.experimental import pallas as pl
from jax.experimental.pallas import tpu as pltpu
from jax.sharding import PartitionSpec as P

HP = lax.Precision.HIGHEST
VMEM = pl.BlockSpec(memory_space=pltpu.VMEM)
SMEM = pl.BlockSpec(memory_space=pltpu.SMEM)


def mult(left, right):
    return lax.dot_general(left, right, (((1,), (0,)), ((), ())), precision=HP, preferred_element_type=jnp.float32)


def mult_last(left, right):
    return lax.dot_general(left, right, (((1,), (1,)), ((), ())), precision=HP, preferred_element_type=jnp.float32)


def swap(blocks, axis):
    return lax.all_to_all(blocks, axis, 0, 0, tiled=True)


def trade(value, axis, flip):
    size = lax.axis_size(axis)
    return lax.ppermute(value, axis, [(p, p ^ flip) for p in range(size)])


def own_lanes(nvec, width):
    row = lax.broadcasted_iota(jnp.int32, (nvec, width), 0)
    lane = lax.broadcasted_iota(jnp.int32, (nvec, width), 1)
    return lane // nvec == row % (width // nvec)


def packed_gram(left, right):
    nvec, width = right.shape
    per = width // nvec
    wide = mult_last(left, jnp.concatenate([right] * per, axis=0))
    mask = own_lanes(nvec, width)
    squares = []
    for first in range(0, left.shape[0], nvec):
        own = jnp.where(mask, wide[first : first + nvec], 0.0)
        squares.append(jnp.sum(own.reshape(nvec // per, per, width), axis=1))
    return squares


def unpack(packed, nvec):
    rows, width = packed[0].shape
    per = width // nvec
    lane = lax.broadcasted_iota(jnp.int32, (width, nvec), 0)
    column = lax.broadcasted_iota(jnp.int32, (width, nvec), 1)
    mask = own_lanes(nvec, width)
    wide = []
    for square in packed:
        spread = jnp.concatenate([jnp.broadcast_to(square[g : g + 1], (per, width)) for g in range(rows)], axis=0)
        wide.append(jnp.where(mask, spread, 0.0))
    return mult(jnp.concatenate(wide, axis=0), (lane % nvec == column).astype(jnp.float32))


def split(value):
    first = value.astype(jnp.bfloat16)
    rest = value - first.astype(jnp.float32)
    second = rest.astype(jnp.bfloat16)
    return first, second, (rest - second.astype(jnp.float32)).astype(jnp.bfloat16)


def stack_split(value):
    return jnp.concatenate(split(value), axis=0)


def parts_product(stacked, parts, dims):
    nvec = stacked.shape[0] // 3
    total = None
    for used, part in zip((1, 2, 3), parts[::-1]):
        wide = lax.dot_general(stacked[: used * nvec], part, dims, preferred_element_type=jnp.float32)
        for row in reversed(range(used)):
            piece = wide[row * nvec : (row + 1) * nvec]
            total = piece if total is None else total + piece
    return total


def pair_kernel(x_ref, other, out):
    out[0] = x_ref[...]
    out[1] = other[...]


def column_kernel(n_row, n_col, slots, place, arow, bcol, count, d_ref, *refs):
    x_rows, (tiles, even, odd, *parts, rows, sums) = refs[:n_col], refs[n_col:]
    me_row, me_col = place[0], place[1]
    for flip in range(n_col):
        rows[flip] = stack_split(x_rows[flip][...])
    sums[...] = jnp.zeros_like(sums)
    sums[0] = d_ref[...] * x_rows[0][...]
    for slot in range(slots):
        pieces = split(tiles[0, 0, slot])
        for part, piece in zip(parts, pieces):
            part[slot] = piece
        block = jnp.where(slot < count[0, 0], bcol[0, 0, slot] ^ me_row, n_row)
        sums[block] += parts_product(rows[arow[0, 0, slot] ^ me_col], pieces, (((1,), (0,)), ((), ())))
    for chip in range(n_row // 2):
        even[chip] = sums[2 * chip]
        odd[chip] = sums[2 * chip + 1]


def row_kernel(n_row, n_col, slots, place, arow, bcol, count, *refs):
    x_pairs, refs = refs[: n_row // 2], refs[n_row // 2 :]
    (odd, *parts), (to_core, *outs), (cols, sums) = refs[:4], refs[4:-2], refs[-2:]
    to_core[...] = odd[...]
    me_row, me_col = place[0], place[1]
    for flip in range(n_row):
        cols[flip] = stack_split(x_pairs[flip // 2][flip % 2])
    sums[...] = jnp.zeros_like(sums)
    for slot in range(slots):
        block = jnp.where(slot < count[0, 0], arow[0, 0, slot] ^ me_col, n_col)
        pieces = [part[slot] for part in parts]
        sums[block] += parts_product(cols[bcol[0, 0, slot] ^ me_row], pieces, (((1,), (1,)), ((), ())))
    for flip, out in enumerate(outs):
        out[...] = sums[flip]


def chip_kernel(mine, other, *outs):
    for chip, out in enumerate(outs):
        out[...] = mine[chip] + other[chip]


def product_kernel(x_ref, *refs):
    parts, (product, out) = refs[:-2], refs[-2:]
    own = x_ref[...]
    total = parts[0][...]
    for part in parts[1:]:
        total += part[...]
    product[...] = total
    squares = packed_gram(jnp.concatenate([own, total], axis=0), total) + packed_gram(own, own)
    for block in range(out.shape[0]):
        for which, square in enumerate(squares):
            out[block, which] = square


def result_kernel(scale, x_ref, product, parts, residual, rayleigh, gram, sound):
    own = x_ref[...]
    nvec = own.shape[0]
    sums = jnp.sum(parts[...], axis=0)
    squares = unpack([sums[which] for which in range(3)], nvec) * scale
    ray, outer, inner = squares[:nvec], squares[nvec : 2 * nvec], squares[2 * nvec :]
    rayleigh[...] = ray
    residual[...] = product[...] - mult(ray, own)
    twice = mult(ray, ray)
    lifted = mult_last(mult(ray, inner), ray)
    result = outer - (twice + twice.T) + lifted
    gram[...] = result
    diagonal = lax.broadcasted_iota(jnp.int32, (nvec, nvec), 0) == lax.broadcasted_iota(jnp.int32, (nvec, nvec), 1)
    margin = jnp.sum(jnp.where(diagonal, 64.0 * result - (outer + lifted), 0.0))
    sound[0, 0] = (margin >= 0.0).astype(jnp.int32)


def gram_parts_kernel(residual, out):
    square = packed_gram(residual[...], residual[...])[0]
    for block in range(out.shape[0]):
        out[block] = square


def gram_kernel(scale, parts, out):
    out[...] = unpack([jnp.sum(parts[...], axis=0)], out.shape[0]) * scale


def per_device(vectors, diagonal_energy, tiles, tile_rows, tile_cols, tile_count):
    n_row = lax.axis_size("row")
    n_col = lax.axis_size("col")
    devices = n_row * n_col
    nvec, width = vectors.shape
    slots = tiles.shape[2]
    scale = 1.0 / float(devices * width)
    n_chip = n_row // 2
    packed_rows = nvec * nvec // width
    block = jax.ShapeDtypeStruct((nvec, width), jnp.float32)
    blocks = jax.ShapeDtypeStruct((n_chip, nvec, width), jnp.float32)
    square = jax.ShapeDtypeStruct((nvec, nvec), jnp.float32)
    part = jax.ShapeDtypeStruct((slots, width, width), jnp.bfloat16)
    place = jnp.stack([lax.axis_index("row"), lax.axis_index("col")]).astype(jnp.int32)
    energy = diagonal_energy.reshape(1, width)
    params = pltpu.CompilerParams(vmem_limit_bytes=16 * 2**20)
    cost = pl.CostEstimate(flops=12 * slots * nvec * width * width, bytes_accessed=2**20, transcendentals=0)
    with jax.named_scope("share_vectors"):
        other = trade(vectors, "row", 1)
        x_rows = [vectors] + [trade(vectors, "col", flip) for flip in range(1, n_col)]
        pair = pl.pallas_call(
            pair_kernel,
            out_shape=jax.ShapeDtypeStruct((2, nvec, width), jnp.float32),
            in_specs=[VMEM] * 2,
            out_specs=VMEM,
            compiler_params=params,
            name="pair",
        )(vectors, other)
        x_pairs = [pair] + [trade(pair, "row", 2 * chip) for chip in range(1, n_chip)]
    with jax.named_scope("column_terms"):
        even, odd, *parts = pl.pallas_call(
            functools.partial(column_kernel, n_row, n_col, slots),
            out_shape=[blocks, blocks, part, part, part],
            in_specs=[SMEM] * 4 + [VMEM] * (n_col + 2),
            out_specs=[VMEM] * 5,
            scratch_shapes=[
                pltpu.VMEM((n_col, 3 * nvec, width), jnp.bfloat16),
                pltpu.VMEM((n_row + 1, nvec, width), jnp.float32),
            ],
            compiler_params=params,
            cost_estimate=cost,
            name="column_terms",
        )(place, tile_rows, tile_cols, tile_count, energy, *x_rows, tiles)
    with jax.named_scope("row_terms"):
        to_core, *row_terms = pl.pallas_call(
            functools.partial(row_kernel, n_row, n_col, slots),
            out_shape=[blocks] + [block] * n_col,
            in_specs=[SMEM] * 4 + [VMEM] * (n_chip + 4),
            out_specs=[VMEM] * (1 + n_col),
            scratch_shapes=[
                pltpu.VMEM((n_row, 3 * nvec, width), jnp.bfloat16),
                pltpu.VMEM((n_col + 1, nvec, width), jnp.float32),
            ],
            compiler_params=params,
            cost_estimate=cost,
            name="row_terms",
        )(place, tile_rows, tile_cols, tile_count, *x_pairs, odd, *parts)
    with jax.named_scope("return_products"):
        from_core = trade(to_core, "row", 1)
        sums = [row_terms[0]] + [trade(row_terms[flip], "col", flip) for flip in range(1, n_col)]
        chips = pl.pallas_call(
            chip_kernel,
            out_shape=[block] * n_chip,
            in_specs=[VMEM] * 2,
            out_specs=[VMEM] * n_chip,
            compiler_params=params,
            name="chip_sum",
        )(even, from_core)
        sums += [chips[0]] + [trade(chips[chip], "row", 2 * chip) for chip in range(1, n_chip)]
    with jax.named_scope("product"):
        product, squares = pl.pallas_call(
            product_kernel,
            out_shape=[block, jax.ShapeDtypeStruct((devices, 3, packed_rows, width), jnp.float32)],
            in_specs=[VMEM] * (1 + n_col + n_chip),
            out_specs=[VMEM] * 2,
            compiler_params=params,
            name="product",
        )(vectors, *sums)
    with jax.named_scope("results"):
        residual, rayleigh, gram, sound = pl.pallas_call(
            functools.partial(result_kernel, scale),
            out_shape=[block, square, square, jax.ShapeDtypeStruct((1, 1), jnp.int32)],
            in_specs=[VMEM] * 3,
            out_specs=[VMEM] * 3 + [SMEM],
            compiler_params=params,
            name="results",
        )(vectors, product, swap(squares, ("row", "col")))

    def from_residual(_):
        parts = pl.pallas_call(
            gram_parts_kernel,
            out_shape=jax.ShapeDtypeStruct((devices, packed_rows, width), jnp.float32),
            in_specs=[VMEM],
            out_specs=VMEM,
            compiler_params=params,
            name="gram_parts",
        )(residual)
        gram = pl.pallas_call(
            functools.partial(gram_kernel, scale),
            out_shape=square,
            in_specs=[VMEM],
            out_specs=VMEM,
            compiler_params=params,
            name="gram_sum",
        )(swap(parts, ("row", "col")))
        return jnp.int32(1), gram

    with jax.named_scope("gram"):
        _, gram = lax.while_loop(lambda state: state[0] == 0, from_residual, (sound[0, 0], gram))
    return (residual, rayleigh, gram)


def solution(mesh):
    return jax.shard_map(
        per_device,
        mesh=mesh,
        in_specs=(
            P(None, ("row", "col")),
            P(("row", "col")),
            P("row", "col", None, None, None),
            P("row", "col", None),
            P("row", "col", None),
            P("row", "col"),
        ),
        out_specs=(P(None, ("row", "col")), P(), P()),
        check_vma=False,
    )
```

```python
import functools

import jax
import jax.numpy as jnp
from jax import lax
from jax.experimental import pallas as pl
from jax.experimental.pallas import tpu as pltpu
from jax.sharding import PartitionSpec as P

HP = lax.Precision.HIGHEST
VMEM = pl.BlockSpec(memory_space=pltpu.VMEM)
SMEM = pl.BlockSpec(memory_space=pltpu.SMEM)


def mult(left, right):
    return lax.dot_general(left, right, (((1,), (0,)), ((), ())), precision=HP, preferred_element_type=jnp.float32)


def mult_last(left, right):
    return lax.dot_general(left, right, (((1,), (1,)), ((), ())), precision=HP, preferred_element_type=jnp.float32)


def swap(blocks, axis):
    return lax.all_to_all(blocks, axis, 0, 0, tiled=True)


def trade(value, axis, flip):
    size = lax.axis_size(axis)
    return lax.ppermute(value, axis, [(p, p ^ flip) for p in range(size)])


def own_lanes(nvec, width):
    row = lax.broadcasted_iota(jnp.int32, (nvec, width), 0)
    lane = lax.broadcasted_iota(jnp.int32, (nvec, width), 1)
    return lane // nvec == row % (width // nvec)


def packed_gram(left, right):
    nvec, width = right.shape
    per = width // nvec
    wide = mult_last(left, jnp.concatenate([right] * per, axis=0))
    mask = own_lanes(nvec, width)
    squares = []
    for first in range(0, left.shape[0], nvec):
        own = jnp.where(mask, wide[first : first + nvec], 0.0)
        squares.append(jnp.sum(own.reshape(nvec // per, per, width), axis=1))
    return squares


def unpack(packed, nvec):
    rows, width = packed[0].shape
    per = width // nvec
    lane = lax.broadcasted_iota(jnp.int32, (width, nvec), 0)
    column = lax.broadcasted_iota(jnp.int32, (width, nvec), 1)
    mask = own_lanes(nvec, width)
    wide = []
    for square in packed:
        spread = jnp.concatenate([jnp.broadcast_to(square[g : g + 1], (per, width)) for g in range(rows)], axis=0)
        wide.append(jnp.where(mask, spread, 0.0))
    return mult(jnp.concatenate(wide, axis=0), (lane % nvec == column).astype(jnp.float32))


def split(value):
    first = value.astype(jnp.bfloat16)
    rest = value - first.astype(jnp.float32)
    second = rest.astype(jnp.bfloat16)
    return first, second, (rest - second.astype(jnp.float32)).astype(jnp.bfloat16)


def stack_split(value):
    return jnp.concatenate(split(value), axis=0)


def parts_product(stacked, parts, dims):
    nvec = stacked.shape[0] // 3
    total = None
    for used, part in zip((1, 2, 3), parts[::-1]):
        wide = lax.dot_general(stacked[: used * nvec], part, dims, preferred_element_type=jnp.float32)
        for row in reversed(range(used)):
            piece = wide[row * nvec : (row + 1) * nvec]
            total = piece if total is None else total + piece
    return total


def join_kernel(mine, other, out):
    half = mine.shape[0]
    out[:half] = mine[...]
    out[half:] = other[...]


def part_blocks(sums, total, send, keep):
    for block in range(total // 2):
        keep[block] = sums[2 * block]
        send[block] = sums[2 * block + 1]


def column_kernel(n_row, n_col, slots, place, arow, bcol, count, d_ref, near, far, tiles, send, keep, *refs):
    *parts, rows, sums = refs
    me_row, me_col = place[0], place[1]
    half = n_col // 2
    for flip in range(n_col):
        rows[flip] = stack_split(near[flip] if flip < half else far[flip - half])
    sums[...] = jnp.zeros_like(sums)
    sums[0] = d_ref[...] * near[0]
    for slot in range(slots):
        pieces = split(tiles[0, 0, slot])
        for part, piece in zip(parts, pieces):
            part[slot] = piece
        block = jnp.where(slot < count[0, 0], bcol[0, 0, slot] ^ me_row, n_row)
        sums[block] += parts_product(rows[arow[0, 0, slot] ^ me_col], pieces, (((1,), (0,)), ((), ())))
    part_blocks(sums, n_row, send, keep)


def row_kernel(n_row, n_col, slots, place, arow, bcol, count, near, far, early, *refs):
    *parts, late, send, keep, cols, sums = refs
    me_row, me_col = place[0], place[1]
    late[...] = early[...]
    half = n_row // 2
    for flip in range(n_row):
        cols[flip] = stack_split(near[flip] if flip < half else far[flip - half])
    sums[...] = jnp.zeros_like(sums)
    for slot in range(slots):
        block = jnp.where(slot < count[0, 0], arow[0, 0, slot] ^ me_col, n_col)
        pieces = [part[slot] for part in parts]
        sums[block] += parts_product(cols[bcol[0, 0, slot] ^ me_row], pieces, (((1,), (1,)), ((), ())))
    part_blocks(sums, n_col, send, keep)


def halve_kernel(mine, other, send, keep):
    part_blocks([mine[block] + other[block] for block in range(mine.shape[0])], mine.shape[0], send, keep)


def product_kernel(x_ref, *refs):
    parts, (product, out) = refs[:-2], refs[-2:]
    own = x_ref[...]
    total = parts[0][0]
    for part in parts[1:]:
        total += part[0]
    product[...] = total
    squares = packed_gram(jnp.concatenate([own, total], axis=0), total) + packed_gram(own, own)
    for block in range(out.shape[0]):
        for which, square in enumerate(squares):
            out[block, which] = square


def summed_squares(scale, parts, nvec):
    sums = jnp.sum(parts[...], axis=0)
    squares = unpack([sums[which] for which in range(3)], nvec) * scale
    return squares[:nvec], squares[nvec : 2 * nvec], squares[2 * nvec :]


def result_kernel(scale, x_ref, product, parts, residual, rayleigh, gram, sound):
    own = x_ref[...]
    nvec = own.shape[0]
    ray, outer, inner = summed_squares(scale, parts, nvec)
    rayleigh[...] = ray
    residual[...] = product[...] - mult(ray, own)
    twice = mult(ray, ray)
    lifted = mult_last(mult(ray, inner), ray)
    result = outer - (twice + twice.T) + lifted
    gram[...] = result
    diagonal = lax.broadcasted_iota(jnp.int32, (nvec, nvec), 0) == lax.broadcasted_iota(jnp.int32, (nvec, nvec), 1)
    margin = jnp.sum(jnp.where(diagonal, 64.0 * result - (outer + lifted), 0.0))
    sound[0, 0] = (margin >= 0.0).astype(jnp.int32)


def gram_parts_kernel(scale, x_ref, product, parts, out):
    own = x_ref[...]
    ray, _, _ = summed_squares(scale, parts, own.shape[0])
    residual = product[...] - mult(ray, own)
    square = packed_gram(residual, residual)[0]
    for block in range(out.shape[0]):
        out[block] = square


def gram_kernel(scale, parts, out):
    out[...] = unpack([jnp.sum(parts[...], axis=0)], out.shape[0]) * scale


def per_device(vectors, diagonal_energy, tiles, tile_rows, tile_cols, tile_count):
    n_row = lax.axis_size("row")
    n_col = lax.axis_size("col")
    devices = n_row * n_col
    nvec, width = vectors.shape
    slots = tiles.shape[2]
    scale = 1.0 / float(devices * width)
    packed_rows = nvec * nvec // width
    block = jax.ShapeDtypeStruct((nvec, width), jnp.float32)
    square = jax.ShapeDtypeStruct((nvec, nvec), jnp.float32)
    part = jax.ShapeDtypeStruct((slots, width, width), jnp.bfloat16)
    place = jnp.stack([lax.axis_index("row"), lax.axis_index("col")]).astype(jnp.int32)
    energy = diagonal_energy.reshape(1, width)
    params = pltpu.CompilerParams(vmem_limit_bytes=16 * 2**20)
    cost = pl.CostEstimate(flops=12 * slots * nvec * width * width, bytes_accessed=2**20, transcendentals=0)

    def blocks(total):
        return jax.ShapeDtypeStruct((total, nvec, width), jnp.float32)

    def gather(axis):
        size = lax.axis_size(axis)
        near = vectors[None]
        far = trade(near, axis, 1)
        reach = 2
        while reach < size:
            near = pl.pallas_call(
                join_kernel,
                out_shape=blocks(reach),
                in_specs=[VMEM] * 2,
                out_specs=VMEM,
                compiler_params=params,
                name="join_" + axis,
            )(near, far)
            far = trade(near, axis, reach)
            reach *= 2
        return near, far

    def halve(send, keep, axis):
        flip = 1
        while keep.shape[0] > 1:
            half = keep.shape[0] // 2
            send, keep = pl.pallas_call(
                halve_kernel,
                out_shape=[blocks(half)] * 2,
                in_specs=[VMEM] * 2,
                out_specs=[VMEM] * 2,
                compiler_params=params,
                name="halve_" + axis,
            )(keep, trade(send, axis, flip))
            flip *= 2
        return keep, trade(send, axis, flip)

    with jax.named_scope("share_vectors"):
        x_row = gather("row")
        x_col = gather("col")
    with jax.named_scope("column_terms"):
        col_send, col_keep, *parts = pl.pallas_call(
            functools.partial(column_kernel, n_row, n_col, slots),
            out_shape=[blocks(n_row // 2)] * 2 + [part] * 3,
            in_specs=[SMEM] * 4 + [VMEM] * 4,
            out_specs=[VMEM] * 5,
            scratch_shapes=[
                pltpu.VMEM((n_col, 3 * nvec, width), jnp.bfloat16),
                pltpu.VMEM((n_row + 1, nvec, width), jnp.float32),
            ],
            compiler_params=params,
            cost_estimate=cost,
            name="column_terms",
        )(place, tile_rows, tile_cols, tile_count, energy, *x_col, tiles)
    with jax.named_scope("row_terms"):
        col_send, row_send, row_keep = pl.pallas_call(
            functools.partial(row_kernel, n_row, n_col, slots),
            out_shape=[blocks(n_row // 2)] + [blocks(n_col // 2)] * 2,
            in_specs=[SMEM] * 4 + [VMEM] * 6,
            out_specs=[VMEM] * 3,
            scratch_shapes=[
                pltpu.VMEM((n_row, 3 * nvec, width), jnp.bfloat16),
                pltpu.VMEM((n_col + 1, nvec, width), jnp.float32),
            ],
            compiler_params=params,
            cost_estimate=cost,
            name="row_terms",
        )(place, tile_rows, tile_cols, tile_count, *x_row, col_send, *parts)
    with jax.named_scope("return_products"):
        sums = halve(col_send, col_keep, "row") + halve(row_send, row_keep, "col")
    with jax.named_scope("product"):
        product, squares = pl.pallas_call(
            product_kernel,
            out_shape=[block, jax.ShapeDtypeStruct((devices, 3, packed_rows, width), jnp.float32)],
            in_specs=[VMEM] * 5,
            out_specs=[VMEM] * 2,
            compiler_params=params,
            name="product",
        )(vectors, *sums)
        squares = swap(squares, ("row", "col"))
    with jax.named_scope("results"):
        residual, rayleigh, gram, sound = pl.pallas_call(
            functools.partial(result_kernel, scale),
            out_shape=[block, square, square, jax.ShapeDtypeStruct((1, 1), jnp.int32)],
            in_specs=[VMEM] * 3,
            out_specs=[VMEM] * 3 + [SMEM],
            compiler_params=params,
            name="results",
        )(vectors, product, squares)

    def from_residual(_):
        parts = pl.pallas_call(
            functools.partial(gram_parts_kernel, scale),
            out_shape=jax.ShapeDtypeStruct((devices, packed_rows, width), jnp.float32),
            in_specs=[VMEM] * 3,
            out_specs=VMEM,
            compiler_params=params,
            name="gram_parts",
        )(vectors, product, squares)
        gram = pl.pallas_call(
            functools.partial(gram_kernel, scale),
            out_shape=square,
            in_specs=[VMEM],
            out_specs=VMEM,
            compiler_params=params,
            name="gram_sum",
        )(swap(parts, ("row", "col")))
        return jnp.int32(1), gram

    with jax.named_scope("gram"):
        _, gram = lax.while_loop(lambda state: state[0] == 0, from_residual, (sound[0, 0], gram))
    return (residual, rayleigh, gram)


def solution(mesh):
    return jax.shard_map(
        per_device,
        mesh=mesh,
        in_specs=(
            P(None, ("row", "col")),
            P(("row", "col")),
            P("row", "col", None, None, None),
            P("row", "col", None),
            P("row", "col", None),
            P("row", "col"),
        ),
        out_specs=(P(None, ("row", "col")), P(), P()),
        check_vma=False,
    )
```

```python
import functools

import jax
import jax.numpy as jnp
from jax import lax
from jax.experimental import pallas as pl
from jax.experimental.pallas import tpu as pltpu
from jax.sharding import PartitionSpec as P

HP = lax.Precision.HIGHEST
VMEM = pl.BlockSpec(memory_space=pltpu.VMEM)
SMEM = pl.BlockSpec(memory_space=pltpu.SMEM)


def mult(left, right):
    return lax.dot_general(left, right, (((1,), (0,)), ((), ())), precision=HP, preferred_element_type=jnp.float32)


def mult_last(left, right):
    return lax.dot_general(left, right, (((1,), (1,)), ((), ())), precision=HP, preferred_element_type=jnp.float32)


def swap(blocks, axis):
    return lax.all_to_all(blocks, axis, 0, 0, tiled=True)


def trade(value, axis, flip):
    size = lax.axis_size(axis)
    return lax.ppermute(value, axis, [(p, p ^ flip) for p in range(size)])


def own_lanes(nvec, width):
    row = lax.broadcasted_iota(jnp.int32, (nvec, width), 0)
    lane = lax.broadcasted_iota(jnp.int32, (nvec, width), 1)
    return lane // nvec == row % (width // nvec)


def packed_gram(left, right):
    nvec, width = right.shape
    per = width // nvec
    wide = mult_last(left, jnp.concatenate([right] * per, axis=0))
    mask = own_lanes(nvec, width)
    squares = []
    for first in range(0, left.shape[0], nvec):
        own = jnp.where(mask, wide[first : first + nvec], 0.0)
        squares.append(jnp.sum(own.reshape(nvec // per, per, width), axis=1))
    return squares


def unpack(packed, nvec):
    rows, width = packed[0].shape
    per = width // nvec
    lane = lax.broadcasted_iota(jnp.int32, (width, nvec), 0)
    column = lax.broadcasted_iota(jnp.int32, (width, nvec), 1)
    mask = own_lanes(nvec, width)
    wide = []
    for square in packed:
        spread = jnp.concatenate([jnp.broadcast_to(square[g : g + 1], (per, width)) for g in range(rows)], axis=0)
        wide.append(jnp.where(mask, spread, 0.0))
    return mult(jnp.concatenate(wide, axis=0), (lane % nvec == column).astype(jnp.float32))


def split(value):
    first = value.astype(jnp.bfloat16)
    rest = value - first.astype(jnp.float32)
    second = rest.astype(jnp.bfloat16)
    return first, second, (rest - second.astype(jnp.float32)).astype(jnp.bfloat16)


def stack_split(value):
    return jnp.concatenate(split(value), axis=0)


def parts_product(stacked, parts, dims):
    nvec = stacked.shape[0] // 3
    total = None
    for used, part in zip((1, 2, 3), parts[::-1]):
        wide = lax.dot_general(stacked[: used * nvec], part, dims, preferred_element_type=jnp.float32)
        for row in reversed(range(used)):
            piece = wide[row * nvec : (row + 1) * nvec]
            total = piece if total is None else total + piece
    return total


def join_kernel(axes, *refs):
    for which, out in enumerate(refs[-axes:]):
        mine, other = refs[2 * which : 2 * which + 2]
        half = mine.shape[0]
        out[:half] = mine[...]
        out[half:] = other[...]


def split_kernel(slots, tiles, *parts):
    for slot in range(slots):
        for part, piece in zip(parts, split(tiles[0, 0, slot])):
            part[slot] = piece


def part_blocks(sums, total, send, keep):
    for block in range(total // 2):
        keep[block] = sums[2 * block]
        send[block] = sums[2 * block + 1]


def column_kernel(n_row, n_col, slots, place, arow, bcol, count, d_ref, near, far, *refs):
    *parts, send, keep, rows, sums = refs
    me_row, me_col = place[0], place[1]
    half = n_col // 2
    for flip in range(n_col):
        rows[flip] = stack_split(near[flip] if flip < half else far[flip - half])
    sums[...] = jnp.zeros_like(sums)
    sums[0] = d_ref[...] * near[0]
    for slot in range(slots):
        pieces = [part[slot] for part in parts]
        block = jnp.where(slot < count[0, 0], bcol[0, 0, slot] ^ me_row, n_row)
        sums[block] += parts_product(rows[arow[0, 0, slot] ^ me_col], pieces, (((1,), (0,)), ((), ())))
    part_blocks(sums, n_row, send, keep)


def row_kernel(n_row, n_col, slots, place, arow, bcol, count, near, far, early, *refs):
    *parts, late, send, keep, cols, sums = refs
    me_row, me_col = place[0], place[1]
    late[...] = early[...]
    half = n_row // 2
    for flip in range(n_row):
        cols[flip] = stack_split(near[flip] if flip < half else far[flip - half])
    sums[...] = jnp.zeros_like(sums)
    for slot in range(slots):
        block = jnp.where(slot < count[0, 0], arow[0, 0, slot] ^ me_col, n_col)
        pieces = [part[slot] for part in parts]
        sums[block] += parts_product(cols[bcol[0, 0, slot] ^ me_row], pieces, (((1,), (1,)), ((), ())))
    part_blocks(sums, n_col, send, keep)


def halve_kernel(mine, other, send, keep):
    part_blocks([mine[block] + other[block] for block in range(mine.shape[0])], mine.shape[0], send, keep)


def product_kernel(x_ref, *refs):
    parts, (product, out) = refs[:-2], refs[-2:]
    own = x_ref[...]
    total = parts[0][0]
    for part in parts[1:]:
        total += part[0]
    product[...] = total
    squares = packed_gram(jnp.concatenate([own, total], axis=0), total) + packed_gram(own, own)
    for block in range(out.shape[0]):
        for which, square in enumerate(squares):
            out[block, which] = square


def summed_squares(scale, parts, nvec):
    sums = jnp.sum(parts[...], axis=0)
    squares = unpack([sums[which] for which in range(3)], nvec) * scale
    return squares[:nvec], squares[nvec : 2 * nvec], squares[2 * nvec :]


def result_kernel(scale, x_ref, product, parts, residual, rayleigh, gram, sound):
    own = x_ref[...]
    nvec = own.shape[0]
    ray, outer, inner = summed_squares(scale, parts, nvec)
    rayleigh[...] = ray
    residual[...] = product[...] - mult(ray, own)
    twice = mult(ray, ray)
    lifted = mult_last(mult(ray, inner), ray)
    result = outer - (twice + twice.T) + lifted
    gram[...] = result
    diagonal = lax.broadcasted_iota(jnp.int32, (nvec, nvec), 0) == lax.broadcasted_iota(jnp.int32, (nvec, nvec), 1)
    margin = jnp.sum(jnp.where(diagonal, 64.0 * result - (outer + lifted), 0.0))
    sound[0, 0] = (margin >= 0.0).astype(jnp.int32)


def gram_parts_kernel(scale, x_ref, product, parts, out):
    own = x_ref[...]
    ray, _, _ = summed_squares(scale, parts, own.shape[0])
    residual = product[...] - mult(ray, own)
    square = packed_gram(residual, residual)[0]
    for block in range(out.shape[0]):
        out[block] = square


def gram_kernel(scale, parts, out):
    out[...] = unpack([jnp.sum(parts[...], axis=0)], out.shape[0]) * scale


def per_device(vectors, diagonal_energy, tiles, tile_rows, tile_cols, tile_count):
    n_row = lax.axis_size("row")
    n_col = lax.axis_size("col")
    devices = n_row * n_col
    nvec, width = vectors.shape
    slots = tiles.shape[2]
    scale = 1.0 / float(devices * width)
    packed_rows = nvec * nvec // width
    block = jax.ShapeDtypeStruct((nvec, width), jnp.float32)
    square = jax.ShapeDtypeStruct((nvec, nvec), jnp.float32)
    part = jax.ShapeDtypeStruct((slots, width, width), jnp.bfloat16)
    place = jnp.stack([lax.axis_index("row"), lax.axis_index("col")]).astype(jnp.int32)
    energy = diagonal_energy.reshape(1, width)
    params = pltpu.CompilerParams(vmem_limit_bytes=16 * 2**20)
    cost = pl.CostEstimate(flops=12 * slots * nvec * width * width, bytes_accessed=2**20, transcendentals=0)

    def blocks(total):
        return jax.ShapeDtypeStruct((total, nvec, width), jnp.float32)

    def gather(axes, after):
        near = [vectors[None]] * len(axes)
        far = [trade(vectors[None], axis, 1) for axis in axes]
        reach = 2
        while any(reach < lax.axis_size(axis) for axis in axes):
            going = [which for which, axis in enumerate(axes) if reach < lax.axis_size(axis)]
            joined = pl.pallas_call(
                functools.partial(join_kernel, len(going)),
                out_shape=[blocks(reach)] * len(going),
                in_specs=[VMEM] * (2 * len(going)) + [pl.BlockSpec(memory_space=pl.ANY)] * len(after),
                out_specs=[VMEM] * len(going),
                compiler_params=params,
                name="join",
            )(*[half for which in going for half in (near[which], far[which])], *after)
            for which, half in zip(going, joined):
                near[which], far[which] = half, trade(half, axes[which], reach)
            reach *= 2
            after = ()
        return list(zip(near, far))

    def halve(send, keep, axis):
        flip = 1
        while keep.shape[0] > 1:
            half = keep.shape[0] // 2
            send, keep = pl.pallas_call(
                halve_kernel,
                out_shape=[blocks(half)] * 2,
                in_specs=[VMEM] * 2,
                out_specs=[VMEM] * 2,
                compiler_params=params,
                name="halve_" + axis,
            )(keep, trade(send, axis, flip))
            flip *= 2
        return keep, trade(send, axis, flip)

    with jax.named_scope("split_tiles"):
        parts = pl.pallas_call(
            functools.partial(split_kernel, slots),
            out_shape=[part] * 3,
            in_specs=[VMEM],
            out_specs=[VMEM] * 3,
            compiler_params=params,
            cost_estimate=pl.CostEstimate(flops=0, bytes_accessed=5 * slots * width * width, transcendentals=0),
            name="split_tiles",
        )(tiles)
    with jax.named_scope("share_vectors"):
        x_row, x_col = gather(("row", "col"), parts[:1])
    with jax.named_scope("column_terms"):
        col_send, col_keep = pl.pallas_call(
            functools.partial(column_kernel, n_row, n_col, slots),
            out_shape=[blocks(n_row // 2)] * 2,
            in_specs=[SMEM] * 4 + [VMEM] * 6,
            out_specs=[VMEM] * 2,
            scratch_shapes=[
                pltpu.VMEM((n_col, 3 * nvec, width), jnp.bfloat16),
                pltpu.VMEM((n_row + 1, nvec, width), jnp.float32),
            ],
            compiler_params=params,
            cost_estimate=cost,
            name="column_terms",
        )(place, tile_rows, tile_cols, tile_count, energy, *x_col, *parts)
    with jax.named_scope("row_terms"):
        col_send, row_send, row_keep = pl.pallas_call(
            functools.partial(row_kernel, n_row, n_col, slots),
            out_shape=[blocks(n_row // 2)] + [blocks(n_col // 2)] * 2,
            in_specs=[SMEM] * 4 + [VMEM] * 6,
            out_specs=[VMEM] * 3,
            scratch_shapes=[
                pltpu.VMEM((n_row, 3 * nvec, width), jnp.bfloat16),
                pltpu.VMEM((n_col + 1, nvec, width), jnp.float32),
            ],
            compiler_params=params,
            cost_estimate=cost,
            name="row_terms",
        )(place, tile_rows, tile_cols, tile_count, *x_row, col_send, *parts)
    with jax.named_scope("return_products"):
        sums = halve(col_send, col_keep, "row") + halve(row_send, row_keep, "col")
    with jax.named_scope("product"):
        product, squares = pl.pallas_call(
            product_kernel,
            out_shape=[block, jax.ShapeDtypeStruct((devices, 3, packed_rows, width), jnp.float32)],
            in_specs=[VMEM] * 5,
            out_specs=[VMEM] * 2,
            compiler_params=params,
            name="product",
        )(vectors, *sums)
        squares = swap(squares, ("row", "col"))
    with jax.named_scope("results"):
        residual, rayleigh, gram, sound = pl.pallas_call(
            functools.partial(result_kernel, scale),
            out_shape=[block, square, square, jax.ShapeDtypeStruct((1, 1), jnp.int32)],
            in_specs=[VMEM] * 3,
            out_specs=[VMEM] * 3 + [SMEM],
            compiler_params=params,
            name="results",
        )(vectors, product, squares)

    def from_residual(_):
        parts = pl.pallas_call(
            functools.partial(gram_parts_kernel, scale),
            out_shape=jax.ShapeDtypeStruct((devices, packed_rows, width), jnp.float32),
            in_specs=[VMEM] * 3,
            out_specs=VMEM,
            compiler_params=params,
            name="gram_parts",
        )(vectors, product, squares)
        gram = pl.pallas_call(
            functools.partial(gram_kernel, scale),
            out_shape=square,
            in_specs=[VMEM],
            out_specs=VMEM,
            compiler_params=params,
            name="gram_sum",
        )(swap(parts, ("row", "col")))
        return jnp.int32(1), gram

    with jax.named_scope("gram"):
        _, gram = lax.while_loop(lambda state: state[0] == 0, from_residual, (sound[0, 0], gram))
    return (residual, rayleigh, gram)


def solution(mesh):
    return jax.shard_map(
        per_device,
        mesh=mesh,
        in_specs=(
            P(None, ("row", "col")),
            P(("row", "col")),
            P("row", "col", None, None, None),
            P("row", "col", None),
            P("row", "col", None),
            P("row", "col"),
        ),
        out_specs=(P(None, ("row", "col")), P(), P()),
        check_vma=False,
    )
```

```python
import functools

import jax
import jax.numpy as jnp
from jax import lax
from jax.experimental import pallas as pl
from jax.experimental.pallas import tpu as pltpu
from jax.sharding import PartitionSpec as P

HP = lax.Precision.HIGHEST
VMEM = pl.BlockSpec(memory_space=pltpu.VMEM)
SMEM = pl.BlockSpec(memory_space=pltpu.SMEM)


def mult(left, right):
    return lax.dot_general(left, right, (((1,), (0,)), ((), ())), precision=HP, preferred_element_type=jnp.float32)


def mult_last(left, right):
    return lax.dot_general(left, right, (((1,), (1,)), ((), ())), precision=HP, preferred_element_type=jnp.float32)


def swap(blocks, axis):
    return lax.all_to_all(blocks, axis, 0, 0, tiled=True)


def trade(value, axis, flip):
    size = lax.axis_size(axis)
    return lax.ppermute(value, axis, [(p, p ^ flip) for p in range(size)])


def own_lanes(nvec, width):
    row = lax.broadcasted_iota(jnp.int32, (nvec, width), 0)
    lane = lax.broadcasted_iota(jnp.int32, (nvec, width), 1)
    return lane // nvec == row % (width // nvec)


def packed_gram(left, right):
    nvec, width = right.shape
    per = width // nvec
    wide = mult_last(left, jnp.concatenate([right] * per, axis=0))
    mask = own_lanes(nvec, width)
    squares = []
    for first in range(0, left.shape[0], nvec):
        own = jnp.where(mask, wide[first : first + nvec], 0.0)
        squares.append(jnp.sum(own.reshape(nvec // per, per, width), axis=1))
    return squares


def unpack(packed, nvec):
    rows, width = packed[0].shape
    per = width // nvec
    lane = lax.broadcasted_iota(jnp.int32, (width, nvec), 0)
    column = lax.broadcasted_iota(jnp.int32, (width, nvec), 1)
    mask = own_lanes(nvec, width)
    wide = []
    for square in packed:
        spread = jnp.concatenate([jnp.broadcast_to(square[g : g + 1], (per, width)) for g in range(rows)], axis=0)
        wide.append(jnp.where(mask, spread, 0.0))
    fold = (lane % nvec == column).astype(jnp.bfloat16)
    pieces = [jnp.dot(part, fold, preferred_element_type=jnp.float32) for part in split(jnp.concatenate(wide, axis=0))]
    return (pieces[2] + pieces[1]) + pieces[0]


def split(value):
    first = value.astype(jnp.bfloat16)
    rest = value - first.astype(jnp.float32)
    second = rest.astype(jnp.bfloat16)
    return first, second, (rest - second.astype(jnp.float32)).astype(jnp.bfloat16)


def stack_split(value):
    return jnp.concatenate(split(value), axis=0)


def parts_product(stacked, parts, dims):
    nvec = stacked.shape[0] // 3
    total = None
    for used, part in zip((1, 2, 3), parts[::-1]):
        wide = lax.dot_general(stacked[: used * nvec], part, dims, preferred_element_type=jnp.float32)
        for row in reversed(range(used)):
            piece = wide[row * nvec : (row + 1) * nvec]
            total = piece if total is None else total + piece
    return total


def join_kernel(axes, *refs):
    for which, out in enumerate(refs[-axes:]):
        mine, other = refs[2 * which : 2 * which + 2]
        half = mine.shape[0]
        out[:half] = mine[...]
        out[half:] = other[...]


def prepare_kernel(slots, tiles, *refs):
    small, parts, copies = refs[:3], refs[3:6], refs[6:]
    for array, copy in zip(small, copies):
        copy[...] = array[...]
    for slot in range(slots):
        for part, piece in zip(parts, split(tiles[0, 0, slot])):
            part[slot] = piece


def part_blocks(sums, total, send, keep):
    for block in range(total // 2):
        keep[block] = sums[2 * block]
        send[block] = sums[2 * block + 1]


def column_kernel(n_row, n_col, slots, place, arow, bcol, count, d_ref, near, far, *refs):
    *parts, send, keep, rows, sums = refs
    me_row, me_col = place[0], place[1]
    half = n_col // 2
    for flip in range(n_col):
        rows[flip] = stack_split(near[flip] if flip < half else far[flip - half])
    sums[...] = jnp.zeros_like(sums)
    sums[0] = d_ref[...] * near[0]
    for slot in range(slots):
        pieces = [part[slot] for part in parts]
        block = jnp.where(slot < count[0, 0], bcol[0, 0, slot] ^ me_row, n_row)
        sums[block] += parts_product(rows[arow[0, 0, slot] ^ me_col], pieces, (((1,), (0,)), ((), ())))
    part_blocks(sums, n_row, send, keep)


def hand_on_kernel(early, after, late):
    del after
    late[...] = early[...]


def row_kernel(n_row, n_col, slots, place, arow, bcol, count, near, far, *refs):
    *parts, send, keep, cols, sums = refs
    me_row, me_col = place[0], place[1]
    half = n_row // 2
    for flip in range(n_row):
        cols[flip] = stack_split(near[flip] if flip < half else far[flip - half])
    sums[...] = jnp.zeros_like(sums)
    for slot in range(slots):
        block = jnp.where(slot < count[0, 0], arow[0, 0, slot] ^ me_col, n_col)
        pieces = [part[slot] for part in parts]
        sums[block] += parts_product(cols[bcol[0, 0, slot] ^ me_row], pieces, (((1,), (1,)), ((), ())))
    part_blocks(sums, n_col, send, keep)


def halve_kernel(mine, other, send, keep):
    part_blocks([mine[block] + other[block] for block in range(mine.shape[0])], mine.shape[0], send, keep)


def product_kernel(x_ref, *refs):
    parts, (product, out) = refs[:-2], refs[-2:]
    own = x_ref[...]
    total = parts[0][0]
    for part in parts[1:]:
        total += part[0]
    product[...] = total
    squares = packed_gram(jnp.concatenate([own, total], axis=0), total) + packed_gram(own, own)
    for block in range(out.shape[0]):
        for which, square in enumerate(squares):
            out[block, which] = square


def summed_squares(scale, parts, nvec):
    sums = jnp.sum(parts[...], axis=0)
    squares = unpack([sums[which] for which in range(3)], nvec) * scale
    return squares[:nvec], squares[nvec : 2 * nvec], squares[2 * nvec :]


def result_kernel(scale, x_ref, product, parts, residual, rayleigh, gram, sound):
    own = x_ref[...]
    nvec = own.shape[0]
    ray, outer, inner = summed_squares(scale, parts, nvec)
    rayleigh[...] = ray
    residual[...] = product[...] - mult(ray, own)
    twice = mult(ray, ray)
    lifted = mult_last(mult(ray, inner), ray)
    result = outer - (twice + twice.T) + lifted
    gram[...] = result
    diagonal = lax.broadcasted_iota(jnp.int32, (nvec, nvec), 0) == lax.broadcasted_iota(jnp.int32, (nvec, nvec), 1)
    margin = jnp.sum(jnp.where(diagonal, 64.0 * result - (outer + lifted), 0.0))
    sound[0, 0] = (margin >= 0.0).astype(jnp.int32)


def gram_parts_kernel(scale, x_ref, product, parts, out):
    own = x_ref[...]
    ray, _, _ = summed_squares(scale, parts, own.shape[0])
    residual = product[...] - mult(ray, own)
    square = packed_gram(residual, residual)[0]
    for block in range(out.shape[0]):
        out[block] = square


def gram_kernel(scale, parts, out):
    out[...] = unpack([jnp.sum(parts[...], axis=0)], out.shape[0]) * scale


def per_device(vectors, diagonal_energy, tiles, tile_rows, tile_cols, tile_count):
    n_row = lax.axis_size("row")
    n_col = lax.axis_size("col")
    devices = n_row * n_col
    nvec, width = vectors.shape
    slots = tiles.shape[2]
    scale = 1.0 / float(devices * width)
    packed_rows = nvec * nvec // width
    block = jax.ShapeDtypeStruct((nvec, width), jnp.float32)
    square = jax.ShapeDtypeStruct((nvec, nvec), jnp.float32)
    part = jax.ShapeDtypeStruct((slots, width, width), jnp.bfloat16)
    place = jnp.stack([lax.axis_index("row"), lax.axis_index("col")]).astype(jnp.int32)
    energy = diagonal_energy.reshape(1, width)
    params = pltpu.CompilerParams(vmem_limit_bytes=16 * 2**20)
    cost = pl.CostEstimate(flops=12 * slots * nvec * width * width, bytes_accessed=2**20, transcendentals=0)

    def blocks(total):
        return jax.ShapeDtypeStruct((total, nvec, width), jnp.float32)

    def gather(axes, after):
        near = [vectors[None]] * len(axes)
        far = [trade(vectors[None], axis, 1) for axis in axes]
        reach = 2
        while any(reach < lax.axis_size(axis) for axis in axes):
            going = [which for which, axis in enumerate(axes) if reach < lax.axis_size(axis)]
            joined = pl.pallas_call(
                functools.partial(join_kernel, len(going)),
                out_shape=[blocks(reach)] * len(going),
                in_specs=[VMEM] * (2 * len(going)) + [pl.BlockSpec(memory_space=pl.ANY)] * len(after),
                out_specs=[VMEM] * len(going),
                compiler_params=params,
                name="join",
            )(*[half for which in going for half in (near[which], far[which])], *after)
            for which, half in zip(going, joined):
                near[which], far[which] = half, trade(half, axes[which], reach)
            reach *= 2
            after = ()
        return list(zip(near, far))

    def halve(send, keep, axis):
        flip = 1
        while keep.shape[0] > 1:
            half = keep.shape[0] // 2
            send, keep = pl.pallas_call(
                halve_kernel,
                out_shape=[blocks(half)] * 2,
                in_specs=[VMEM] * 2,
                out_specs=[VMEM] * 2,
                compiler_params=params,
                name="halve_" + axis,
            )(keep, trade(send, axis, flip))
            flip *= 2
        return keep, trade(send, axis, flip)

    with jax.named_scope("prepare"):
        small = (tile_rows, tile_cols, energy)
        *parts, arow, bcol, energy = pl.pallas_call(
            functools.partial(prepare_kernel, slots),
            out_shape=[part] * 3 + [jax.ShapeDtypeStruct(array.shape, array.dtype) for array in small],
            in_specs=[VMEM] * 4,
            out_specs=[VMEM] * 6,
            compiler_params=params,
            cost_estimate=pl.CostEstimate(flops=0, bytes_accessed=5 * slots * width * width, transcendentals=0),
            name="prepare",
        )(tiles, *small)
    with jax.named_scope("share_vectors"):
        x_row, x_col = gather(("row", "col"), parts[:1])
    with jax.named_scope("column_terms"):
        col_send, col_keep = pl.pallas_call(
            functools.partial(column_kernel, n_row, n_col, slots),
            out_shape=[blocks(n_row // 2)] * 2,
            in_specs=[SMEM] * 4 + [VMEM] * 6,
            out_specs=[VMEM] * 2,
            scratch_shapes=[
                pltpu.VMEM((n_col, 3 * nvec, width), jnp.bfloat16),
                pltpu.VMEM((n_row + 1, nvec, width), jnp.float32),
            ],
            compiler_params=params,
            cost_estimate=cost,
            name="column_terms",
        )(place, arow, bcol, tile_count, energy, *x_col, *parts)
        col_send = pl.pallas_call(
            hand_on_kernel,
            out_shape=blocks(n_row // 2),
            in_specs=[VMEM, pl.BlockSpec(memory_space=pl.ANY)],
            out_specs=VMEM,
            compiler_params=params,
            name="hand_on",
        )(col_send, x_row[1])
    with jax.named_scope("row_terms"):
        row_send, row_keep = pl.pallas_call(
            functools.partial(row_kernel, n_row, n_col, slots),
            out_shape=[blocks(n_col // 2)] * 2,
            in_specs=[SMEM] * 4 + [VMEM] * 5,
            out_specs=[VMEM] * 2,
            scratch_shapes=[
                pltpu.VMEM((n_row, 3 * nvec, width), jnp.bfloat16),
                pltpu.VMEM((n_col + 1, nvec, width), jnp.float32),
            ],
            compiler_params=params,
            cost_estimate=cost,
            name="row_terms",
        )(place, arow, bcol, tile_count, *x_row, *parts)
    with jax.named_scope("return_products"):
        sums = halve(col_send, col_keep, "row") + halve(row_send, row_keep, "col")
    with jax.named_scope("product"):
        product, squares = pl.pallas_call(
            product_kernel,
            out_shape=[block, jax.ShapeDtypeStruct((devices, 3, packed_rows, width), jnp.float32)],
            in_specs=[VMEM] * 5,
            out_specs=[VMEM] * 2,
            compiler_params=params,
            name="product",
        )(vectors, *sums)
        squares = swap(squares, ("row", "col"))
    with jax.named_scope("results"):
        residual, rayleigh, gram, sound = pl.pallas_call(
            functools.partial(result_kernel, scale),
            out_shape=[block, square, square, jax.ShapeDtypeStruct((1, 1), jnp.int32)],
            in_specs=[VMEM] * 3,
            out_specs=[VMEM] * 3 + [SMEM],
            compiler_params=params,
            name="results",
        )(vectors, product, squares)

    def from_residual(_):
        parts = pl.pallas_call(
            functools.partial(gram_parts_kernel, scale),
            out_shape=jax.ShapeDtypeStruct((devices, packed_rows, width), jnp.float32),
            in_specs=[VMEM] * 3,
            out_specs=VMEM,
            compiler_params=params,
            name="gram_parts",
        )(vectors, product, squares)
        gram = pl.pallas_call(
            functools.partial(gram_kernel, scale),
            out_shape=square,
            in_specs=[VMEM],
            out_specs=VMEM,
            compiler_params=params,
            name="gram_sum",
        )(swap(parts, ("row", "col")))
        return jnp.int32(1), gram

    with jax.named_scope("gram"):
        _, gram = lax.while_loop(lambda state: state[0] == 0, from_residual, (sound[0, 0], gram))
    return (residual, rayleigh, gram)


def solution(mesh):
    return jax.shard_map(
        per_device,
        mesh=mesh,
        in_specs=(
            P(None, ("row", "col")),
            P(("row", "col")),
            P("row", "col", None, None, None),
            P("row", "col", None),
            P("row", "col", None),
            P("row", "col"),
        ),
        out_specs=(P(None, ("row", "col")), P(), P()),
        check_vma=False,
    )
```

```python
import functools

import jax
import jax.numpy as jnp
from jax import lax
from jax.experimental import pallas as pl
from jax.experimental.pallas import tpu as pltpu
from jax.sharding import PartitionSpec as P

HP = lax.Precision.HIGHEST
VMEM = pl.BlockSpec(memory_space=pltpu.VMEM)
SMEM = pl.BlockSpec(memory_space=pltpu.SMEM)


def mult(left, right):
    return lax.dot_general(left, right, (((1,), (0,)), ((), ())), precision=HP, preferred_element_type=jnp.float32)


def mult_last(left, right):
    return lax.dot_general(left, right, (((1,), (1,)), ((), ())), precision=HP, preferred_element_type=jnp.float32)


def swap(blocks, axis):
    return lax.all_to_all(blocks, axis, 0, 0, tiled=True)


def trade(value, axis, flip):
    size = lax.axis_size(axis)
    return lax.ppermute(value, axis, [(p, p ^ flip) for p in range(size)])


def own_lanes(nvec, width):
    row = lax.broadcasted_iota(jnp.int32, (nvec, width), 0)
    lane = lax.broadcasted_iota(jnp.int32, (nvec, width), 1)
    return lane // nvec == row % (width // nvec)


def packed_gram(left, right):
    nvec, width = right.shape
    per = width // nvec
    wide = mult_last(left, jnp.concatenate([right] * per, axis=0))
    mask = own_lanes(nvec, width)
    squares = []
    for first in range(0, left.shape[0], nvec):
        own = jnp.where(mask, wide[first : first + nvec], 0.0)
        squares.append(jnp.sum(own.reshape(nvec // per, per, width), axis=1))
    return squares


def unpack(packed, nvec):
    rows, width = packed[0].shape
    per = width // nvec
    lane = lax.broadcasted_iota(jnp.int32, (width, nvec), 0)
    column = lax.broadcasted_iota(jnp.int32, (width, nvec), 1)
    mask = own_lanes(nvec, width)
    wide = []
    for square in packed:
        spread = jnp.concatenate([jnp.broadcast_to(square[g : g + 1], (per, width)) for g in range(rows)], axis=0)
        wide.append(jnp.where(mask, spread, 0.0))
    fold = (lane % nvec == column).astype(jnp.bfloat16)
    pieces = [jnp.dot(part, fold, preferred_element_type=jnp.float32) for part in split(jnp.concatenate(wide, axis=0))]
    return (pieces[2] + pieces[1]) + pieces[0]


def split(value):
    first = value.astype(jnp.bfloat16)
    rest = value - first.astype(jnp.float32)
    second = rest.astype(jnp.bfloat16)
    return first, second, (rest - second.astype(jnp.float32)).astype(jnp.bfloat16)


def stack_split(value):
    return jnp.concatenate(split(value), axis=0)


def pair_products(stacked, parts, transposed):
    nvec, width = stacked[0].shape[0] // 3, stacked[0].shape[1]
    dims = (((1,), (1 if transposed else 0,)), ((), ()))
    axis = 0 if transposed else 1

    def wide(left, pieces):
        return lax.dot_general(left, jnp.concatenate(pieces, axis=axis), dims, preferred_element_type=jnp.float32)

    last = wide(jnp.concatenate([value[:nvec] for value in stacked], axis=0), [part[2] for part in parts])
    results = []
    for which, (value, part) in enumerate(zip(stacked, parts)):
        both = wide(value, part[:2])
        first, second = both[:, :width], both[:, width:]
        total = last[which * nvec : (which + 1) * nvec, which * width : (which + 1) * width]
        total = (total + second[nvec : 2 * nvec]) + first[2 * nvec :]
        total = (total + second[:nvec]) + first[nvec : 2 * nvec]
        results.append(total + first[:nvec])
    return results


def join_kernel(axes, *refs):
    for which, out in enumerate(refs[-axes:]):
        mine, other = refs[2 * which : 2 * which + 2]
        half = mine.shape[0]
        out[:half] = mine[...]
        out[half:] = other[...]


def prepare_kernel(slots, tiles, *refs):
    small, parts, copies = refs[:3], refs[3:6], refs[6:]
    for array, copy in zip(small, copies):
        copy[...] = array[...]
    for slot in range(slots):
        for part, piece in zip(parts, split(tiles[0, 0, slot])):
            part[slot] = piece


def part_blocks(sums, total, send, keep):
    for block in range(total // 2):
        keep[block] = sums[2 * block]
        send[block] = sums[2 * block + 1]


def column_kernel(n_row, n_col, slots, place, arow, bcol, count, d_ref, near, far, *refs):
    *parts, send, keep, rows, sums = refs
    me_row, me_col = place[0], place[1]
    half = n_col // 2
    for flip in range(n_col):
        rows[flip] = stack_split(near[flip] if flip < half else far[flip - half])
    sums[...] = jnp.zeros_like(sums)
    sums[0] = d_ref[...] * near[0]
    for pair in range(0, slots, 2):
        pieces = [[part[slot] for part in parts] for slot in (pair, pair + 1)]
        values = [rows[arow[0, 0, slot] ^ me_col] for slot in (pair, pair + 1)]
        for slot, terms in zip((pair, pair + 1), pair_products(values, pieces, False)):
            block = jnp.where(slot < count[0, 0], bcol[0, 0, slot] ^ me_row, n_row)
            sums[block] += terms
    part_blocks(sums, n_row, send, keep)


def hand_on_kernel(early, after, late):
    del after
    late[...] = early[...]


def row_kernel(n_row, n_col, slots, place, arow, bcol, count, near, far, *refs):
    *parts, send, keep, cols, sums = refs
    me_row, me_col = place[0], place[1]
    half = n_row // 2
    for flip in range(n_row):
        cols[flip] = stack_split(near[flip] if flip < half else far[flip - half])
    sums[...] = jnp.zeros_like(sums)
    for pair in range(0, slots, 2):
        pieces = [[part[slot] for part in parts] for slot in (pair, pair + 1)]
        values = [cols[bcol[0, 0, slot] ^ me_row] for slot in (pair, pair + 1)]
        for slot, terms in zip((pair, pair + 1), pair_products(values, pieces, True)):
            block = jnp.where(slot < count[0, 0], arow[0, 0, slot] ^ me_col, n_col)
            sums[block] += terms
    part_blocks(sums, n_col, send, keep)


def halve_kernel(mine, other, send, keep):
    part_blocks([mine[block] + other[block] for block in range(mine.shape[0])], mine.shape[0], send, keep)


def product_kernel(x_ref, *refs):
    parts, (product, out) = refs[:-2], refs[-2:]
    own = x_ref[...]
    total = parts[0][0]
    for part in parts[1:]:
        total += part[0]
    product[...] = total
    squares = packed_gram(jnp.concatenate([own, total], axis=0), total) + packed_gram(own, own)
    for block in range(out.shape[0]):
        for which, square in enumerate(squares):
            out[block, which] = square


def summed_squares(scale, parts, nvec):
    sums = jnp.sum(parts[...], axis=0)
    squares = unpack([sums[which] for which in range(3)], nvec) * scale
    return squares[:nvec], squares[nvec : 2 * nvec], squares[2 * nvec :]


def result_kernel(scale, x_ref, product, parts, residual, rayleigh, gram, sound):
    own = x_ref[...]
    nvec = own.shape[0]
    ray, outer, inner = summed_squares(scale, parts, nvec)
    rayleigh[...] = ray
    residual[...] = product[...] - mult(ray, own)
    twice = mult(ray, ray)
    lifted = mult_last(mult(ray, inner), ray)
    result = outer - (twice + twice.T) + lifted
    gram[...] = result
    diagonal = lax.broadcasted_iota(jnp.int32, (nvec, nvec), 0) == lax.broadcasted_iota(jnp.int32, (nvec, nvec), 1)
    margin = jnp.sum(jnp.where(diagonal, 64.0 * result - (outer + lifted), 0.0), keepdims=True)
    sound[...] = (margin >= 0.0).astype(jnp.int32)


def gram_parts_kernel(scale, x_ref, product, parts, out):
    own = x_ref[...]
    ray, _, _ = summed_squares(scale, parts, own.shape[0])
    residual = product[...] - mult(ray, own)
    square = packed_gram(residual, residual)[0]
    for block in range(out.shape[0]):
        out[block] = square


def gram_kernel(scale, parts, out):
    out[...] = unpack([jnp.sum(parts[...], axis=0)], out.shape[0]) * scale


def per_device(vectors, diagonal_energy, tiles, tile_rows, tile_cols, tile_count):
    n_row = lax.axis_size("row")
    n_col = lax.axis_size("col")
    devices = n_row * n_col
    nvec, width = vectors.shape
    slots = tiles.shape[2]
    scale = 1.0 / float(devices * width)
    packed_rows = nvec * nvec // width
    block = jax.ShapeDtypeStruct((nvec, width), jnp.float32)
    square = jax.ShapeDtypeStruct((nvec, nvec), jnp.float32)
    part = jax.ShapeDtypeStruct((slots, width, width), jnp.bfloat16)
    place = jnp.stack([lax.axis_index("row"), lax.axis_index("col")]).astype(jnp.int32)
    energy = diagonal_energy.reshape(1, width)
    params = pltpu.CompilerParams(vmem_limit_bytes=16 * 2**20)
    cost = pl.CostEstimate(flops=12 * slots * nvec * width * width, bytes_accessed=2**20, transcendentals=0)

    def blocks(total):
        return jax.ShapeDtypeStruct((total, nvec, width), jnp.float32)

    def gather(axes, after):
        near = [vectors[None]] * len(axes)
        far = [trade(vectors[None], axis, 1) for axis in axes]
        reach = 2
        while any(reach < lax.axis_size(axis) for axis in axes):
            going = [which for which, axis in enumerate(axes) if reach < lax.axis_size(axis)]
            joined = pl.pallas_call(
                functools.partial(join_kernel, len(going)),
                out_shape=[blocks(reach)] * len(going),
                in_specs=[VMEM] * (2 * len(going)) + [pl.BlockSpec(memory_space=pl.ANY)] * len(after),
                out_specs=[VMEM] * len(going),
                compiler_params=params,
                name="join",
            )(*[half for which in going for half in (near[which], far[which])], *after)
            for which, half in zip(going, joined):
                near[which], far[which] = half, trade(half, axes[which], reach)
            reach *= 2
            after = ()
        return list(zip(near, far))

    def halve(send, keep, axis):
        flip = 1
        while keep.shape[0] > 1:
            half = keep.shape[0] // 2
            send, keep = pl.pallas_call(
                halve_kernel,
                out_shape=[blocks(half)] * 2,
                in_specs=[VMEM] * 2,
                out_specs=[VMEM] * 2,
                compiler_params=params,
                name="halve_" + axis,
            )(keep, trade(send, axis, flip))
            flip *= 2
        return keep, trade(send, axis, flip)

    with jax.named_scope("prepare"):
        small = (tile_rows, tile_cols, energy)
        *parts, arow, bcol, energy = pl.pallas_call(
            functools.partial(prepare_kernel, slots),
            out_shape=[part] * 3 + [jax.ShapeDtypeStruct(array.shape, array.dtype) for array in small],
            in_specs=[VMEM] * 4,
            out_specs=[VMEM] * 6,
            compiler_params=params,
            cost_estimate=pl.CostEstimate(flops=0, bytes_accessed=5 * slots * width * width, transcendentals=0),
            name="prepare",
        )(tiles, *small)
    with jax.named_scope("share_vectors"):
        x_row, x_col = gather(("row", "col"), parts[:1])
    with jax.named_scope("column_terms"):
        col_send, col_keep = pl.pallas_call(
            functools.partial(column_kernel, n_row, n_col, slots),
            out_shape=[blocks(n_row // 2)] * 2,
            in_specs=[SMEM] * 4 + [VMEM] * 6,
            out_specs=[VMEM] * 2,
            scratch_shapes=[
                pltpu.VMEM((n_col, 3 * nvec, width), jnp.bfloat16),
                pltpu.VMEM((n_row + 1, nvec, width), jnp.float32),
            ],
            compiler_params=params,
            cost_estimate=cost,
            name="column_terms",
        )(place, arow, bcol, tile_count, energy, *x_col, *parts)
        col_send = pl.pallas_call(
            hand_on_kernel,
            out_shape=blocks(n_row // 2),
            in_specs=[VMEM, pl.BlockSpec(memory_space=pl.ANY)],
            out_specs=VMEM,
            compiler_params=params,
            name="hand_on",
        )(col_send, x_row[1])
    with jax.named_scope("row_terms"):
        row_send, row_keep = pl.pallas_call(
            functools.partial(row_kernel, n_row, n_col, slots),
            out_shape=[blocks(n_col // 2)] * 2,
            in_specs=[SMEM] * 4 + [VMEM] * 5,
            out_specs=[VMEM] * 2,
            scratch_shapes=[
                pltpu.VMEM((n_row, 3 * nvec, width), jnp.bfloat16),
                pltpu.VMEM((n_col + 1, nvec, width), jnp.float32),
            ],
            compiler_params=params,
            cost_estimate=cost,
            name="row_terms",
        )(place, arow, bcol, tile_count, *x_row, *parts)
    with jax.named_scope("return_products"):
        sums = halve(col_send, col_keep, "row") + halve(row_send, row_keep, "col")
    with jax.named_scope("product"):
        product, squares = pl.pallas_call(
            product_kernel,
            out_shape=[block, jax.ShapeDtypeStruct((devices, 3, packed_rows, width), jnp.float32)],
            in_specs=[VMEM] * 5,
            out_specs=[VMEM] * 2,
            compiler_params=params,
            name="product",
        )(vectors, *sums)
        squares = swap(squares, ("row", "col"))
    with jax.named_scope("results"):
        residual, rayleigh, gram, sound = pl.pallas_call(
            functools.partial(result_kernel, scale),
            out_shape=[block, square, square, jax.ShapeDtypeStruct((1, 1), jnp.int32)],
            in_specs=[VMEM] * 3,
            out_specs=[VMEM] * 4,
            compiler_params=params,
            name="results",
        )(vectors, product, squares)

    def from_residual(_):
        parts = pl.pallas_call(
            functools.partial(gram_parts_kernel, scale),
            out_shape=jax.ShapeDtypeStruct((devices, packed_rows, width), jnp.float32),
            in_specs=[VMEM] * 3,
            out_specs=VMEM,
            compiler_params=params,
            name="gram_parts",
        )(vectors, product, squares)
        gram = pl.pallas_call(
            functools.partial(gram_kernel, scale),
            out_shape=square,
            in_specs=[VMEM],
            out_specs=VMEM,
            compiler_params=params,
            name="gram_sum",
        )(swap(parts, ("row", "col")))
        return jnp.int32(1), gram

    with jax.named_scope("gram"):
        _, gram = lax.while_loop(lambda state: state[0] == 0, from_residual, (sound[0, 0], gram))
    return (residual, rayleigh, gram)


def solution(mesh):
    return jax.shard_map(
        per_device,
        mesh=mesh,
        in_specs=(
            P(None, ("row", "col")),
            P(("row", "col")),
            P("row", "col", None, None, None),
            P("row", "col", None),
            P("row", "col", None),
            P("row", "col"),
        ),
        out_specs=(P(None, ("row", "col")), P(), P()),
        check_vma=False,
    )
```

```python
import functools

import jax
import jax.numpy as jnp
from jax import lax
from jax.experimental import pallas as pl
from jax.experimental.pallas import tpu as pltpu
from jax.sharding import PartitionSpec as P

HP = lax.Precision.HIGHEST
VMEM = pl.BlockSpec(memory_space=pltpu.VMEM)
SMEM = pl.BlockSpec(memory_space=pltpu.SMEM)


def mult(left, right):
    return lax.dot_general(left, right, (((1,), (0,)), ((), ())), precision=HP, preferred_element_type=jnp.float32)


def mult_last(left, right):
    return lax.dot_general(left, right, (((1,), (1,)), ((), ())), precision=HP, preferred_element_type=jnp.float32)


def swap(blocks, axis):
    return lax.all_to_all(blocks, axis, 0, 0, tiled=True)


def trade(value, axis, flip):
    size = lax.axis_size(axis)
    return lax.ppermute(value, axis, [(p, p ^ flip) for p in range(size)])


def own_lanes(nvec, width):
    row = lax.broadcasted_iota(jnp.int32, (nvec, width), 0)
    lane = lax.broadcasted_iota(jnp.int32, (nvec, width), 1)
    return lane // nvec == row % (width // nvec)


def packed_gram(left, right):
    nvec, width = right.shape
    per = width // nvec
    wide = mult_last(left, jnp.concatenate([right] * per, axis=0))
    mask = own_lanes(nvec, width)
    squares = []
    for first in range(0, left.shape[0], nvec):
        own = jnp.where(mask, wide[first : first + nvec], 0.0)
        squares.append(jnp.sum(own.reshape(nvec // per, per, width), axis=1))
    return squares


def unpack(packed, nvec):
    rows, width = packed[0].shape
    per = width // nvec
    lane = lax.broadcasted_iota(jnp.int32, (width, nvec), 0)
    column = lax.broadcasted_iota(jnp.int32, (width, nvec), 1)
    mask = own_lanes(nvec, width)
    wide = []
    for square in packed:
        spread = jnp.concatenate([jnp.broadcast_to(square[g : g + 1], (per, width)) for g in range(rows)], axis=0)
        wide.append(jnp.where(mask, spread, 0.0))
    fold = (lane % nvec == column).astype(jnp.bfloat16)
    pieces = [jnp.dot(part, fold, preferred_element_type=jnp.float32) for part in split(jnp.concatenate(wide, axis=0))]
    return (pieces[2] + pieces[1]) + pieces[0]


def split(value):
    first = value.astype(jnp.bfloat16)
    rest = value - first.astype(jnp.float32)
    second = rest.astype(jnp.bfloat16)
    return first, second, (rest - second.astype(jnp.float32)).astype(jnp.bfloat16)


def stack_split(value):
    return jnp.concatenate(split(value), axis=0)


def pair_products(stacked, parts, transposed):
    nvec, width = stacked[0].shape[0] // 3, stacked[0].shape[1]
    dims = (((1,), (1 if transposed else 0,)), ((), ()))
    axis = 0 if transposed else 1

    def wide(left, pieces):
        return lax.dot_general(left, jnp.concatenate(pieces, axis=axis), dims, preferred_element_type=jnp.float32)

    last = wide(jnp.concatenate([value[:nvec] for value in stacked], axis=0), [part[2] for part in parts])
    results = []
    for which, (value, part) in enumerate(zip(stacked, parts)):
        both = wide(value, part[:2])
        first, second = both[:, :width], both[:, width:]
        total = last[which * nvec : (which + 1) * nvec, which * width : (which + 1) * width]
        total = (total + second[nvec : 2 * nvec]) + first[2 * nvec :]
        total = (total + second[:nvec]) + first[nvec : 2 * nvec]
        results.append(total + first[:nvec])
    return results


def pair_kernel(mine, other, after, out):
    del after
    out[0] = mine[...]
    out[1] = other[...]


def prepare_kernel(slots, tiles, *refs):
    small, parts, copies = refs[:3], refs[3:6], refs[6:]
    for array, copy in zip(small, copies):
        copy[...] = array[...]
    for slot in range(slots):
        for part, piece in zip(parts, split(tiles[0, 0, slot])):
            part[slot] = piece


def part_blocks(sums, total, send, keep):
    for block in range(total // 2):
        keep[block] = sums[2 * block]
        send[block] = sums[2 * block + 1]


def column_kernel(n_row, n_col, slots, place, arow, bcol, count, d_ref, *refs):
    x_col, (*parts, send, keep, rows, sums) = refs[:n_col], refs[n_col:]
    me_row, me_col = place[0], place[1]
    for flip in range(n_col):
        rows[flip] = stack_split(x_col[flip][...])
    sums[...] = jnp.zeros_like(sums)
    sums[0] = d_ref[...] * x_col[0][...]
    for pair in range(0, slots, 2):
        pieces = [[part[slot] for part in parts] for slot in (pair, pair + 1)]
        values = [rows[arow[0, 0, slot] ^ me_col] for slot in (pair, pair + 1)]
        for slot, terms in zip((pair, pair + 1), pair_products(values, pieces, False)):
            block = jnp.where(slot < count[0, 0], bcol[0, 0, slot] ^ me_row, n_row)
            sums[block] += terms
    part_blocks(sums, n_row, send, keep)


def hand_on_kernel(early, *refs):
    late = refs[-1]
    late[...] = early[...]


def row_kernel(n_row, n_col, slots, place, arow, bcol, count, *refs):
    x_pairs, (*parts, send, keep, cols, sums) = refs[: n_row // 2], refs[n_row // 2 :]
    me_row, me_col = place[0], place[1]
    for flip in range(n_row):
        cols[flip] = stack_split(x_pairs[flip // 2][flip % 2])
    sums[...] = jnp.zeros_like(sums)
    for pair in range(0, slots, 2):
        pieces = [[part[slot] for part in parts] for slot in (pair, pair + 1)]
        values = [cols[bcol[0, 0, slot] ^ me_row] for slot in (pair, pair + 1)]
        for slot, terms in zip((pair, pair + 1), pair_products(values, pieces, True)):
            block = jnp.where(slot < count[0, 0], arow[0, 0, slot] ^ me_col, n_col)
            sums[block] += terms
    part_blocks(sums, n_col, send, keep)


def halve_kernel(mine, other, send, keep):
    part_blocks([mine[block] + other[block] for block in range(mine.shape[0])], mine.shape[0], send, keep)


def product_kernel(x_ref, *refs):
    parts, (product, out) = refs[:-2], refs[-2:]
    own = x_ref[...]
    total = parts[0][0]
    for part in parts[1:]:
        total += part[0]
    product[...] = total
    squares = packed_gram(jnp.concatenate([own, total], axis=0), total) + packed_gram(own, own)
    for block in range(out.shape[0]):
        for which, square in enumerate(squares):
            out[block, which] = square


def summed_squares(scale, parts, nvec):
    sums = jnp.sum(parts[...], axis=0)
    squares = unpack([sums[which] for which in range(3)], nvec) * scale
    return squares[:nvec], squares[nvec : 2 * nvec], squares[2 * nvec :]


def result_kernel(scale, x_ref, product, parts, residual, rayleigh, gram, sound):
    own = x_ref[...]
    nvec = own.shape[0]
    ray, outer, inner = summed_squares(scale, parts, nvec)
    rayleigh[...] = ray
    residual[...] = product[...] - mult(ray, own)
    twice = mult(ray, ray)
    lifted = mult_last(mult(ray, inner), ray)
    result = outer - (twice + twice.T) + lifted
    gram[...] = result
    diagonal = lax.broadcasted_iota(jnp.int32, (nvec, nvec), 0) == lax.broadcasted_iota(jnp.int32, (nvec, nvec), 1)
    margin = jnp.sum(jnp.where(diagonal, 64.0 * result - (outer + lifted), 0.0), keepdims=True)
    sound[...] = (margin >= 0.0).astype(jnp.int32)


def gram_parts_kernel(scale, x_ref, product, parts, out):
    own = x_ref[...]
    ray, _, _ = summed_squares(scale, parts, own.shape[0])
    residual = product[...] - mult(ray, own)
    square = packed_gram(residual, residual)[0]
    for block in range(out.shape[0]):
        out[block] = square


def gram_kernel(scale, parts, out):
    out[...] = unpack([jnp.sum(parts[...], axis=0)], out.shape[0]) * scale


def per_device(vectors, diagonal_energy, tiles, tile_rows, tile_cols, tile_count):
    n_row = lax.axis_size("row")
    n_col = lax.axis_size("col")
    devices = n_row * n_col
    nvec, width = vectors.shape
    slots = tiles.shape[2]
    scale = 1.0 / float(devices * width)
    packed_rows = nvec * nvec // width
    block = jax.ShapeDtypeStruct((nvec, width), jnp.float32)
    square = jax.ShapeDtypeStruct((nvec, nvec), jnp.float32)
    part = jax.ShapeDtypeStruct((slots, width, width), jnp.bfloat16)
    place = jnp.stack([lax.axis_index("row"), lax.axis_index("col")]).astype(jnp.int32)
    energy = diagonal_energy.reshape(1, width)
    params = pltpu.CompilerParams(vmem_limit_bytes=16 * 2**20)
    cost = pl.CostEstimate(flops=12 * slots * nvec * width * width, bytes_accessed=2**20, transcendentals=0)

    def blocks(total):
        return jax.ShapeDtypeStruct((total, nvec, width), jnp.float32)

    def trades(value, axis, flips):
        return [trade(value, axis, flip) for flip in reversed(flips)][::-1]

    def halve(send, keep, axis):
        flip = 1
        while keep.shape[0] > 1:
            half = keep.shape[0] // 2
            send, keep = pl.pallas_call(
                halve_kernel,
                out_shape=[blocks(half)] * 2,
                in_specs=[VMEM] * 2,
                out_specs=[VMEM] * 2,
                compiler_params=params,
                name="halve_" + axis,
            )(keep, trade(send, axis, flip))
            flip *= 2
        return keep, trade(send, axis, flip)

    with jax.named_scope("prepare"):
        small = (tile_rows, tile_cols, energy)
        *parts, arow, bcol, energy = pl.pallas_call(
            functools.partial(prepare_kernel, slots),
            out_shape=[part] * 3 + [jax.ShapeDtypeStruct(array.shape, array.dtype) for array in small],
            in_specs=[VMEM] * 4,
            out_specs=[VMEM] * 6,
            compiler_params=params,
            cost_estimate=pl.CostEstimate(flops=0, bytes_accessed=5 * slots * width * width, transcendentals=0),
            name="prepare",
        )(tiles, *small)
    with jax.named_scope("share_vectors"):
        other = trade(vectors, "row", 1)
        x_col = [vectors] + trades(vectors, "col", range(1, n_col))
        pair = pl.pallas_call(
            pair_kernel,
            out_shape=blocks(2),
            in_specs=[VMEM] * 2 + [pl.BlockSpec(memory_space=pl.ANY)],
            out_specs=VMEM,
            compiler_params=params,
            name="pair",
        )(vectors, other, parts[0])
        x_pairs = [pair] + trades(pair, "row", range(2, n_row, 2))
    with jax.named_scope("column_terms"):
        col_send, col_keep = pl.pallas_call(
            functools.partial(column_kernel, n_row, n_col, slots),
            out_shape=[blocks(n_row // 2)] * 2,
            in_specs=[SMEM] * 4 + [VMEM] * (n_col + 4),
            out_specs=[VMEM] * 2,
            scratch_shapes=[
                pltpu.VMEM((n_col, 3 * nvec, width), jnp.bfloat16),
                pltpu.VMEM((n_row + 1, nvec, width), jnp.float32),
            ],
            compiler_params=params,
            cost_estimate=cost,
            name="column_terms",
        )(place, arow, bcol, tile_count, energy, *x_col, *parts)
        col_send = pl.pallas_call(
            hand_on_kernel,
            out_shape=blocks(n_row // 2),
            in_specs=[VMEM] + [pl.BlockSpec(memory_space=pl.ANY)] * (n_row // 2 - 1),
            out_specs=VMEM,
            compiler_params=params,
            name="hand_on",
        )(col_send, *x_pairs[1:])
    with jax.named_scope("row_terms"):
        row_send, row_keep = pl.pallas_call(
            functools.partial(row_kernel, n_row, n_col, slots),
            out_shape=[blocks(n_col // 2)] * 2,
            in_specs=[SMEM] * 4 + [VMEM] * (n_row // 2 + 3),
            out_specs=[VMEM] * 2,
            scratch_shapes=[
                pltpu.VMEM((n_row, 3 * nvec, width), jnp.bfloat16),
                pltpu.VMEM((n_col + 1, nvec, width), jnp.float32),
            ],
            compiler_params=params,
            cost_estimate=cost,
            name="row_terms",
        )(place, arow, bcol, tile_count, *x_pairs, *parts)
    with jax.named_scope("return_products"):
        sums = halve(col_send, col_keep, "row") + halve(row_send, row_keep, "col")
    with jax.named_scope("product"):
        product, squares = pl.pallas_call(
            product_kernel,
            out_shape=[block, jax.ShapeDtypeStruct((devices, 3, packed_rows, width), jnp.float32)],
            in_specs=[VMEM] * 5,
            out_specs=[VMEM] * 2,
            compiler_params=params,
            name="product",
        )(vectors, *sums)
        squares = swap(squares, ("row", "col"))
    with jax.named_scope("results"):
        residual, rayleigh, gram, sound = pl.pallas_call(
            functools.partial(result_kernel, scale),
            out_shape=[block, square, square, jax.ShapeDtypeStruct((1, 1), jnp.int32)],
            in_specs=[VMEM] * 3,
            out_specs=[VMEM] * 4,
            compiler_params=params,
            name="results",
        )(vectors, product, squares)

    def from_residual(_):
        parts = pl.pallas_call(
            functools.partial(gram_parts_kernel, scale),
            out_shape=jax.ShapeDtypeStruct((devices, packed_rows, width), jnp.float32),
            in_specs=[VMEM] * 3,
            out_specs=VMEM,
            compiler_params=params,
            name="gram_parts",
        )(vectors, product, squares)
        gram = pl.pallas_call(
            functools.partial(gram_kernel, scale),
            out_shape=square,
            in_specs=[VMEM],
            out_specs=VMEM,
            compiler_params=params,
            name="gram_sum",
        )(swap(parts, ("row", "col")))
        return jnp.int32(1), gram

    with jax.named_scope("gram"):
        _, gram = lax.while_loop(lambda state: state[0] == 0, from_residual, (sound[0, 0], gram))
    return (residual, rayleigh, gram)


def solution(mesh):
    return jax.shard_map(
        per_device,
        mesh=mesh,
        in_specs=(
            P(None, ("row", "col")),
            P(("row", "col")),
            P("row", "col", None, None, None),
            P("row", "col", None),
            P("row", "col", None),
            P("row", "col"),
        ),
        out_specs=(P(None, ("row", "col")), P(), P()),
        check_vma=False,
    )
```

```python
import functools

import jax
import jax.numpy as jnp
from jax import lax
from jax.experimental import pallas as pl
from jax.experimental.pallas import tpu as pltpu
from jax.sharding import PartitionSpec as P

HP = lax.Precision.HIGHEST
VMEM = pl.BlockSpec(memory_space=pltpu.VMEM)
SMEM = pl.BlockSpec(memory_space=pltpu.SMEM)


def mult(left, right):
    return lax.dot_general(left, right, (((1,), (0,)), ((), ())), precision=HP, preferred_element_type=jnp.float32)


def mult_last(left, right):
    return lax.dot_general(left, right, (((1,), (1,)), ((), ())), precision=HP, preferred_element_type=jnp.float32)


def swap(blocks, axis):
    return lax.all_to_all(blocks, axis, 0, 0, tiled=True)


def trade(value, axis, flip):
    size = lax.axis_size(axis)
    return lax.ppermute(value, axis, [(p, p ^ flip) for p in range(size)])


def own_lanes(nvec, width):
    row = lax.broadcasted_iota(jnp.int32, (nvec, width), 0)
    lane = lax.broadcasted_iota(jnp.int32, (nvec, width), 1)
    return lane // nvec == row % (width // nvec)


def packed_gram(left, right):
    nvec, width = right.shape
    per = width // nvec
    wide = mult_last(left, jnp.concatenate([right] * per, axis=0))
    mask = own_lanes(nvec, width)
    squares = []
    for first in range(0, left.shape[0], nvec):
        own = jnp.where(mask, wide[first : first + nvec], 0.0)
        squares.append(jnp.sum(own.reshape(nvec // per, per, width), axis=1))
    return squares


def unpack(packed, nvec):
    rows, width = packed[0].shape
    per = width // nvec
    lane = lax.broadcasted_iota(jnp.int32, (width, nvec), 0)
    column = lax.broadcasted_iota(jnp.int32, (width, nvec), 1)
    mask = own_lanes(nvec, width)
    wide = []
    for square in packed:
        spread = jnp.concatenate([jnp.broadcast_to(square[g : g + 1], (per, width)) for g in range(rows)], axis=0)
        wide.append(jnp.where(mask, spread, 0.0))
    fold = (lane % nvec == column).astype(jnp.bfloat16)
    pieces = [jnp.dot(part, fold, preferred_element_type=jnp.float32) for part in split(jnp.concatenate(wide, axis=0))]
    return (pieces[2] + pieces[1]) + pieces[0]


def split(value):
    first = value.astype(jnp.bfloat16)
    rest = value - first.astype(jnp.float32)
    second = rest.astype(jnp.bfloat16)
    return first, second, (rest - second.astype(jnp.float32)).astype(jnp.bfloat16)


def stack_split(value):
    return jnp.concatenate(split(value), axis=0)


def pair_products(stacked, parts, transposed):
    nvec, width = stacked[0].shape[0] // 3, stacked[0].shape[1]
    dims = (((1,), (1 if transposed else 0,)), ((), ()))
    axis = 0 if transposed else 1

    def wide(left, pieces):
        return lax.dot_general(left, jnp.concatenate(pieces, axis=axis), dims, preferred_element_type=jnp.float32)

    last = wide(jnp.concatenate([value[:nvec] for value in stacked], axis=0), [part[2] for part in parts])
    results = []
    for which, (value, part) in enumerate(zip(stacked, parts)):
        both = wide(value, part[:2])
        first, second = both[:, :width], both[:, width:]
        total = last[which * nvec : (which + 1) * nvec, which * width : (which + 1) * width]
        total = (total + second[nvec : 2 * nvec]) + first[2 * nvec :]
        total = (total + second[:nvec]) + first[nvec : 2 * nvec]
        results.append(total + first[:nvec])
    return results


def join_kernel(mine, other, *refs):
    out = refs[-1]
    half = mine.shape[0]
    out[:half] = mine[...]
    out[half:] = other[...]


def prepare_kernel(slots, tiles, *refs):
    small, parts, copies = refs[:3], refs[3:6], refs[6:]
    for array, copy in zip(small, copies):
        copy[...] = array[...]
    for slot in range(slots):
        for part, piece in zip(parts, split(tiles[0, 0, slot])):
            part[slot] = piece


def part_blocks(sums, total, send, keep):
    for block in range(total // 2):
        keep[block] = sums[2 * block]
        send[block] = sums[2 * block + 1]


def column_kernel(n_row, n_col, slots, place, arow, bcol, count, d_ref, near, far, *refs):
    *parts, _, send, keep, rows, sums = refs
    me_row, me_col = place[0], place[1]
    half = n_col // 2
    for flip in range(n_col):
        rows[flip] = stack_split(near[flip] if flip < half else far[flip - half])
    sums[...] = jnp.zeros_like(sums)
    sums[0] = d_ref[...] * near[0]
    for pair in range(0, slots, 2):
        pieces = [[part[slot] for part in parts] for slot in (pair, pair + 1)]
        values = [rows[arow[0, 0, slot] ^ me_col] for slot in (pair, pair + 1)]
        for slot, terms in zip((pair, pair + 1), pair_products(values, pieces, False)):
            block = jnp.where(slot < count[0, 0], bcol[0, 0, slot] ^ me_row, n_row)
            sums[block] += terms
    part_blocks(sums, n_row, send, keep)


def row_kernel(n_row, n_col, slots, place, arow, bcol, count, *refs):
    x_pairs, (*parts, send, keep, cols, sums) = refs[: n_row // 2], refs[n_row // 2 :]
    me_row, me_col = place[0], place[1]
    for flip in range(n_row):
        cols[flip] = stack_split(x_pairs[flip // 2][flip % 2])
    sums[...] = jnp.zeros_like(sums)
    for pair in range(0, slots, 2):
        pieces = [[part[slot] for part in parts] for slot in (pair, pair + 1)]
        values = [cols[bcol[0, 0, slot] ^ me_row] for slot in (pair, pair + 1)]
        for slot, terms in zip((pair, pair + 1), pair_products(values, pieces, True)):
            block = jnp.where(slot < count[0, 0], arow[0, 0, slot] ^ me_col, n_col)
            sums[block] += terms
    part_blocks(sums, n_col, send, keep)


def halve_kernel(mine, other, send, keep):
    part_blocks([mine[block] + other[block] for block in range(mine.shape[0])], mine.shape[0], send, keep)


def chip_kernel(mine, other, *outs):
    for chip, out in enumerate(outs):
        out[0] = mine[chip] + other[chip]


def product_kernel(x_ref, *refs):
    parts, (product, out) = refs[:-2], refs[-2:]
    own = x_ref[...]
    total = parts[0][0]
    for part in parts[1:]:
        total += part[0]
    product[...] = total
    squares = packed_gram(jnp.concatenate([own, total], axis=0), total) + packed_gram(own, own)
    for block in range(out.shape[0]):
        for which, square in enumerate(squares):
            out[block, which] = square


def summed_squares(scale, parts, nvec):
    sums = jnp.sum(parts[...], axis=0)
    squares = unpack([sums[which] for which in range(3)], nvec) * scale
    return squares[:nvec], squares[nvec : 2 * nvec], squares[2 * nvec :]


def result_kernel(scale, x_ref, product, parts, residual, rayleigh, gram, sound):
    own = x_ref[...]
    nvec = own.shape[0]
    ray, outer, inner = summed_squares(scale, parts, nvec)
    rayleigh[...] = ray
    residual[...] = product[...] - mult(ray, own)
    twice = mult(ray, ray)
    lifted = mult_last(mult(ray, inner), ray)
    result = outer - (twice + twice.T) + lifted
    gram[...] = result
    diagonal = lax.broadcasted_iota(jnp.int32, (nvec, nvec), 0) == lax.broadcasted_iota(jnp.int32, (nvec, nvec), 1)
    margin = jnp.sum(jnp.where(diagonal, 64.0 * result - (outer + lifted), 0.0), keepdims=True)
    sound[...] = (margin >= 0.0).astype(jnp.int32)


def gram_parts_kernel(scale, x_ref, product, parts, out):
    own = x_ref[...]
    ray, _, _ = summed_squares(scale, parts, own.shape[0])
    residual = product[...] - mult(ray, own)
    square = packed_gram(residual, residual)[0]
    for block in range(out.shape[0]):
        out[block] = square


def gram_kernel(scale, parts, out):
    out[...] = unpack([jnp.sum(parts[...], axis=0)], out.shape[0]) * scale


def per_device(vectors, diagonal_energy, tiles, tile_rows, tile_cols, tile_count):
    n_row = lax.axis_size("row")
    n_col = lax.axis_size("col")
    devices = n_row * n_col
    nvec, width = vectors.shape
    slots = tiles.shape[2]
    scale = 1.0 / float(devices * width)
    packed_rows = nvec * nvec // width
    block = jax.ShapeDtypeStruct((nvec, width), jnp.float32)
    square = jax.ShapeDtypeStruct((nvec, nvec), jnp.float32)
    part = jax.ShapeDtypeStruct((slots, width, width), jnp.bfloat16)
    place = jnp.stack([lax.axis_index("row"), lax.axis_index("col")]).astype(jnp.int32)
    energy = diagonal_energy.reshape(1, width)
    params = pltpu.CompilerParams(vmem_limit_bytes=16 * 2**20)
    cost = pl.CostEstimate(flops=12 * slots * nvec * width * width, bytes_accessed=2**20, transcendentals=0)

    def blocks(total):
        return jax.ShapeDtypeStruct((total, nvec, width), jnp.float32)

    def trades(value, axis, flips):
        return [trade(value, axis, flip) for flip in reversed(flips)][::-1]

    def halve(send, keep, axis):
        flip = 1
        while keep.shape[0] > 1:
            half = keep.shape[0] // 2
            send, keep = pl.pallas_call(
                halve_kernel,
                out_shape=[blocks(half)] * 2,
                in_specs=[VMEM] * 2,
                out_specs=[VMEM] * 2,
                compiler_params=params,
                name="halve_" + axis,
            )(keep, trade(send, axis, flip))
            flip *= 2
        return keep, trade(send, axis, flip)

    with jax.named_scope("prepare"):
        small = (tile_rows, tile_cols, energy)
        *parts, arow, bcol, energy = pl.pallas_call(
            functools.partial(prepare_kernel, slots),
            out_shape=[part] * 3 + [jax.ShapeDtypeStruct(array.shape, array.dtype) for array in small],
            in_specs=[VMEM] * 4,
            out_specs=[VMEM] * 6,
            compiler_params=params,
            cost_estimate=pl.CostEstimate(flops=0, bytes_accessed=5 * slots * width * width, transcendentals=0),
            name="prepare",
        )(tiles, *small)
    def join(mine, other, *after):
        return pl.pallas_call(
            join_kernel,
            out_shape=blocks(2 * mine.shape[0]),
            in_specs=[VMEM] * 2 + [pl.BlockSpec(memory_space=pl.ANY)] * len(after),
            out_specs=VMEM,
            compiler_params=params,
            name="join",
        )(mine, other, *after)

    with jax.named_scope("share_vectors"):
        own = vectors[None]
        other = trade(own, "row", 1)
        near, far = own, trade(own, "col", 1)
        pair = join(own, other, parts[0])
        x_pairs = [pair] + trades(pair, "row", range(2, n_row, 2))
        reach = 2
        while reach < n_col:
            near = join(near, far)
            far = trade(near, "col", reach)
            reach *= 2
    with jax.named_scope("row_terms"):
        row_send, row_keep = pl.pallas_call(
            functools.partial(row_kernel, n_row, n_col, slots),
            out_shape=[blocks(n_col // 2)] * 2,
            in_specs=[SMEM] * 4 + [VMEM] * (n_row // 2 + 3),
            out_specs=[VMEM] * 2,
            scratch_shapes=[
                pltpu.VMEM((n_row, 3 * nvec, width), jnp.bfloat16),
                pltpu.VMEM((n_col + 1, nvec, width), jnp.float32),
            ],
            compiler_params=params,
            cost_estimate=cost,
            name="row_terms",
        )(place, arow, bcol, tile_count, *x_pairs, *parts)
    with jax.named_scope("column_terms"):
        col_send, col_keep = pl.pallas_call(
            functools.partial(column_kernel, n_row, n_col, slots),
            out_shape=[blocks(n_row // 2)] * 2,
            in_specs=[SMEM] * 4 + [VMEM] * 6 + [pl.BlockSpec(memory_space=pl.ANY)],
            out_specs=[VMEM] * 2,
            scratch_shapes=[
                pltpu.VMEM((n_col, 3 * nvec, width), jnp.bfloat16),
                pltpu.VMEM((n_row + 1, nvec, width), jnp.float32),
            ],
            compiler_params=params,
            cost_estimate=cost,
            name="column_terms",
        )(place, arow, bcol, tile_count, energy, near, far, *parts, row_send)
    with jax.named_scope("return_products"):
        sums = halve(row_send, row_keep, "col")
        chips = pl.pallas_call(
            chip_kernel,
            out_shape=[blocks(1)] * (n_row // 2),
            in_specs=[VMEM] * 2,
            out_specs=[VMEM] * (n_row // 2),
            compiler_params=params,
            name="chip_sum",
        )(col_keep, trade(col_send, "row", 1))
        sums += (chips[0], *[trade(chips[chip], "row", 2 * chip) for chip in range(1, n_row // 2)])
    with jax.named_scope("product"):
        product, squares = pl.pallas_call(
            product_kernel,
            out_shape=[block, jax.ShapeDtypeStruct((devices, 3, packed_rows, width), jnp.float32)],
            in_specs=[VMEM] * (1 + len(sums)),
            out_specs=[VMEM] * 2,
            compiler_params=params,
            name="product",
        )(vectors, *sums)
        squares = swap(squares, ("row", "col"))
    with jax.named_scope("results"):
        residual, rayleigh, gram, sound = pl.pallas_call(
            functools.partial(result_kernel, scale),
            out_shape=[block, square, square, jax.ShapeDtypeStruct((1, 1), jnp.int32)],
            in_specs=[VMEM] * 3,
            out_specs=[VMEM] * 4,
            compiler_params=params,
            name="results",
        )(vectors, product, squares)

    def from_residual(_):
        parts = pl.pallas_call(
            functools.partial(gram_parts_kernel, scale),
            out_shape=jax.ShapeDtypeStruct((devices, packed_rows, width), jnp.float32),
            in_specs=[VMEM] * 3,
            out_specs=VMEM,
            compiler_params=params,
            name="gram_parts",
        )(vectors, product, squares)
        gram = pl.pallas_call(
            functools.partial(gram_kernel, scale),
            out_shape=square,
            in_specs=[VMEM],
            out_specs=VMEM,
            compiler_params=params,
            name="gram_sum",
        )(swap(parts, ("row", "col")))
        return jnp.int32(1), gram

    with jax.named_scope("gram"):
        _, gram = lax.while_loop(lambda state: state[0] == 0, from_residual, (sound[0, 0], gram))
    return (residual, rayleigh, gram)


def solution(mesh):
    return jax.shard_map(
        per_device,
        mesh=mesh,
        in_specs=(
            P(None, ("row", "col")),
            P(("row", "col")),
            P("row", "col", None, None, None),
            P("row", "col", None),
            P("row", "col", None),
            P("row", "col"),
        ),
        out_specs=(P(None, ("row", "col")), P(), P()),
        check_vma=False,
    )
```

```python
import functools

import jax
import jax.numpy as jnp
from jax import lax
from jax.experimental import pallas as pl
from jax.experimental.pallas import tpu as pltpu
from jax.sharding import PartitionSpec as P

HP = lax.Precision.HIGHEST
VMEM = pl.BlockSpec(memory_space=pltpu.VMEM)
SMEM = pl.BlockSpec(memory_space=pltpu.SMEM)


def mult(left, right):
    return lax.dot_general(left, right, (((1,), (0,)), ((), ())), precision=HP, preferred_element_type=jnp.float32)


def mult_last(left, right):
    return lax.dot_general(left, right, (((1,), (1,)), ((), ())), precision=HP, preferred_element_type=jnp.float32)


def swap(blocks, axis):
    return lax.all_to_all(blocks, axis, 0, 0, tiled=True)


def trade(value, axis, flip):
    size = lax.axis_size(axis)
    return lax.ppermute(value, axis, [(p, p ^ flip) for p in range(size)])


def own_lanes(nvec, width):
    row = lax.broadcasted_iota(jnp.int32, (nvec, width), 0)
    lane = lax.broadcasted_iota(jnp.int32, (nvec, width), 1)
    return lane // nvec == row % (width // nvec)


def packed_gram(left, right):
    nvec, width = right.shape
    per = width // nvec
    wide = mult_last(left, jnp.concatenate([right] * per, axis=0))
    mask = own_lanes(nvec, width)
    squares = []
    for first in range(0, left.shape[0], nvec):
        own = jnp.where(mask, wide[first : first + nvec], 0.0)
        squares.append(jnp.sum(own.reshape(nvec // per, per, width), axis=1))
    return squares


def unpack(packed, nvec):
    rows, width = packed[0].shape
    per = width // nvec
    lane = lax.broadcasted_iota(jnp.int32, (width, nvec), 0)
    column = lax.broadcasted_iota(jnp.int32, (width, nvec), 1)
    mask = own_lanes(nvec, width)
    wide = []
    for square in packed:
        spread = jnp.concatenate([jnp.broadcast_to(square[g : g + 1], (per, width)) for g in range(rows)], axis=0)
        wide.append(jnp.where(mask, spread, 0.0))
    fold = (lane % nvec == column).astype(jnp.bfloat16)
    pieces = [jnp.dot(part, fold, preferred_element_type=jnp.float32) for part in split(jnp.concatenate(wide, axis=0))]
    return (pieces[2] + pieces[1]) + pieces[0]


def split(value):
    first = value.astype(jnp.bfloat16)
    rest = value - first.astype(jnp.float32)
    second = rest.astype(jnp.bfloat16)
    return first, second, (rest - second.astype(jnp.float32)).astype(jnp.bfloat16)


def stack_split(value):
    return jnp.concatenate(split(value), axis=0)


def pair_products(stacked, parts, transposed):
    nvec, width = stacked[0].shape[0] // 3, stacked[0].shape[1]
    dims = (((1,), (1 if transposed else 0,)), ((), ()))
    axis = 0 if transposed else 1

    def wide(left, pieces):
        return lax.dot_general(left, jnp.concatenate(pieces, axis=axis), dims, preferred_element_type=jnp.float32)

    last = wide(jnp.concatenate([value[:nvec] for value in stacked], axis=0), [part[2] for part in parts])
    results = []
    for which, (value, part) in enumerate(zip(stacked, parts)):
        both = wide(value, part[:2])
        first, second = both[:, :width], both[:, width:]
        total = last[which * nvec : (which + 1) * nvec, which * width : (which + 1) * width]
        total = (total + second[nvec : 2 * nvec]) + first[2 * nvec :]
        total = (total + second[:nvec]) + first[nvec : 2 * nvec]
        results.append(total + first[:nvec])
    return results


def join_kernel(mine, other, *refs):
    out = refs[-1]
    half = mine.shape[0]
    out[:half] = mine[...]
    out[half:] = other[...]


def prepare_kernel(slots, tiles, *refs):
    small, parts, copies = refs[:3], refs[3:6], refs[6:]
    for array, copy in zip(small, copies):
        copy[...] = array[...]
    for slot in range(slots):
        for part, piece in zip(parts, split(tiles[0, 0, slot])):
            part[slot] = piece


def part_blocks(sums, total, send, keep):
    for block in range(total // 2):
        keep[block] = sums[2 * block]
        send[block] = sums[2 * block + 1]


def column_kernel(n_row, n_col, slots, place, arow, bcol, count, d_ref, near, far, *refs):
    *parts, send, keep, rows, sums = refs
    me_row, me_col = place[0], place[1]
    half = n_col // 2
    for flip in range(n_col):
        rows[flip] = stack_split(near[flip] if flip < half else far[flip - half])
    sums[...] = jnp.zeros_like(sums)
    sums[0] = d_ref[...] * near[0]
    for pair in range(0, slots, 2):
        pieces = [[part[slot] for part in parts] for slot in (pair, pair + 1)]
        values = [rows[arow[0, 0, slot] ^ me_col] for slot in (pair, pair + 1)]
        for slot, terms in zip((pair, pair + 1), pair_products(values, pieces, False)):
            block = jnp.where(slot < count[0, 0], bcol[0, 0, slot] ^ me_row, n_row)
            sums[block] += terms
    part_blocks(sums, n_row, send, keep)


def hand_on_kernel(early, after, late):
    del after
    late[...] = early[...]


def row_kernel(n_row, n_col, slots, place, arow, bcol, count, near, far, *refs):
    *parts, send, keep, cols, sums = refs
    me_row, me_col = place[0], place[1]
    half = n_row // 2
    for flip in range(n_row):
        cols[flip] = stack_split(near[flip] if flip < half else far[flip - half])
    sums[...] = jnp.zeros_like(sums)
    for pair in range(0, slots, 2):
        pieces = [[part[slot] for part in parts] for slot in (pair, pair + 1)]
        values = [cols[bcol[0, 0, slot] ^ me_row] for slot in (pair, pair + 1)]
        for slot, terms in zip((pair, pair + 1), pair_products(values, pieces, True)):
            block = jnp.where(slot < count[0, 0], arow[0, 0, slot] ^ me_col, n_col)
            sums[block] += terms
    part_blocks(sums, n_col, send, keep)


def halve_kernel(mine, other, send, keep):
    part_blocks([mine[block] + other[block] for block in range(mine.shape[0])], mine.shape[0], send, keep)


def product_kernel(x_ref, *refs):
    parts, (product, out) = refs[:-2], refs[-2:]
    own = x_ref[...]
    total = parts[0][0]
    for part in parts[1:]:
        total += part[0]
    product[...] = total
    squares = packed_gram(jnp.concatenate([own, total], axis=0), total) + packed_gram(own, own)
    for block in range(out.shape[0]):
        for which, square in enumerate(squares):
            out[block, which] = square


def summed_squares(scale, parts, nvec):
    sums = jnp.sum(parts[...], axis=0)
    squares = unpack([sums[which] for which in range(3)], nvec) * scale
    return squares[:nvec], squares[nvec : 2 * nvec], squares[2 * nvec :]


def result_kernel(scale, x_ref, product, parts, residual, rayleigh, gram, sound):
    own = x_ref[...]
    nvec = own.shape[0]
    ray, outer, inner = summed_squares(scale, parts, nvec)
    rayleigh[...] = ray
    residual[...] = product[...] - mult(ray, own)
    twice = mult(ray, ray)
    lifted = mult_last(mult(ray, inner), ray)
    result = outer - (twice + twice.T) + lifted
    gram[...] = result
    diagonal = lax.broadcasted_iota(jnp.int32, (nvec, nvec), 0) == lax.broadcasted_iota(jnp.int32, (nvec, nvec), 1)
    margin = jnp.sum(jnp.where(diagonal, 64.0 * result - (outer + lifted), 0.0), keepdims=True)
    sound[...] = (margin >= 0.0).astype(jnp.int32)


def gram_parts_kernel(scale, x_ref, product, parts, out):
    own = x_ref[...]
    ray, _, _ = summed_squares(scale, parts, own.shape[0])
    residual = product[...] - mult(ray, own)
    square = packed_gram(residual, residual)[0]
    for block in range(out.shape[0]):
        out[block] = square


def gram_kernel(scale, parts, out):
    out[...] = unpack([jnp.sum(parts[...], axis=0)], out.shape[0]) * scale


def per_device(vectors, diagonal_energy, tiles, tile_rows, tile_cols, tile_count):
    n_row = lax.axis_size("row")
    n_col = lax.axis_size("col")
    devices = n_row * n_col
    nvec, width = vectors.shape
    slots = tiles.shape[2]
    scale = 1.0 / float(devices * width)
    packed_rows = nvec * nvec // width
    block = jax.ShapeDtypeStruct((nvec, width), jnp.float32)
    square = jax.ShapeDtypeStruct((nvec, nvec), jnp.float32)
    part = jax.ShapeDtypeStruct((slots, width, width), jnp.bfloat16)
    place = jnp.stack([lax.axis_index("row"), lax.axis_index("col")]).astype(jnp.int32)
    energy = diagonal_energy.reshape(1, width)
    params = pltpu.CompilerParams(vmem_limit_bytes=16 * 2**20)
    cost = pl.CostEstimate(flops=12 * slots * nvec * width * width, bytes_accessed=2**20, transcendentals=0)

    def blocks(total):
        return jax.ShapeDtypeStruct((total, nvec, width), jnp.float32)

    def gather(axis, *after):
        near = vectors[None]
        far = trade(near, axis, 1)
        reach = 2
        while reach < lax.axis_size(axis):
            near = pl.pallas_call(
                join_kernel,
                out_shape=blocks(reach),
                in_specs=[VMEM] * 2 + [pl.BlockSpec(memory_space=pl.ANY)] * len(after),
                out_specs=VMEM,
                compiler_params=params,
                name="join_" + axis,
            )(near, far, *after)
            far = trade(near, axis, reach)
            reach *= 2
            after = ()
        return near, far

    def halve(send, keep, axis):
        flip = 1
        while keep.shape[0] > 1:
            half = keep.shape[0] // 2
            send, keep = pl.pallas_call(
                halve_kernel,
                out_shape=[blocks(half)] * 2,
                in_specs=[VMEM] * 2,
                out_specs=[VMEM] * 2,
                compiler_params=params,
                name="halve_" + axis,
            )(keep, trade(send, axis, flip))
            flip *= 2
        return keep, trade(send, axis, flip)

    with jax.named_scope("prepare"):
        small = (tile_rows, tile_cols, energy)
        *parts, arow, bcol, energy = pl.pallas_call(
            functools.partial(prepare_kernel, slots),
            out_shape=[part] * 3 + [jax.ShapeDtypeStruct(array.shape, array.dtype) for array in small],
            in_specs=[VMEM] * 4,
            out_specs=[VMEM] * 6,
            compiler_params=params,
            cost_estimate=pl.CostEstimate(flops=0, bytes_accessed=5 * slots * width * width, transcendentals=0),
            name="prepare",
        )(tiles, *small)
    with jax.named_scope("share_vectors"):
        x_row = gather("row", parts[0])
        x_col = gather("col")
    with jax.named_scope("column_terms"):
        col_send, col_keep = pl.pallas_call(
            functools.partial(column_kernel, n_row, n_col, slots),
            out_shape=[blocks(n_row // 2)] * 2,
            in_specs=[SMEM] * 4 + [VMEM] * 6,
            out_specs=[VMEM] * 2,
            scratch_shapes=[
                pltpu.VMEM((n_col, 3 * nvec, width), jnp.bfloat16),
                pltpu.VMEM((n_row + 1, nvec, width), jnp.float32),
            ],
            compiler_params=params,
            cost_estimate=cost,
            name="column_terms",
        )(place, arow, bcol, tile_count, energy, *x_col, *parts)
        col_send = pl.pallas_call(
            hand_on_kernel,
            out_shape=blocks(n_row // 2),
            in_specs=[VMEM, pl.BlockSpec(memory_space=pl.ANY)],
            out_specs=VMEM,
            compiler_params=params,
            name="hand_on",
        )(col_send, x_row[1])
    with jax.named_scope("row_terms"):
        row_send, row_keep = pl.pallas_call(
            functools.partial(row_kernel, n_row, n_col, slots),
            out_shape=[blocks(n_col // 2)] * 2,
            in_specs=[SMEM] * 4 + [VMEM] * 5,
            out_specs=[VMEM] * 2,
            scratch_shapes=[
                pltpu.VMEM((n_row, 3 * nvec, width), jnp.bfloat16),
                pltpu.VMEM((n_col + 1, nvec, width), jnp.float32),
            ],
            compiler_params=params,
            cost_estimate=cost,
            name="row_terms",
        )(place, arow, bcol, tile_count, *x_row, *parts)
    with jax.named_scope("return_products"):
        sums = halve(col_send, col_keep, "row") + halve(row_send, row_keep, "col")
    with jax.named_scope("product"):
        product, squares = pl.pallas_call(
            product_kernel,
            out_shape=[block, jax.ShapeDtypeStruct((devices, 3, packed_rows, width), jnp.float32)],
            in_specs=[VMEM] * 5,
            out_specs=[VMEM] * 2,
            compiler_params=params,
            name="product",
        )(vectors, *sums)
        squares = swap(squares, ("row", "col"))
    with jax.named_scope("results"):
        residual, rayleigh, gram, sound = pl.pallas_call(
            functools.partial(result_kernel, scale),
            out_shape=[block, square, square, jax.ShapeDtypeStruct((1, 1), jnp.int32)],
            in_specs=[VMEM] * 3,
            out_specs=[VMEM] * 4,
            compiler_params=params,
            name="results",
        )(vectors, product, squares)

    def from_residual(_):
        parts = pl.pallas_call(
            functools.partial(gram_parts_kernel, scale),
            out_shape=jax.ShapeDtypeStruct((devices, packed_rows, width), jnp.float32),
            in_specs=[VMEM] * 3,
            out_specs=VMEM,
            compiler_params=params,
            name="gram_parts",
        )(vectors, product, squares)
        gram = pl.pallas_call(
            functools.partial(gram_kernel, scale),
            out_shape=square,
            in_specs=[VMEM],
            out_specs=VMEM,
            compiler_params=params,
            name="gram_sum",
        )(swap(parts, ("row", "col")))
        return jnp.int32(1), gram

    with jax.named_scope("gram"):
        _, gram = lax.while_loop(lambda state: state[0] == 0, from_residual, (sound[0, 0], gram))
    return (residual, rayleigh, gram)


def solution(mesh):
    return jax.shard_map(
        per_device,
        mesh=mesh,
        in_specs=(
            P(None, ("row", "col")),
            P(("row", "col")),
            P("row", "col", None, None, None),
            P("row", "col", None),
            P("row", "col", None),
            P("row", "col"),
        ),
        out_specs=(P(None, ("row", "col")), P(), P()),
        check_vma=False,
    )
```

```python
import functools

import jax
import jax.numpy as jnp
from jax import lax
from jax.experimental import pallas as pl
from jax.experimental.pallas import tpu as pltpu
from jax.sharding import PartitionSpec as P

HP = lax.Precision.HIGHEST
VMEM = pl.BlockSpec(memory_space=pltpu.VMEM)
SMEM = pl.BlockSpec(memory_space=pltpu.SMEM)


def mult(left, right):
    return lax.dot_general(left, right, (((1,), (0,)), ((), ())), precision=HP, preferred_element_type=jnp.float32)


def mult_last(left, right):
    return lax.dot_general(left, right, (((1,), (1,)), ((), ())), precision=HP, preferred_element_type=jnp.float32)


def swap(blocks, axis):
    return lax.all_to_all(blocks, axis, 0, 0, tiled=True)


def trade(value, axis, flip):
    size = lax.axis_size(axis)
    return lax.ppermute(value, axis, [(p, p ^ flip) for p in range(size)])


def own_lanes(nvec, width):
    row = lax.broadcasted_iota(jnp.int32, (nvec, width), 0)
    lane = lax.broadcasted_iota(jnp.int32, (nvec, width), 1)
    return lane // nvec == row % (width // nvec)


def packed_gram(left, right):
    nvec, width = right.shape
    per = width // nvec
    wide = mult_last(left, jnp.concatenate([right] * per, axis=0))
    mask = own_lanes(nvec, width)
    squares = []
    for first in range(0, left.shape[0], nvec):
        own = jnp.where(mask, wide[first : first + nvec], 0.0)
        squares.append(jnp.sum(own.reshape(nvec // per, per, width), axis=1))
    return squares


def unpack(packed, nvec):
    rows, width = packed[0].shape
    per = width // nvec
    lane = lax.broadcasted_iota(jnp.int32, (width, nvec), 0)
    column = lax.broadcasted_iota(jnp.int32, (width, nvec), 1)
    mask = own_lanes(nvec, width)
    wide = []
    for square in packed:
        spread = jnp.concatenate([jnp.broadcast_to(square[g : g + 1], (per, width)) for g in range(rows)], axis=0)
        wide.append(jnp.where(mask, spread, 0.0))
    fold = (lane % nvec == column).astype(jnp.bfloat16)
    pieces = [jnp.dot(part, fold, preferred_element_type=jnp.float32) for part in split(jnp.concatenate(wide, axis=0))]
    return (pieces[2] + pieces[1]) + pieces[0]


def split(value):
    first = value.astype(jnp.bfloat16)
    rest = value - first.astype(jnp.float32)
    second = rest.astype(jnp.bfloat16)
    return first, second, (rest - second.astype(jnp.float32)).astype(jnp.bfloat16)


def stack_split(value):
    return jnp.concatenate(split(value), axis=0)


def pair_products(stacked, parts, transposed):
    nvec, width = stacked[0].shape[0] // 3, stacked[0].shape[1]
    dims = (((1,), (1 if transposed else 0,)), ((), ()))
    axis = 0 if transposed else 1

    def wide(left, pieces):
        return lax.dot_general(left, jnp.concatenate(pieces, axis=axis), dims, preferred_element_type=jnp.float32)

    last = wide(jnp.concatenate([value[:nvec] for value in stacked], axis=0), [part[2] for part in parts])
    results = []
    for which, (value, part) in enumerate(zip(stacked, parts)):
        both = wide(value, part[:2])
        first, second = both[:, :width], both[:, width:]
        total = last[which * nvec : (which + 1) * nvec, which * width : (which + 1) * width]
        total = (total + second[nvec : 2 * nvec]) + first[2 * nvec :]
        total = (total + second[:nvec]) + first[nvec : 2 * nvec]
        results.append(total + first[:nvec])
    return results


def join_kernel(axes, *refs):
    for which, out in enumerate(refs[-axes:]):
        mine, other = refs[2 * which : 2 * which + 2]
        half = mine.shape[0]
        out[:half] = mine[...]
        out[half:] = other[...]


def prepare_kernel(slots, tiles, *refs):
    small, parts, copies = refs[:3], refs[3:6], refs[6:]
    for array, copy in zip(small, copies):
        copy[...] = array[...]
    for slot in range(slots):
        for part, piece in zip(parts, split(tiles[0, 0, slot])):
            part[slot] = piece


def part_blocks(sums, total, send, keep):
    for block in range(total // 2):
        keep[block] = sums[2 * block]
        send[block] = sums[2 * block + 1]


def column_kernel(n_row, n_col, slots, place, arow, bcol, count, d_ref, near, far, *refs):
    *parts, send, keep, rows, sums = refs
    me_row, me_col = place[0], place[1]
    half = n_col // 2
    for flip in range(n_col):
        rows[flip] = stack_split(near[flip] if flip < half else far[flip - half])
    sums[...] = jnp.zeros_like(sums)
    sums[0] = d_ref[...] * near[0]
    for pair in range(0, slots, 2):
        pieces = [[part[slot] for part in parts] for slot in (pair, pair + 1)]
        values = [rows[arow[0, 0, slot] ^ me_col] for slot in (pair, pair + 1)]
        for slot, terms in zip((pair, pair + 1), pair_products(values, pieces, False)):
            block = jnp.where(slot < count[0, 0], bcol[0, 0, slot] ^ me_row, n_row)
            sums[block] += terms
    part_blocks(sums, n_row, send, keep)


def hand_on_kernel(early, after, late):
    del after
    late[...] = early[...]


def row_kernel(n_row, n_col, slots, place, arow, bcol, count, near, far, *refs):
    *parts, send, keep, cols, sums = refs
    me_row, me_col = place[0], place[1]
    for pair in range(n_row // 2):
        cols[2 * pair] = stack_split(near[pair])
        cols[2 * pair + 1] = stack_split(far[pair])
    sums[...] = jnp.zeros_like(sums)
    for pair in range(0, slots, 2):
        pieces = [[part[slot] for part in parts] for slot in (pair, pair + 1)]
        values = [cols[bcol[0, 0, slot] ^ me_row] for slot in (pair, pair + 1)]
        for slot, terms in zip((pair, pair + 1), pair_products(values, pieces, True)):
            block = jnp.where(slot < count[0, 0], arow[0, 0, slot] ^ me_col, n_col)
            sums[block] += terms
    part_blocks(sums, n_col, send, keep)


def halve_kernel(mine, other, send, keep):
    part_blocks([mine[block] + other[block] for block in range(mine.shape[0])], mine.shape[0], send, keep)


def product_kernel(x_ref, *refs):
    parts, (product, out) = refs[:-2], refs[-2:]
    own = x_ref[...]
    total = parts[0][0]
    for part in parts[1:]:
        total += part[0]
    product[...] = total
    squares = packed_gram(jnp.concatenate([own, total], axis=0), total) + packed_gram(own, own)
    for block in range(out.shape[0]):
        for which, square in enumerate(squares):
            out[block, which] = square


def summed_squares(scale, parts, nvec):
    sums = jnp.sum(parts[...], axis=0)
    squares = unpack([sums[which] for which in range(3)], nvec) * scale
    return squares[:nvec], squares[nvec : 2 * nvec], squares[2 * nvec :]


def result_kernel(scale, x_ref, product, parts, residual, rayleigh, gram, sound):
    own = x_ref[...]
    nvec = own.shape[0]
    ray, outer, inner = summed_squares(scale, parts, nvec)
    rayleigh[...] = ray
    residual[...] = product[...] - mult(ray, own)
    twice = mult(ray, ray)
    lifted = mult_last(mult(ray, inner), ray)
    result = outer - (twice + twice.T) + lifted
    gram[...] = result
    diagonal = lax.broadcasted_iota(jnp.int32, (nvec, nvec), 0) == lax.broadcasted_iota(jnp.int32, (nvec, nvec), 1)
    margin = jnp.sum(jnp.where(diagonal, 64.0 * result - (outer + lifted), 0.0), keepdims=True)
    sound[...] = (margin >= 0.0).astype(jnp.int32)


def gram_parts_kernel(scale, x_ref, product, parts, out):
    own = x_ref[...]
    ray, _, _ = summed_squares(scale, parts, own.shape[0])
    residual = product[...] - mult(ray, own)
    square = packed_gram(residual, residual)[0]
    for block in range(out.shape[0]):
        out[block] = square


def gram_kernel(scale, parts, out):
    out[...] = unpack([jnp.sum(parts[...], axis=0)], out.shape[0]) * scale


def per_device(vectors, diagonal_energy, tiles, tile_rows, tile_cols, tile_count):
    n_row = lax.axis_size("row")
    n_col = lax.axis_size("col")
    devices = n_row * n_col
    nvec, width = vectors.shape
    slots = tiles.shape[2]
    scale = 1.0 / float(devices * width)
    packed_rows = nvec * nvec // width
    block = jax.ShapeDtypeStruct((nvec, width), jnp.float32)
    square = jax.ShapeDtypeStruct((nvec, nvec), jnp.float32)
    part = jax.ShapeDtypeStruct((slots, width, width), jnp.bfloat16)
    place = jnp.stack([lax.axis_index("row"), lax.axis_index("col")]).astype(jnp.int32)
    energy = diagonal_energy.reshape(1, width)
    params = pltpu.CompilerParams(vmem_limit_bytes=16 * 2**20)
    cost = pl.CostEstimate(flops=12 * slots * nvec * width * width, bytes_accessed=2**20, transcendentals=0)

    def blocks(total):
        return jax.ShapeDtypeStruct((total, nvec, width), jnp.float32)

    def gather(after, **flips):
        axes = list(flips)
        near = [vectors[None]] * len(axes)
        far = [trade(vectors[None], axis, flips[axis][0]) for axis in axes]
        step = 1
        while any(step < len(flips[axis]) for axis in axes):
            going = [which for which, axis in enumerate(axes) if step < len(flips[axis])]
            joined = pl.pallas_call(
                functools.partial(join_kernel, len(going)),
                out_shape=[blocks(2**step)] * len(going),
                in_specs=[VMEM] * (2 * len(going)) + [pl.BlockSpec(memory_space=pl.ANY)] * len(after),
                out_specs=[VMEM] * len(going),
                compiler_params=params,
                name="join",
            )(*[half for which in going for half in (near[which], far[which])], *after)
            for which, half in zip(going, joined):
                near[which], far[which] = half, trade(half, axes[which], flips[axes[which]][step])
            step += 1
            after = ()
        return list(zip(near, far))

    def halve(send, keep, axis):
        flip = 1
        while keep.shape[0] > 1:
            half = keep.shape[0] // 2
            send, keep = pl.pallas_call(
                halve_kernel,
                out_shape=[blocks(half)] * 2,
                in_specs=[VMEM] * 2,
                out_specs=[VMEM] * 2,
                compiler_params=params,
                name="halve_" + axis,
            )(keep, trade(send, axis, flip))
            flip *= 2
        return keep, trade(send, axis, flip)

    with jax.named_scope("prepare"):
        small = (tile_rows, tile_cols, energy)
        *parts, arow, bcol, energy = pl.pallas_call(
            functools.partial(prepare_kernel, slots),
            out_shape=[part] * 3 + [jax.ShapeDtypeStruct(array.shape, array.dtype) for array in small],
            in_specs=[VMEM] * 4,
            out_specs=[VMEM] * 6,
            compiler_params=params,
            cost_estimate=pl.CostEstimate(flops=0, bytes_accessed=5 * slots * width * width, transcendentals=0),
            name="prepare",
        )(tiles, *small)
    with jax.named_scope("share_vectors"):
        bits = [1 << bit for bit in range(n_row.bit_length() - 1)]
        x_row, x_col = gather(parts[:1], row=bits[1:] + bits[:1], col=[1 << bit for bit in range(n_col.bit_length() - 1)])
    with jax.named_scope("column_terms"):
        col_send, col_keep = pl.pallas_call(
            functools.partial(column_kernel, n_row, n_col, slots),
            out_shape=[blocks(n_row // 2)] * 2,
            in_specs=[SMEM] * 4 + [VMEM] * 6,
            out_specs=[VMEM] * 2,
            scratch_shapes=[
                pltpu.VMEM((n_col, 3 * nvec, width), jnp.bfloat16),
                pltpu.VMEM((n_row + 1, nvec, width), jnp.float32),
            ],
            compiler_params=params,
            cost_estimate=cost,
            name="column_terms",
        )(place, arow, bcol, tile_count, energy, *x_col, *parts)
        col_send = pl.pallas_call(
            hand_on_kernel,
            out_shape=blocks(n_row // 2),
            in_specs=[VMEM, pl.BlockSpec(memory_space=pl.ANY)],
            out_specs=VMEM,
            compiler_params=params,
            name="hand_on",
        )(col_send, x_row[1])
    with jax.named_scope("row_terms"):
        row_send, row_keep = pl.pallas_call(
            functools.partial(row_kernel, n_row, n_col, slots),
            out_shape=[blocks(n_col // 2)] * 2,
            in_specs=[SMEM] * 4 + [VMEM] * 5,
            out_specs=[VMEM] * 2,
            scratch_shapes=[
                pltpu.VMEM((n_row, 3 * nvec, width), jnp.bfloat16),
                pltpu.VMEM((n_col + 1, nvec, width), jnp.float32),
            ],
            compiler_params=params,
            cost_estimate=cost,
            name="row_terms",
        )(place, arow, bcol, tile_count, *x_row, *parts)
    with jax.named_scope("return_products"):
        sums = halve(col_send, col_keep, "row") + halve(row_send, row_keep, "col")
    with jax.named_scope("product"):
        product, squares = pl.pallas_call(
            product_kernel,
            out_shape=[block, jax.ShapeDtypeStruct((devices, 3, packed_rows, width), jnp.float32)],
            in_specs=[VMEM] * 5,
            out_specs=[VMEM] * 2,
            compiler_params=params,
            name="product",
        )(vectors, *sums)
        squares = swap(squares, ("row", "col"))
    with jax.named_scope("results"):
        residual, rayleigh, gram, sound = pl.pallas_call(
            functools.partial(result_kernel, scale),
            out_shape=[block, square, square, jax.ShapeDtypeStruct((1, 1), jnp.int32)],
            in_specs=[VMEM] * 3,
            out_specs=[VMEM] * 4,
            compiler_params=params,
            name="results",
        )(vectors, product, squares)

    def from_residual(_):
        parts = pl.pallas_call(
            functools.partial(gram_parts_kernel, scale),
            out_shape=jax.ShapeDtypeStruct((devices, packed_rows, width), jnp.float32),
            in_specs=[VMEM] * 3,
            out_specs=VMEM,
            compiler_params=params,
            name="gram_parts",
        )(vectors, product, squares)
        gram = pl.pallas_call(
            functools.partial(gram_kernel, scale),
            out_shape=square,
            in_specs=[VMEM],
            out_specs=VMEM,
            compiler_params=params,
            name="gram_sum",
        )(swap(parts, ("row", "col")))
        return jnp.int32(1), gram

    with jax.named_scope("gram"):
        _, gram = lax.while_loop(lambda state: state[0] == 0, from_residual, (sound[0, 0], gram))
    return (residual, rayleigh, gram)


def solution(mesh):
    return jax.shard_map(
        per_device,
        mesh=mesh,
        in_specs=(
            P(None, ("row", "col")),
            P(("row", "col")),
            P("row", "col", None, None, None),
            P("row", "col", None),
            P("row", "col", None),
            P("row", "col"),
        ),
        out_specs=(P(None, ("row", "col")), P(), P()),
        check_vma=False,
    )
```

```python
import functools

import jax
import jax.numpy as jnp
from jax import lax
from jax.experimental import pallas as pl
from jax.experimental.pallas import tpu as pltpu
from jax.sharding import PartitionSpec as P

HP = lax.Precision.HIGHEST
VMEM = pl.BlockSpec(memory_space=pltpu.VMEM)
SMEM = pl.BlockSpec(memory_space=pltpu.SMEM)


def mult(left, right):
    return lax.dot_general(left, right, (((1,), (0,)), ((), ())), precision=HP, preferred_element_type=jnp.float32)


def mult_last(left, right):
    return lax.dot_general(left, right, (((1,), (1,)), ((), ())), precision=HP, preferred_element_type=jnp.float32)


def swap(blocks, axis):
    return lax.all_to_all(blocks, axis, 0, 0, tiled=True)


def trade(value, axis, flip):
    size = lax.axis_size(axis)
    return lax.ppermute(value, axis, [(p, p ^ flip) for p in range(size)])


def own_lanes(nvec, width):
    row = lax.broadcasted_iota(jnp.int32, (nvec, width), 0)
    lane = lax.broadcasted_iota(jnp.int32, (nvec, width), 1)
    return lane // nvec == row % (width // nvec)


def packed_gram(left, right):
    nvec, width = right.shape
    per = width // nvec
    wide = mult_last(left, jnp.concatenate([right] * per, axis=0))
    mask = own_lanes(nvec, width)
    squares = []
    for first in range(0, left.shape[0], nvec):
        own = jnp.where(mask, wide[first : first + nvec], 0.0)
        squares.append(jnp.sum(own.reshape(nvec // per, per, width), axis=1))
    return squares


def unpack(packed, nvec):
    rows, width = packed[0].shape
    per = width // nvec
    lane = lax.broadcasted_iota(jnp.int32, (width, nvec), 0)
    column = lax.broadcasted_iota(jnp.int32, (width, nvec), 1)
    mask = own_lanes(nvec, width)
    wide = []
    for square in packed:
        spread = jnp.concatenate([jnp.broadcast_to(square[g : g + 1], (per, width)) for g in range(rows)], axis=0)
        wide.append(jnp.where(mask, spread, 0.0))
    fold = (lane % nvec == column).astype(jnp.bfloat16)
    pieces = [jnp.dot(part, fold, preferred_element_type=jnp.float32) for part in split(jnp.concatenate(wide, axis=0))]
    return (pieces[2] + pieces[1]) + pieces[0]


def split(value):
    first = value.astype(jnp.bfloat16)
    rest = value - first.astype(jnp.float32)
    second = rest.astype(jnp.bfloat16)
    return first, second, (rest - second.astype(jnp.float32)).astype(jnp.bfloat16)


def stack_split(value):
    return jnp.concatenate(split(value), axis=0)


def pair_products(stacked, parts, transposed):
    nvec, width = stacked[0].shape[0] // 3, stacked[0].shape[1]
    dims = (((1,), (1 if transposed else 0,)), ((), ()))
    axis = 0 if transposed else 1

    def wide(left, pieces):
        return lax.dot_general(left, jnp.concatenate(pieces, axis=axis), dims, preferred_element_type=jnp.float32)

    last = wide(jnp.concatenate([value[:nvec] for value in stacked], axis=0), [part[2] for part in parts])
    results = []
    for which, (value, part) in enumerate(zip(stacked, parts)):
        both = wide(value, part[:2])
        first, second = both[:, :width], both[:, width:]
        total = last[which * nvec : (which + 1) * nvec, which * width : (which + 1) * width]
        total = (total + second[nvec : 2 * nvec]) + first[2 * nvec :]
        total = (total + second[:nvec]) + first[nvec : 2 * nvec]
        results.append(total + first[:nvec])
    return results


def join_kernel(axes, *refs):
    for which, out in enumerate(refs[-axes:]):
        mine, other = refs[2 * which : 2 * which + 2]
        half = mine.shape[0]
        out[:half] = mine[...]
        out[half:] = other[...]


def prepare_kernel(slots, tiles, *refs):
    small, parts, copies = refs[:3], refs[3:6], refs[6:]
    for array, copy in zip(small, copies):
        copy[...] = array[...]
    for slot in range(slots):
        for part, piece in zip(parts, split(tiles[0, 0, slot])):
            part[slot] = piece


def part_blocks(sums, total, send, keep):
    for block in range(total // 2):
        keep[block] = sums[2 * block]
        send[block] = sums[2 * block + 1]


def column_kernel(n_row, n_col, slots, place, arow, bcol, count, d_ref, near, far, *refs):
    *parts, send, keep, rows, sums = refs
    me_row, me_col = place[0], place[1]
    half = n_col // 2
    for flip in range(n_col):
        rows[flip] = stack_split(near[flip] if flip < half else far[flip - half])
    sums[...] = jnp.zeros_like(sums)
    sums[0] = d_ref[...] * near[0]
    for pair in range(0, slots, 2):
        pieces = [[part[slot] for part in parts] for slot in (pair, pair + 1)]
        values = [rows[arow[0, 0, slot] ^ me_col] for slot in (pair, pair + 1)]
        for slot, terms in zip((pair, pair + 1), pair_products(values, pieces, False)):
            block = jnp.where(slot < count[0, 0], bcol[0, 0, slot] ^ me_row, n_row)
            sums[block] += terms
    part_blocks(sums, n_row, send, keep)


def hand_on_kernel(early, after, late):
    del after
    late[...] = early[...]


def row_kernel(n_row, n_col, slots, place, arow, bcol, count, near, far, *refs):
    *parts, send, keep, cols, sums = refs
    me_row, me_col = place[0], place[1]
    for pair in range(n_row // 2):
        cols[2 * pair] = stack_split(near[pair])
        cols[2 * pair + 1] = stack_split(far[pair])
    sums[...] = jnp.zeros_like(sums)
    for pair in range(0, slots, 2):
        pieces = [[part[slot] for part in parts] for slot in (pair, pair + 1)]
        values = [cols[bcol[0, 0, slot] ^ me_row] for slot in (pair, pair + 1)]
        for slot, terms in zip((pair, pair + 1), pair_products(values, pieces, True)):
            block = jnp.where(slot < count[0, 0], arow[0, 0, slot] ^ me_col, n_col)
            sums[block] += terms
    part_blocks(sums, n_col, send, keep)


def halve_kernel(mine, other, send, keep):
    part_blocks([mine[block] + other[block] for block in range(mine.shape[0])], mine.shape[0], send, keep)


def product_kernel(x_ref, *refs):
    parts, (product, out) = refs[:-2], refs[-2:]
    own = x_ref[...]
    total = parts[0][0]
    for part in parts[1:]:
        total += part[0]
    product[...] = total
    squares = packed_gram(jnp.concatenate([own, total], axis=0), total) + packed_gram(own, own)
    for block in range(out.shape[0]):
        for which, square in enumerate(squares):
            out[block, which] = square


def summed_squares(scale, parts, nvec):
    sums = jnp.sum(parts[...], axis=0)
    squares = unpack([sums[which] for which in range(3)], nvec) * scale
    return squares[:nvec], squares[nvec : 2 * nvec], squares[2 * nvec :]


def result_kernel(scale, x_ref, product, parts, residual, rayleigh, gram, sound):
    own = x_ref[...]
    nvec = own.shape[0]
    ray, outer, inner = summed_squares(scale, parts, nvec)
    rayleigh[...] = ray
    residual[...] = product[...] - mult(ray, own)
    twice = mult(ray, ray)
    lifted = mult_last(mult(ray, inner), ray)
    result = outer - (twice + twice.T) + lifted
    gram[...] = result
    diagonal = lax.broadcasted_iota(jnp.int32, (nvec, nvec), 0) == lax.broadcasted_iota(jnp.int32, (nvec, nvec), 1)
    margin = jnp.sum(jnp.where(diagonal, 64.0 * result - (outer + lifted), 0.0), keepdims=True)
    sound[...] = (margin >= 0.0).astype(jnp.int32)


def gram_parts_kernel(scale, x_ref, product, parts, out):
    own = x_ref[...]
    ray, _, _ = summed_squares(scale, parts, own.shape[0])
    residual = product[...] - mult(ray, own)
    square = packed_gram(residual, residual)[0]
    for block in range(out.shape[0]):
        out[block] = square


def gram_kernel(scale, parts, out):
    out[...] = unpack([jnp.sum(parts[...], axis=0)], out.shape[0]) * scale


def per_device(vectors, diagonal_energy, tiles, tile_rows, tile_cols, tile_count):
    n_row = lax.axis_size("row")
    n_col = lax.axis_size("col")
    devices = n_row * n_col
    nvec, width = vectors.shape
    slots = tiles.shape[2]
    scale = 1.0 / float(devices * width)
    packed_rows = nvec * nvec // width
    block = jax.ShapeDtypeStruct((nvec, width), jnp.float32)
    square = jax.ShapeDtypeStruct((nvec, nvec), jnp.float32)
    part = jax.ShapeDtypeStruct((slots, width, width), jnp.bfloat16)
    place = jnp.stack([lax.axis_index("row"), lax.axis_index("col")]).astype(jnp.int32)
    energy = diagonal_energy.reshape(1, width)
    params = pltpu.CompilerParams(vmem_limit_bytes=16 * 2**20)
    cost = pl.CostEstimate(flops=12 * slots * nvec * width * width, bytes_accessed=2**20, transcendentals=0)

    def blocks(total):
        return jax.ShapeDtypeStruct((total, nvec, width), jnp.float32)

    def gather(after, **flips):
        axes = list(flips)
        near = [vectors[None]] * len(axes)
        far = [trade(vectors[None], axis, flips[axis][0]) for axis in axes]
        step = 1
        while any(step < len(flips[axis]) for axis in axes):
            going = [which for which, axis in enumerate(axes) if step < len(flips[axis])]
            joined = pl.pallas_call(
                functools.partial(join_kernel, len(going)),
                out_shape=[blocks(2**step)] * len(going),
                in_specs=[VMEM] * (2 * len(going)) + [pl.BlockSpec(memory_space=pl.ANY)] * len(after),
                out_specs=[VMEM] * len(going),
                compiler_params=params,
                name="join",
            )(*[half for which in going for half in (near[which], far[which])], *after)
            for which, half in zip(going, joined):
                near[which], far[which] = half, trade(half, axes[which], flips[axes[which]][step])
            step += 1
            after = ()
        return list(zip(near, far))

    def halve(send, keep, axis):
        flip = 1
        while keep.shape[0] > 1:
            half = keep.shape[0] // 2
            send, keep = pl.pallas_call(
                halve_kernel,
                out_shape=[blocks(half)] * 2,
                in_specs=[VMEM] * 2,
                out_specs=[VMEM] * 2,
                compiler_params=params,
                name="halve_" + axis,
            )(keep, trade(send, axis, flip))
            flip *= 2
        return keep, trade(send, axis, flip)

    with jax.named_scope("prepare"):
        small = (tile_rows, tile_cols, energy)
        *parts, arow, bcol, energy = pl.pallas_call(
            functools.partial(prepare_kernel, slots),
            out_shape=[part] * 3 + [jax.ShapeDtypeStruct(array.shape, array.dtype) for array in small],
            in_specs=[VMEM] * 4,
            out_specs=[VMEM] * 6,
            compiler_params=params,
            cost_estimate=pl.CostEstimate(flops=0, bytes_accessed=5 * slots * width * width, transcendentals=0),
            name="prepare",
        )(tiles, *small)
    with jax.named_scope("share_vectors"):
        bits = [1 << bit for bit in range(n_row.bit_length() - 1)]
        x_col, x_row = gather(parts[:1], col=[1 << bit for bit in range(n_col.bit_length() - 1)], row=bits[1:] + bits[:1])
    with jax.named_scope("column_terms"):
        col_send, col_keep = pl.pallas_call(
            functools.partial(column_kernel, n_row, n_col, slots),
            out_shape=[blocks(n_row // 2)] * 2,
            in_specs=[SMEM] * 4 + [VMEM] * 6,
            out_specs=[VMEM] * 2,
            scratch_shapes=[
                pltpu.VMEM((n_col, 3 * nvec, width), jnp.bfloat16),
                pltpu.VMEM((n_row + 1, nvec, width), jnp.float32),
            ],
            compiler_params=params,
            cost_estimate=cost,
            name="column_terms",
        )(place, arow, bcol, tile_count, energy, *x_col, *parts)
        col_send = pl.pallas_call(
            hand_on_kernel,
            out_shape=blocks(n_row // 2),
            in_specs=[VMEM, pl.BlockSpec(memory_space=pl.ANY)],
            out_specs=VMEM,
            compiler_params=params,
            name="hand_on",
        )(col_send, x_row[1])
    with jax.named_scope("row_terms"):
        row_send, row_keep = pl.pallas_call(
            functools.partial(row_kernel, n_row, n_col, slots),
            out_shape=[blocks(n_col // 2)] * 2,
            in_specs=[SMEM] * 4 + [VMEM] * 5,
            out_specs=[VMEM] * 2,
            scratch_shapes=[
                pltpu.VMEM((n_row, 3 * nvec, width), jnp.bfloat16),
                pltpu.VMEM((n_col + 1, nvec, width), jnp.float32),
            ],
            compiler_params=params,
            cost_estimate=cost,
            name="row_terms",
        )(place, arow, bcol, tile_count, *x_row, *parts)
    with jax.named_scope("return_products"):
        sums = halve(col_send, col_keep, "row") + halve(row_send, row_keep, "col")
    with jax.named_scope("product"):
        product, squares = pl.pallas_call(
            product_kernel,
            out_shape=[block, jax.ShapeDtypeStruct((devices, 3, packed_rows, width), jnp.float32)],
            in_specs=[VMEM] * 5,
            out_specs=[VMEM] * 2,
            compiler_params=params,
            name="product",
        )(vectors, *sums)
        squares = swap(squares, ("row", "col"))
    with jax.named_scope("results"):
        residual, rayleigh, gram, sound = pl.pallas_call(
            functools.partial(result_kernel, scale),
            out_shape=[block, square, square, jax.ShapeDtypeStruct((1, 1), jnp.int32)],
            in_specs=[VMEM] * 3,
            out_specs=[VMEM] * 4,
            compiler_params=params,
            name="results",
        )(vectors, product, squares)

    def from_residual(_):
        parts = pl.pallas_call(
            functools.partial(gram_parts_kernel, scale),
            out_shape=jax.ShapeDtypeStruct((devices, packed_rows, width), jnp.float32),
            in_specs=[VMEM] * 3,
            out_specs=VMEM,
            compiler_params=params,
            name="gram_parts",
        )(vectors, product, squares)
        gram = pl.pallas_call(
            functools.partial(gram_kernel, scale),
            out_shape=square,
            in_specs=[VMEM],
            out_specs=VMEM,
            compiler_params=params,
            name="gram_sum",
        )(swap(parts, ("row", "col")))
        return jnp.int32(1), gram

    with jax.named_scope("gram"):
        _, gram = lax.while_loop(lambda state: state[0] == 0, from_residual, (sound[0, 0], gram))
    return (residual, rayleigh, gram)


def solution(mesh):
    return jax.shard_map(
        per_device,
        mesh=mesh,
        in_specs=(
            P(None, ("row", "col")),
            P(("row", "col")),
            P("row", "col", None, None, None),
            P("row", "col", None),
            P("row", "col", None),
            P("row", "col"),
        ),
        out_specs=(P(None, ("row", "col")), P(), P()),
        check_vma=False,
    )
```

```python
import functools

import jax
import jax.numpy as jnp
from jax import lax
from jax.experimental import pallas as pl
from jax.experimental.pallas import tpu as pltpu
from jax.sharding import PartitionSpec as P

HP = lax.Precision.HIGHEST
VMEM = pl.BlockSpec(memory_space=pltpu.VMEM)
SMEM = pl.BlockSpec(memory_space=pltpu.SMEM)


def mult(left, right):
    return lax.dot_general(left, right, (((1,), (0,)), ((), ())), precision=HP, preferred_element_type=jnp.float32)


def mult_last(left, right):
    return lax.dot_general(left, right, (((1,), (1,)), ((), ())), precision=HP, preferred_element_type=jnp.float32)


def swap(blocks, axis):
    return lax.all_to_all(blocks, axis, 0, 0, tiled=True)


def trade(value, axis, flip):
    size = lax.axis_size(axis)
    return lax.ppermute(value, axis, [(p, p ^ flip) for p in range(size)])


def own_lanes(nvec, width):
    row = lax.broadcasted_iota(jnp.int32, (nvec, width), 0)
    lane = lax.broadcasted_iota(jnp.int32, (nvec, width), 1)
    return lane // nvec == row % (width // nvec)


def packed_gram(left, right):
    nvec, width = right.shape
    per = width // nvec
    wide = mult_last(left, jnp.concatenate([right] * per, axis=0))
    mask = own_lanes(nvec, width)
    squares = []
    for first in range(0, left.shape[0], nvec):
        own = jnp.where(mask, wide[first : first + nvec], 0.0)
        squares.append(jnp.sum(own.reshape(nvec // per, per, width), axis=1))
    return squares


def unpack(packed, nvec):
    rows, width = packed[0].shape
    per = width // nvec
    lane = lax.broadcasted_iota(jnp.int32, (width, nvec), 0)
    column = lax.broadcasted_iota(jnp.int32, (width, nvec), 1)
    mask = own_lanes(nvec, width)
    wide = []
    for square in packed:
        spread = jnp.concatenate([jnp.broadcast_to(square[g : g + 1], (per, width)) for g in range(rows)], axis=0)
        wide.append(jnp.where(mask, spread, 0.0))
    fold = (lane % nvec == column).astype(jnp.bfloat16)
    pieces = [jnp.dot(part, fold, preferred_element_type=jnp.float32) for part in split(jnp.concatenate(wide, axis=0))]
    return (pieces[2] + pieces[1]) + pieces[0]


def split(value):
    first = value.astype(jnp.bfloat16)
    rest = value - first.astype(jnp.float32)
    second = rest.astype(jnp.bfloat16)
    return first, second, (rest - second.astype(jnp.float32)).astype(jnp.bfloat16)


def stack_split(value):
    return jnp.concatenate(split(value), axis=0)


def pair_products(stacked, parts, transposed):
    nvec, width = stacked[0].shape[0] // 3, stacked[0].shape[1]
    dims = (((1,), (1 if transposed else 0,)), ((), ()))
    axis = 0 if transposed else 1

    def wide(left, pieces):
        return lax.dot_general(left, jnp.concatenate(pieces, axis=axis), dims, preferred_element_type=jnp.float32)

    last = wide(jnp.concatenate([value[:nvec] for value in stacked], axis=0), [part[2] for part in parts])
    results = []
    for which, (value, part) in enumerate(zip(stacked, parts)):
        both = wide(value, part[:2])
        first, second = both[:, :width], both[:, width:]
        total = last[which * nvec : (which + 1) * nvec, which * width : (which + 1) * width]
        total = (total + second[nvec : 2 * nvec]) + first[2 * nvec :]
        total = (total + second[:nvec]) + first[nvec : 2 * nvec]
        results.append(total + first[:nvec])
    return results


def join_kernel(axes, *refs):
    for which, out in enumerate(refs[-axes:]):
        mine, other = refs[2 * which : 2 * which + 2]
        half = mine.shape[0]
        out[:half] = mine[...]
        out[half:] = other[...]


def prepare_kernel(slots, tiles, *refs):
    small, parts, copies = refs[:3], refs[3:6], refs[6:]
    for array, copy in zip(small, copies):
        copy[...] = array[...]
    for slot in range(slots):
        for part, piece in zip(parts, split(tiles[0, 0, slot])):
            part[slot] = piece


def part_blocks(sums, total, send, keep):
    for block in range(total // 2):
        keep[block] = sums[2 * block]
        send[block] = sums[2 * block + 1]


def column_kernel(n_row, n_col, slots, place, arow, bcol, count, d_ref, near, far, *refs):
    *parts, send, keep, rows, sums = refs
    me_row, me_col = place[0], place[1]
    half = n_col // 2
    for flip in range(n_col):
        rows[flip] = stack_split(near[flip] if flip < half else far[flip - half])
    sums[...] = jnp.zeros_like(sums)
    sums[0] = d_ref[...] * near[0]
    for pair in range(0, slots, 2):
        pieces = [[part[slot] for part in parts] for slot in (pair, pair + 1)]
        values = [rows[arow[0, 0, slot] ^ me_col] for slot in (pair, pair + 1)]
        for slot, terms in zip((pair, pair + 1), pair_products(values, pieces, False)):
            block = jnp.where(slot < count[0, 0], bcol[0, 0, slot] ^ me_row, n_row)
            sums[block] += terms
    part_blocks(sums, n_row, send, keep)


def hand_on_kernel(early, after, late):
    del after
    late[...] = early[...]


def row_kernel(n_row, n_col, slots, place, arow, bcol, count, near, far, *refs):
    *parts, send, keep, cols, sums = refs
    me_row, me_col = place[0], place[1]
    for pair in range(n_row // 2):
        cols[2 * pair] = stack_split(near[pair])
        cols[2 * pair + 1] = stack_split(far[pair])
    sums[...] = jnp.zeros_like(sums)
    for pair in range(0, slots, 2):
        pieces = [[part[slot] for part in parts] for slot in (pair, pair + 1)]
        values = [cols[bcol[0, 0, slot] ^ me_row] for slot in (pair, pair + 1)]
        for slot, terms in zip((pair, pair + 1), pair_products(values, pieces, True)):
            block = jnp.where(slot < count[0, 0], arow[0, 0, slot] ^ me_col, n_col)
            sums[block] += terms
    part_blocks(sums, n_col, send, keep)


def halve_kernel(mine, other, send, keep):
    part_blocks([mine[block] + other[block] for block in range(mine.shape[0])], mine.shape[0], send, keep)


def product_kernel(x_ref, *refs):
    parts, (product, out) = refs[:-2], refs[-2:]
    own = x_ref[...]
    total = parts[0][0]
    for part in parts[1:]:
        total += part[0]
    product[...] = total
    squares = packed_gram(jnp.concatenate([own, total], axis=0), total) + packed_gram(own, own)
    for block in range(out.shape[0]):
        for which, square in enumerate(squares):
            out[block, which] = square


def summed_squares(scale, parts, nvec):
    sums = jnp.sum(parts[...], axis=0)
    squares = unpack([sums[which] for which in range(3)], nvec) * scale
    return squares[:nvec], squares[nvec : 2 * nvec], squares[2 * nvec :]


def result_kernel(scale, x_ref, product, parts, residual, rayleigh, gram, sound):
    own = x_ref[...]
    nvec = own.shape[0]
    ray, outer, inner = summed_squares(scale, parts, nvec)
    rayleigh[...] = ray
    width = own.shape[1]
    blank = jnp.zeros((nvec, width - nvec), jnp.float32)
    wide = mult(ray, jnp.concatenate([own, ray, blank, inner, blank], axis=1))
    residual[...] = product[...] - wide[:, :width]
    twice = wide[:, width : width + nvec]
    lifted = mult_last(wide[:, 2 * width : 2 * width + nvec], ray)
    result = outer - (twice + twice.T) + lifted
    gram[...] = result
    diagonal = lax.broadcasted_iota(jnp.int32, (nvec, nvec), 0) == lax.broadcasted_iota(jnp.int32, (nvec, nvec), 1)
    margin = jnp.sum(jnp.where(diagonal, 64.0 * result - (outer + lifted), 0.0), keepdims=True)
    sound[...] = (margin >= 0.0).astype(jnp.int32)


def gram_parts_kernel(scale, x_ref, product, parts, out):
    own = x_ref[...]
    ray, _, _ = summed_squares(scale, parts, own.shape[0])
    residual = product[...] - mult(ray, own)
    square = packed_gram(residual, residual)[0]
    for block in range(out.shape[0]):
        out[block] = square


def gram_kernel(scale, parts, out):
    out[...] = unpack([jnp.sum(parts[...], axis=0)], out.shape[0]) * scale


def per_device(vectors, diagonal_energy, tiles, tile_rows, tile_cols, tile_count):
    n_row = lax.axis_size("row")
    n_col = lax.axis_size("col")
    devices = n_row * n_col
    nvec, width = vectors.shape
    slots = tiles.shape[2]
    scale = 1.0 / float(devices * width)
    packed_rows = nvec * nvec // width
    block = jax.ShapeDtypeStruct((nvec, width), jnp.float32)
    square = jax.ShapeDtypeStruct((nvec, nvec), jnp.float32)
    part = jax.ShapeDtypeStruct((slots, width, width), jnp.bfloat16)
    place = jnp.stack([lax.axis_index("row"), lax.axis_index("col")]).astype(jnp.int32)
    energy = diagonal_energy.reshape(1, width)
    params = pltpu.CompilerParams(vmem_limit_bytes=16 * 2**20)
    cost = pl.CostEstimate(flops=12 * slots * nvec * width * width, bytes_accessed=2**20, transcendentals=0)

    def blocks(total):
        return jax.ShapeDtypeStruct((total, nvec, width), jnp.float32)

    def gather(after, **flips):
        axes = list(flips)
        near = [vectors[None]] * len(axes)
        far = [trade(vectors[None], axis, flips[axis][0]) for axis in axes]
        step = 1
        while any(step < len(flips[axis]) for axis in axes):
            going = [which for which, axis in enumerate(axes) if step < len(flips[axis])]
            joined = pl.pallas_call(
                functools.partial(join_kernel, len(going)),
                out_shape=[blocks(2**step)] * len(going),
                in_specs=[VMEM] * (2 * len(going)) + [pl.BlockSpec(memory_space=pl.ANY)] * len(after),
                out_specs=[VMEM] * len(going),
                compiler_params=params,
                name="join",
            )(*[half for which in going for half in (near[which], far[which])], *after)
            for which, half in zip(going, joined):
                near[which], far[which] = half, trade(half, axes[which], flips[axes[which]][step])
            step += 1
            after = ()
        return list(zip(near, far))

    def halve(send, keep, axis):
        flip = 1
        while keep.shape[0] > 1:
            half = keep.shape[0] // 2
            send, keep = pl.pallas_call(
                halve_kernel,
                out_shape=[blocks(half)] * 2,
                in_specs=[VMEM] * 2,
                out_specs=[VMEM] * 2,
                compiler_params=params,
                name="halve_" + axis,
            )(keep, trade(send, axis, flip))
            flip *= 2
        return keep, trade(send, axis, flip)

    with jax.named_scope("prepare"):
        small = (tile_rows, tile_cols, energy)
        *parts, arow, bcol, energy = pl.pallas_call(
            functools.partial(prepare_kernel, slots),
            out_shape=[part] * 3 + [jax.ShapeDtypeStruct(array.shape, array.dtype) for array in small],
            in_specs=[VMEM] * 4,
            out_specs=[VMEM] * 6,
            compiler_params=params,
            cost_estimate=pl.CostEstimate(flops=0, bytes_accessed=5 * slots * width * width, transcendentals=0),
            name="prepare",
        )(tiles, *small)
    with jax.named_scope("share_vectors"):
        bits = [1 << bit for bit in range(n_row.bit_length() - 1)]
        x_row, x_col = gather(parts[:1], row=bits[1:] + bits[:1], col=[1 << bit for bit in range(n_col.bit_length() - 1)])
    with jax.named_scope("column_terms"):
        col_send, col_keep = pl.pallas_call(
            functools.partial(column_kernel, n_row, n_col, slots),
            out_shape=[blocks(n_row // 2)] * 2,
            in_specs=[SMEM] * 4 + [VMEM] * 6,
            out_specs=[VMEM] * 2,
            scratch_shapes=[
                pltpu.VMEM((n_col, 3 * nvec, width), jnp.bfloat16),
                pltpu.VMEM((n_row + 1, nvec, width), jnp.float32),
            ],
            compiler_params=params,
            cost_estimate=cost,
            name="column_terms",
        )(place, arow, bcol, tile_count, energy, *x_col, *parts)
        col_send = pl.pallas_call(
            hand_on_kernel,
            out_shape=blocks(n_row // 2),
            in_specs=[VMEM, pl.BlockSpec(memory_space=pl.ANY)],
            out_specs=VMEM,
            compiler_params=params,
            name="hand_on",
        )(col_send, x_row[1])
    with jax.named_scope("row_terms"):
        row_send, row_keep = pl.pallas_call(
            functools.partial(row_kernel, n_row, n_col, slots),
            out_shape=[blocks(n_col // 2)] * 2,
            in_specs=[SMEM] * 4 + [VMEM] * 5,
            out_specs=[VMEM] * 2,
            scratch_shapes=[
                pltpu.VMEM((n_row, 3 * nvec, width), jnp.bfloat16),
                pltpu.VMEM((n_col + 1, nvec, width), jnp.float32),
            ],
            compiler_params=params,
            cost_estimate=cost,
            name="row_terms",
        )(place, arow, bcol, tile_count, *x_row, *parts)
    with jax.named_scope("return_products"):
        sums = halve(col_send, col_keep, "row") + halve(row_send, row_keep, "col")
    with jax.named_scope("product"):
        product, squares = pl.pallas_call(
            product_kernel,
            out_shape=[block, jax.ShapeDtypeStruct((devices, 3, packed_rows, width), jnp.float32)],
            in_specs=[VMEM] * 5,
            out_specs=[VMEM] * 2,
            compiler_params=params,
            name="product",
        )(vectors, *sums)
        squares = swap(squares, ("row", "col"))
    with jax.named_scope("results"):
        residual, rayleigh, gram, sound = pl.pallas_call(
            functools.partial(result_kernel, scale),
            out_shape=[block, square, square, jax.ShapeDtypeStruct((1, 1), jnp.int32)],
            in_specs=[VMEM] * 3,
            out_specs=[VMEM] * 4,
            compiler_params=params,
            name="results",
        )(vectors, product, squares)

    def from_residual(_):
        parts = pl.pallas_call(
            functools.partial(gram_parts_kernel, scale),
            out_shape=jax.ShapeDtypeStruct((devices, packed_rows, width), jnp.float32),
            in_specs=[VMEM] * 3,
            out_specs=VMEM,
            compiler_params=params,
            name="gram_parts",
        )(vectors, product, squares)
        gram = pl.pallas_call(
            functools.partial(gram_kernel, scale),
            out_shape=square,
            in_specs=[VMEM],
            out_specs=VMEM,
            compiler_params=params,
            name="gram_sum",
        )(swap(parts, ("row", "col")))
        return jnp.int32(1), gram

    with jax.named_scope("gram"):
        _, gram = lax.while_loop(lambda state: state[0] == 0, from_residual, (sound[0, 0], gram))
    return (residual, rayleigh, gram)


def solution(mesh):
    return jax.shard_map(
        per_device,
        mesh=mesh,
        in_specs=(
            P(None, ("row", "col")),
            P(("row", "col")),
            P("row", "col", None, None, None),
            P("row", "col", None),
            P("row", "col", None),
            P("row", "col"),
        ),
        out_specs=(P(None, ("row", "col")), P(), P()),
        check_vma=False,
    )
```

```python
import functools

import jax
import jax.numpy as jnp
from jax import lax
from jax.experimental import pallas as pl
from jax.experimental.pallas import tpu as pltpu
from jax.sharding import PartitionSpec as P

HP = lax.Precision.HIGHEST
VMEM = pl.BlockSpec(memory_space=pltpu.VMEM)
SMEM = pl.BlockSpec(memory_space=pltpu.SMEM)


def mult(left, right):
    return lax.dot_general(left, right, (((1,), (0,)), ((), ())), precision=HP, preferred_element_type=jnp.float32)


def mult_last(left, right):
    return lax.dot_general(left, right, (((1,), (1,)), ((), ())), precision=HP, preferred_element_type=jnp.float32)


def swap(blocks, axis):
    return lax.all_to_all(blocks, axis, 0, 0, tiled=True)


def trade(value, axis, flip):
    size = lax.axis_size(axis)
    return lax.ppermute(value, axis, [(p, p ^ flip) for p in range(size)])


def own_lanes(nvec, width):
    row = lax.broadcasted_iota(jnp.int32, (nvec, width), 0)
    lane = lax.broadcasted_iota(jnp.int32, (nvec, width), 1)
    return lane // nvec == row % (width // nvec)


def packed_gram(left, right):
    nvec, width = right.shape
    per = width // nvec
    wide = mult_last(left, jnp.concatenate([right] * per, axis=0))
    mask = own_lanes(nvec, width)
    squares = []
    for first in range(0, left.shape[0], nvec):
        own = jnp.where(mask, wide[first : first + nvec], 0.0)
        squares.append(jnp.sum(own.reshape(nvec // per, per, width), axis=1))
    return squares


def unpack(packed, nvec):
    rows, width = packed[0].shape
    per = width // nvec
    lane = lax.broadcasted_iota(jnp.int32, (width, nvec), 0)
    column = lax.broadcasted_iota(jnp.int32, (width, nvec), 1)
    mask = own_lanes(nvec, width)
    wide = []
    for square in packed:
        spread = jnp.concatenate([jnp.broadcast_to(square[g : g + 1], (per, width)) for g in range(rows)], axis=0)
        wide.append(jnp.where(mask, spread, 0.0))
    fold = (lane % nvec == column).astype(jnp.bfloat16)
    pieces = [jnp.dot(part, fold, preferred_element_type=jnp.float32) for part in split(jnp.concatenate(wide, axis=0))]
    return (pieces[2] + pieces[1]) + pieces[0]


def split(value):
    first = value.astype(jnp.bfloat16)
    rest = value - first.astype(jnp.float32)
    second = rest.astype(jnp.bfloat16)
    return first, second, (rest - second.astype(jnp.float32)).astype(jnp.bfloat16)


def stack_split(value):
    return jnp.concatenate(split(value), axis=0)


def pair_products(stacked, parts, transposed):
    nvec, width = stacked[0].shape[0] // 3, stacked[0].shape[1]
    dims = (((1,), (1 if transposed else 0,)), ((), ()))
    axis = 0 if transposed else 1

    def wide(left, pieces):
        return lax.dot_general(left, jnp.concatenate(pieces, axis=axis), dims, preferred_element_type=jnp.float32)

    last = wide(jnp.concatenate([value[:nvec] for value in stacked], axis=0), [part[2] for part in parts])
    results = []
    for which, (value, part) in enumerate(zip(stacked, parts)):
        both = wide(value, part[:2])
        first, second = both[:, :width], both[:, width:]
        total = last[which * nvec : (which + 1) * nvec, which * width : (which + 1) * width]
        total = (total + second[nvec : 2 * nvec]) + first[2 * nvec :]
        total = (total + second[:nvec]) + first[nvec : 2 * nvec]
        results.append(total + first[:nvec])
    return results


def join_kernel(axes, *refs):
    for which, out in enumerate(refs[-axes:]):
        mine, other = refs[2 * which : 2 * which + 2]
        half = mine.shape[0]
        out[:half] = mine[...]
        out[half:] = other[...]


def prepare_kernel(slots, tiles, *refs):
    small, parts, copies = refs[:3], refs[3:6], refs[6:]
    for array, copy in zip(small, copies):
        copy[...] = array[...]
    for slot in range(slots):
        for part, piece in zip(parts, split(tiles[0, 0, slot])):
            part[slot] = piece


def part_blocks(sums, total, send, keep):
    for block in range(total // 2):
        keep[block] = sums[2 * block]
        send[block] = sums[2 * block + 1]


def column_kernel(n_row, n_col, slots, place, arow, bcol, count, d_ref, near, far, *refs):
    *parts, send, keep, rows, sums = refs
    me_row, me_col = place[0], place[1]
    half = n_col // 2
    for flip in range(n_col):
        rows[flip] = stack_split(near[flip] if flip < half else far[flip - half])
    sums[...] = jnp.zeros_like(sums)
    sums[0] = d_ref[...] * near[0]
    for pair in range(0, slots, 2):
        pieces = [[part[slot] for part in parts] for slot in (pair, pair + 1)]
        values = [rows[arow[0, 0, slot] ^ me_col] for slot in (pair, pair + 1)]
        for slot, terms in zip((pair, pair + 1), pair_products(values, pieces, False)):
            block = jnp.where(slot < count[0, 0], bcol[0, 0, slot] ^ me_row, n_row)
            sums[block] += terms
    part_blocks(sums, n_row, send, keep)


def hand_on_kernel(early, after, late):
    del after
    late[...] = early[...]


def row_kernel(n_row, n_col, slots, place, arow, bcol, count, near, far, *refs):
    *parts, send, keep, cols, sums = refs
    me_row, me_col = place[0], place[1]
    for pair in range(n_row // 2):
        cols[2 * pair] = stack_split(near[pair])
        cols[2 * pair + 1] = stack_split(far[pair])
    sums[...] = jnp.zeros_like(sums)
    for pair in range(0, slots, 2):
        pieces = [[part[slot] for part in parts] for slot in (pair, pair + 1)]
        values = [cols[bcol[0, 0, slot] ^ me_row] for slot in (pair, pair + 1)]
        for slot, terms in zip((pair, pair + 1), pair_products(values, pieces, True)):
            block = jnp.where(slot < count[0, 0], arow[0, 0, slot] ^ me_col, n_col)
            sums[block] += terms
    part_blocks(sums, n_col, send, keep)


def halve_kernel(mine, other, send, keep):
    part_blocks([mine[block] + other[block] for block in range(mine.shape[0])], mine.shape[0], send, keep)


def product_kernel(x_ref, *refs):
    parts, (product, out) = refs[:-2], refs[-2:]
    own = x_ref[...]
    total = parts[0][0]
    for part in parts[1:]:
        total += part[0]
    product[...] = total
    squares = packed_gram(jnp.concatenate([own, total], axis=0), total) + packed_gram(own, own)
    for block in range(out.shape[0]):
        for which, square in enumerate(squares):
            out[block, which] = square


def summed_squares(scale, parts, nvec):
    sums = jnp.sum(parts[...], axis=0)
    squares = unpack([sums[which] for which in range(3)], nvec) * scale
    return squares[:nvec], squares[nvec : 2 * nvec], squares[2 * nvec :]


def result_kernel(scale, x_ref, product, parts, residual, rayleigh, gram, sound):
    own = x_ref[...]
    nvec = own.shape[0]
    ray, outer, inner = summed_squares(scale, parts, nvec)
    rayleigh[...] = ray
    residual[...] = product[...] - mult(ray, own)
    twice = mult(ray, ray)
    lifted = mult_last(mult(ray, inner), ray)
    result = outer - (twice + twice.T) + lifted
    gram[...] = result
    diagonal = lax.broadcasted_iota(jnp.int32, (nvec, nvec), 0) == lax.broadcasted_iota(jnp.int32, (nvec, nvec), 1)
    margin = jnp.sum(jnp.where(diagonal, 64.0 * result - (outer + lifted), 0.0), keepdims=True)
    sound[...] = (margin >= 0.0).astype(jnp.int32)


def gram_parts_kernel(scale, x_ref, product, parts, out):
    own = x_ref[...]
    ray, _, _ = summed_squares(scale, parts, own.shape[0])
    residual = product[...] - mult(ray, own)
    square = packed_gram(residual, residual)[0]
    for block in range(out.shape[0]):
        out[block] = square


def gram_kernel(scale, parts, out):
    out[...] = unpack([jnp.sum(parts[...], axis=0)], out.shape[0]) * scale


def per_device(vectors, diagonal_energy, tiles, tile_rows, tile_cols, tile_count):
    n_row = lax.axis_size("row")
    n_col = lax.axis_size("col")
    devices = n_row * n_col
    nvec, width = vectors.shape
    slots = tiles.shape[2]
    scale = 1.0 / float(devices * width)
    packed_rows = nvec * nvec // width
    block = jax.ShapeDtypeStruct((nvec, width), jnp.float32)
    square = jax.ShapeDtypeStruct((nvec, nvec), jnp.float32)
    part = jax.ShapeDtypeStruct((slots, width, width), jnp.bfloat16)
    place = jnp.stack([lax.axis_index("row"), lax.axis_index("col")]).astype(jnp.int32)
    energy = diagonal_energy.reshape(1, width)
    params = pltpu.CompilerParams(vmem_limit_bytes=16 * 2**20)
    cost = pl.CostEstimate(flops=12 * slots * nvec * width * width, bytes_accessed=2**20, transcendentals=0)

    def blocks(total):
        return jax.ShapeDtypeStruct((total, nvec, width), jnp.float32)

    def gather(after, **flips):
        axes = list(flips)
        near = [vectors[None]] * len(axes)
        far = [trade(vectors[None], axis, flips[axis][0]) for axis in axes]
        step = 1
        while any(step < len(flips[axis]) for axis in axes):
            going = [which for which, axis in enumerate(axes) if step < len(flips[axis])]
            joined = pl.pallas_call(
                functools.partial(join_kernel, len(going)),
                out_shape=[blocks(2**step)] * len(going),
                in_specs=[VMEM] * (2 * len(going)) + [pl.BlockSpec(memory_space=pl.ANY)] * len(after),
                out_specs=[VMEM] * len(going),
                compiler_params=params,
                name="join",
            )(*[half for which in going for half in (near[which], far[which])], *after)
            for which, half in zip(going, joined):
                near[which], far[which] = half, trade(half, axes[which], flips[axes[which]][step])
            step += 1
            after = ()
        return list(zip(near, far))

    def halve(send, keep, axis):
        flip = 1
        while keep.shape[0] > 1:
            half = keep.shape[0] // 2
            send, keep = pl.pallas_call(
                halve_kernel,
                out_shape=[blocks(half)] * 2,
                in_specs=[VMEM] * 2,
                out_specs=[VMEM] * 2,
                compiler_params=params,
                name="halve_" + axis,
            )(keep, trade(send, axis, flip))
            flip *= 2
        return keep, trade(send, axis, flip)

    with jax.named_scope("prepare"):
        small = (tile_rows, tile_cols, energy)
        *parts, arow, bcol, energy = pl.pallas_call(
            functools.partial(prepare_kernel, slots),
            out_shape=[part] * 3 + [jax.ShapeDtypeStruct(array.shape, array.dtype) for array in small],
            in_specs=[VMEM] * 4,
            out_specs=[VMEM] * 6,
            compiler_params=params,
            cost_estimate=pl.CostEstimate(flops=0, bytes_accessed=5 * slots * width * width, transcendentals=0),
            name="prepare",
        )(tiles, *small)
    with jax.named_scope("share_vectors"):
        bits = [1 << bit for bit in range(n_row.bit_length() - 1)]
        x_row, x_col = gather(parts[:1], row=bits[1:] + bits[:1], col=[1 << bit for bit in range(n_col.bit_length() - 1)])
    with jax.named_scope("column_terms"):
        col_send, col_keep = pl.pallas_call(
            functools.partial(column_kernel, n_row, n_col, slots),
            out_shape=[blocks(n_row // 2)] * 2,
            in_specs=[SMEM] * 4 + [VMEM] * 6,
            out_specs=[VMEM] * 2,
            scratch_shapes=[
                pltpu.VMEM((n_col, 3 * nvec, width), jnp.bfloat16),
                pltpu.VMEM((n_row + 1, nvec, width), jnp.float32),
            ],
            compiler_params=params,
            cost_estimate=cost,
            name="column_terms",
        )(place, arow, bcol, tile_count, energy, *x_col, *parts)
        col_send = pl.pallas_call(
            hand_on_kernel,
            out_shape=blocks(n_row // 2),
            in_specs=[VMEM, pl.BlockSpec(memory_space=pl.ANY)],
            out_specs=VMEM,
            compiler_params=params,
            name="hand_on",
        )(col_send, x_row[0])
    with jax.named_scope("row_terms"):
        row_send, row_keep = pl.pallas_call(
            functools.partial(row_kernel, n_row, n_col, slots),
            out_shape=[blocks(n_col // 2)] * 2,
            in_specs=[SMEM] * 4 + [VMEM] * 5,
            out_specs=[VMEM] * 2,
            scratch_shapes=[
                pltpu.VMEM((n_row, 3 * nvec, width), jnp.bfloat16),
                pltpu.VMEM((n_col + 1, nvec, width), jnp.float32),
            ],
            compiler_params=params,
            cost_estimate=cost,
            name="row_terms",
        )(place, arow, bcol, tile_count, *x_row, *parts)
    with jax.named_scope("return_products"):
        sums = halve(col_send, col_keep, "row") + halve(row_send, row_keep, "col")
    with jax.named_scope("product"):
        product, squares = pl.pallas_call(
            product_kernel,
            out_shape=[block, jax.ShapeDtypeStruct((devices, 3, packed_rows, width), jnp.float32)],
            in_specs=[VMEM] * 5,
            out_specs=[VMEM] * 2,
            compiler_params=params,
            name="product",
        )(vectors, *sums)
        squares = swap(squares, ("row", "col"))
    with jax.named_scope("results"):
        residual, rayleigh, gram, sound = pl.pallas_call(
            functools.partial(result_kernel, scale),
            out_shape=[block, square, square, jax.ShapeDtypeStruct((1, 1), jnp.int32)],
            in_specs=[VMEM] * 3,
            out_specs=[VMEM] * 4,
            compiler_params=params,
            name="results",
        )(vectors, product, squares)

    def from_residual(_):
        parts = pl.pallas_call(
            functools.partial(gram_parts_kernel, scale),
            out_shape=jax.ShapeDtypeStruct((devices, packed_rows, width), jnp.float32),
            in_specs=[VMEM] * 3,
            out_specs=VMEM,
            compiler_params=params,
            name="gram_parts",
        )(vectors, product, squares)
        gram = pl.pallas_call(
            functools.partial(gram_kernel, scale),
            out_shape=square,
            in_specs=[VMEM],
            out_specs=VMEM,
            compiler_params=params,
            name="gram_sum",
        )(swap(parts, ("row", "col")))
        return jnp.int32(1), gram

    with jax.named_scope("gram"):
        _, gram = lax.while_loop(lambda state: state[0] == 0, from_residual, (sound[0, 0], gram))
    return (residual, rayleigh, gram)


def solution(mesh):
    return jax.shard_map(
        per_device,
        mesh=mesh,
        in_specs=(
            P(None, ("row", "col")),
            P(("row", "col")),
            P("row", "col", None, None, None),
            P("row", "col", None),
            P("row", "col", None),
            P("row", "col"),
        ),
        out_specs=(P(None, ("row", "col")), P(), P()),
        check_vma=False,
    )
```
